32 devices in a mesh: dp: 4 (over y, x), expert: 8 (over z, core).
Axes of the slice: x: 2, y: 2, z: 4, core: 2. Of those that a mesh axis runs over, the one named last changes fastest.
Arguments:
- tokens: bfloat16 [4, 1024, 2048], P('dp', 'expert'), may hold values from -6 to 6
- cotangent: bfloat16 [4, 1024, 2048], P('dp', 'expert'), may hold values from -6 to 6
- lengths: int32 [4], P('dp'), may hold values from 256 to 1024, as said below
- routes: int32 [4, 1024, 8], P('dp', 'expert'), may hold values from 0 to 15, all different within a row; in each aligned block of 128 rows (0 to 127, 128 to 255, ..., all dimensions but the last counted through in order) at most 128 rows name the same one
- w_query: float32 [2048, 2048], P(('dp', 'expert')), may hold values from -0.125 to 0.125
- w_key: float32 [2048, 2048], P(('dp', 'expert')), may hold values from -0.125 to 0.125
- w_value: float32 [2048, 2048], P(('dp', 'expert')), may hold values from -0.125 to 0.125
- w_output: float32 [2048, 2048], P(('dp', 'expert')), may hold values from -0.5 to 0.5
- router: float32 [2048, 16], P(('dp', 'expert')), may hold values from -0.0625 to 0.0625
- gain_attn: float32 [2048], P(('dp', 'expert')), may hold values from 0.5 to 1.5
- gain_query: float32 [2048], P(('dp', 'expert')), may hold values from 0.5 to 1.5
- gain_key: float32 [2048], P(('dp', 'expert')), may hold values from 0.5 to 1.5
- gain_mlp: float32 [2048], P(('dp', 'expert')), may hold values from 0.5 to 1.5
- w_gate: float32 [16, 2048, 1024], P('expert', None, 'dp'), may hold values from -0.125 to 0.125
- w_up: float32 [16, 2048, 1024], P('expert', None, 'dp'), may hold values from -0.125 to 0.125
- w_down: float32 [16, 1024, 2048], P('expert', 'dp'), may hold values from -0.5 to 0.5
Outputs:
- output: bfloat16 [4, 1024, 2048], P('dp', 'expert')
- grad_tokens: bfloat16 [4, 1024, 2048], P('dp', 'expert')
- grad_w_query: float32 [2048, 2048], P(('dp', 'expert'))
- grad_w_key: float32 [2048, 2048], P(('dp', 'expert'))
- grad_w_value: float32 [2048, 2048], P(('dp', 'expert'))
- grad_w_output: float32 [2048, 2048], P(('dp', 'expert'))
- grad_router: float32 [2048, 16], P(('dp', 'expert'))
- grad_gain_attn: float32 [2048], P(('dp', 'expert'))
- grad_gain_query: float32 [2048], P(('dp', 'expert'))
- grad_gain_key: float32 [2048], P(('dp', 'expert'))
- grad_gain_mlp: float32 [2048], P(('dp', 'expert'))
- grad_w_gate: float32 [16, 2048, 1024], P('expert', None, 'dp')
- grad_w_up: float32 [16, 2048, 1024], P('expert', None, 'dp')
- grad_w_down: float32 [16, 1024, 2048], P('expert', 'dp')
The draws below stay inside these ranges and needn't reach their ends.
Inputs may be any that keep to these rules, and one draw needn't show every extreme that they name: `lengths`: at least one sequence has the full length 1024. `routes`: A token's 8 experts differ. Among the 128 tokens of one device (aligned blocks of the flattened positions) no expert is named by more than 128 tokens, a bound that some block reaches of them in some of these blocks.
All inputs are finite; a program needn't handle non-finite values.
Results may differ from the reference program's by a relative error of at most 0.019.
Values may be sent and summed in bfloat16 or wider, within the bound.
No kernel may reach another device: no remote copies, remote signals or barrier semaphores. Data moves between devices by JAX's collectives and lax.ppermute only.
A program may use at most 384 MiB of HBM per device.

```python
import math
import jax
import jax.numpy as jnp
import numpy as np
from jax import lax

D = 2048
HEADS = 16
HEAD_DIM = 128
FF = 1024
TOP = 8
TOK_DEV = 128
EXPERTS = 16
SEQS = 4
SEQ_LEN = 1024
MOST = 128
N_EXPERT = 8


def draw_lengths(key, part):
    key = jax.random.fold_in(key, 11)
    first_key, second_key = jax.random.split(key)
    drawn = jax.random.randint(first_key, (SEQS,), SEQ_LEN // 4, SEQ_LEN + 1)
    longest = jax.random.randint(second_key, (), 0, SEQS)
    return jnp.where(jnp.arange(SEQS) == longest, SEQ_LEN, drawn).astype(jnp.int32)


def strengthened(array, rng, source, target, shards_of, factor):
    def block_of(position):
        return (jnp.arange(array.shape[position]) // (array.shape[position] // shards_of)).reshape((-1,) + (1,) * (array.ndim - 1 - position))

    one_side = jax.random.permutation(rng, shards_of)[block_of(target)]
    second = (block_of(target) + shards_of // 2) % shards_of
    return jnp.where((block_of(source) == one_side) | (block_of(source) == second), factor * array, array)


def block_levels(key, extent, shards, smallest, high):
    factor_of = 1.0
    for dim, blocks in shards:
        heights = jax.random.uniform(jax.random.fold_in(jax.random.fold_in(key, 6), dim), (blocks,), jnp.float32, smallest / len(shards), high / len(shards))
        factor_of = factor_of * jnp.repeat(jnp.exp(heights), extent[dim] // blocks).reshape((-1,) + (1,) * (len(extent) - 1 - dim))
    return factor_of


def shared_out(rng, own, number, rows, number_of, top, reach, skew):
    ranking = jax.random.permutation(rng, number_of)
    packed, common = portions_of(number_of, rows * top, reach, skew, True), portions_of(number_of, rows * top, reach, skew, False)
    places = jnp.arange(number_of)

    def named(sizes, rotation):
        used = int((sizes > 0).sum())
        fixed = max(1, used // 4)
        passed = fixed + (places - fixed + rotation * (used - fixed)) % max(1, number_of - fixed)
        return jnp.zeros((number_of,), jnp.int32).at[ranking[jnp.where(places < fixed, places, passed)]].set(jnp.asarray(sizes, jnp.int32))

    sizes = jnp.where(number % 4 == 0, named(packed, number // 4), named(common, number - number // 4 - 1))
    mixed = jax.random.permutation(jax.random.fold_in(own, 3), number_of)
    donor, taker = mixed[0:number_of // 2 * 2:2], mixed[1:number_of // 2 * 2:2]
    margin = jnp.minimum(sizes[donor] - 1, reach - sizes[taker]) // 2
    margin = jnp.where((donor == ranking[0]) | (taker == ranking[0]) | (sizes[taker] == 0), 0, jnp.maximum(margin, 0))
    passed = jax.random.randint(jax.random.fold_in(own, 4), (number_of // 2,), 0, 1 << 20) % (margin + 1)
    sizes = sizes.at[donor].add(-passed).at[taker].add(passed)
    items = jnp.searchsorted(jnp.cumsum(sizes), jnp.arange(rows * top), side="right").astype(jnp.int32)
    listing = items.reshape(top, rows).T
    listing = listing[jax.random.permutation(jax.random.fold_in(own, 1), rows)]
    rotation = jax.random.randint(jax.random.fold_in(own, 2), (rows, 1), 0, top)
    return jnp.take_along_axis(listing, (jnp.arange(top)[None, :] + rotation) % top, axis=1)


def portions_of(number_of, total, reach, skew, full):
    portions = [(1 << 20) // math.isqrt(rank ** skew) + 1 for rank in range(1, number_of + 1)]
    largest = reach if full else min(reach, max(-(-total // number_of), total * portions[0] // sum(portions)))
    least = 1 if total - largest >= number_of - 1 else 0
    given, surplus = [largest] + [least] * (number_of - 1), total - largest - least * (number_of - 1)
    while surplus > 0:
        movable = [i for i in range(1, number_of) if given[i] < largest] or [i for i in range(1, number_of) if given[i] < reach]
        pool, remaining = sum([portions[i] for i in movable]), surplus
        for i in movable:
            more = min(reach - given[i], max(1, remaining * portions[i] // pool), surplus)
            given[i] = given[i] + more
            surplus = surplus - more
    return np.array(given)


def bell_draw(key, shape, scale, limit, cuts=(), held_as=jnp.bfloat16):
    values = scale * jax.random.normal(key, shape, jnp.float32)
    if cuts:
        values = values * block_levels(key, shape, cuts, -0.22, 0.18)
    return jnp.clip(values, -limit, limit).astype(held_as)


def gaussian_with(own_key, extent, deviation, bound, cuts, heavy, held_as=jnp.bfloat16):
    result = deviation * jax.random.normal(own_key, extent, jnp.float32)
    if cuts:
        result = result * block_levels(own_key, extent, cuts, -0.22, 0.18)
    return jnp.clip(strengthened(result, jax.random.fold_in(own_key, 3), *heavy), -bound, bound).astype(held_as)


def setup_inputs(seed: int = 0) -> dict:
    keys = jax.random.split(jax.random.key(seed), 17)
    tokens = gaussian_with(keys[0], (SEQS, SEQ_LEN, D), 1.0, 6.0, ((0, 4), (1, 8)), (1, 2, 8, 2.0))
    cotangent = bell_draw(keys[1], (SEQS, SEQ_LEN, D), 1.0, 6.0, ((0, 4), (1, 8)))
    lengths = draw_lengths(jax.random.fold_in(keys[16], 71), 0)
    routes_keys = jax.random.split(jax.random.fold_in(keys[3], 1), SEQS * SEQ_LEN // TOK_DEV)
    routes_turns = jax.random.permutation(jax.random.fold_in(keys[3], 3), SEQS * SEQ_LEN // TOK_DEV)
    routes = jax.vmap(lambda own, number: shared_out(jax.random.fold_in(keys[3], 2), own, number, TOK_DEV, EXPERTS, TOP, MOST, 1))(routes_keys, routes_turns).reshape((SEQS, SEQ_LEN, TOP))
    w_query = bell_draw(keys[4], (D, D), D ** -0.5, 0.125, ((0, 32),), jnp.float32)
    w_key = bell_draw(keys[5], (D, D), D ** -0.5, 0.125, ((0, 32),), jnp.float32)
    w_value = bell_draw(keys[6], (D, D), D ** -0.5, 0.125, ((0, 32),), jnp.float32)
    w_output = bell_draw(keys[7], (D, D), (D // 16) ** -0.5, 0.5, ((0, 32),), jnp.float32)
    router = bell_draw(keys[8], (D, EXPERTS), (4 * D) ** -0.5, 0.0625, ((0, 32),), jnp.float32)
    gain_attn = jnp.clip(1.0 + 0.1 * jax.random.normal(keys[9], (D,), jnp.float32), 0.5, 1.5)
    gain_query = jnp.clip(1.0 + 0.1 * jax.random.normal(keys[10], (D,), jnp.float32), 0.5, 1.5)
    gain_key = jnp.clip(1.0 + 0.1 * jax.random.normal(keys[11], (D,), jnp.float32), 0.5, 1.5)
    gain_mlp = jnp.clip(1.0 + 0.1 * jax.random.normal(keys[12], (D,), jnp.float32), 0.5, 1.5)
    w_gate = bell_draw(keys[13], (EXPERTS, D, FF), D ** -0.5, 0.125, ((0, 8), (2, 4)), jnp.float32)
    w_up = bell_draw(keys[14], (EXPERTS, D, FF), D ** -0.5, 0.125, ((0, 8), (2, 4)), jnp.float32)
    w_down = bell_draw(keys[15], (EXPERTS, FF, D), (FF // 8) ** -0.5, 0.5, ((0, 8), (1, 4)), jnp.float32)
    return dict(tokens=tokens, cotangent=cotangent, lengths=lengths, routes=routes, w_query=w_query, w_key=w_key, w_value=w_value, w_output=w_output, router=router, gain_attn=gain_attn, gain_query=gain_query, gain_key=gain_key, gain_mlp=gain_mlp, w_gate=w_gate, w_up=w_up, w_down=w_down)


@jax.custom_vjp
def low(v):
    return lax.optimization_barrier(v.astype(jnp.bfloat16)).astype(jnp.float32)

@jax.custom_vjp
def low_back(v):
    return v

def low_keep(v):
    return (low(v), None)

def low_pass(kept, grad):
    return (grad,)

def back_keep(v):
    return (v, None)

def back_low(kept, grad):
    return (low(grad),)
low.defvjp(low_keep, low_pass)
low_back.defvjp(back_keep, back_low)
PRECISE = lax.Precision.HIGHEST
EPSILON = 1e-05
ROPE_BASE = 10000.0
MASKED = -1e+30

def rms_scaled(values, gain):
    return values * lax.rsqrt(lax.optimization_barrier(jnp.mean(values * values, axis=-1, keepdims=True)) + EPSILON) * gain

def rotate(values, positions):
    half_dim = HEAD_DIM // 2
    frequency = ROPE_BASE ** (-2.0 * jnp.arange(half_dim).astype(jnp.float32) / HEAD_DIM)
    angles = positions.astype(jnp.float32)[:, None] * frequency[None, :]
    cosine = jnp.cos(angles)[:, None, :]
    sine_part = jnp.sin(angles)[:, None, :]
    front_half = values[..., :half_dim]
    behind = values[..., half_dim:]
    return jnp.concatenate([front_half * cosine - behind * sine_part, behind * cosine + front_half * sine_part], axis=-1)

def attend_sequence(query, key_rows, value_rows, length):
    block_rows = min(512, SEQ_LEN)
    factor = HEAD_DIM ** (-0.5)
    key_place = jnp.arange(SEQ_LEN)

    def one_block(inputs):
        query_block, offset = inputs
        scores = low_back(jnp.einsum('qhd,khd->hqk', query_block, key_rows, precision=PRECISE) * factor)
        query_place = offset + jnp.arange(block_rows)
        allowed = (key_place[None, :] <= query_place[:, None]) & (key_place[None, :] < length)
        scores = jnp.where(allowed[None], scores, MASKED)
        log_total = jax.nn.logsumexp(scores, axis=-1, keepdims=True)
        weights = low(jnp.where(allowed[None], jnp.exp(scores - log_total), 0.0))
        return jnp.einsum('hqk,khd->qhd', weights, value_rows, precision=PRECISE)
    block_count = SEQ_LEN // block_rows
    blocks = query.reshape(block_count, block_rows, HEADS, HEAD_DIM)
    offsets = jnp.arange(block_count) * block_rows
    attended = lax.map(jax.checkpoint(one_block), (blocks, offsets))
    return attended.reshape(SEQ_LEN, D)

def mix_experts(normed, gate_probs, routes, w_gate, w_up, w_down):
    capacity = N_EXPERT * MOST
    flat_routes = routes.reshape(-1)
    flat_gates = gate_probs.reshape(-1)

    def add_expert(running, inputs):
        number, gate_matrix, up_matrix, down_matrix = inputs
        picked = flat_routes == number
        pair_ids = jnp.nonzero(picked, size=capacity, fill_value=0)[0].astype(jnp.int32)
        living = jnp.arange(capacity) < jnp.sum(picked.astype(jnp.int32))
        token_ids = pair_ids // TOP
        rows_in = low_back(normed[token_ids])
        gate_pre = low_back(jnp.dot(rows_in, gate_matrix, precision=PRECISE))
        up_pre = low_back(jnp.dot(rows_in, up_matrix, precision=PRECISE))
        activity = low(jax.nn.silu(gate_pre) * up_pre)
        rows_out = low_back(low(jnp.dot(activity, down_matrix, precision=PRECISE)))
        weighting = jnp.where(living, flat_gates[pair_ids], 0.0)
        return (running.at[token_ids].add(weighting[:, None] * rows_out), None)
    mixture, unused = lax.scan(jax.checkpoint(add_expert), jnp.zeros_like(normed), (jnp.arange(EXPERTS).astype(jnp.int32), w_gate, w_up, w_down))
    return mixture

def one_sequence(tokens, length, routes, params):
    w_query, w_key, w_value, w_output, router, gain_attn, gain_query, gain_key, gain_mlp, w_gate, w_up, w_down = params
    positions = jnp.arange(SEQ_LEN)
    attn_in = low(rms_scaled(tokens, gain_attn))
    query_pre = low_back(jnp.dot(attn_in, w_query, precision=PRECISE))
    key_pre = low_back(jnp.dot(attn_in, w_key, precision=PRECISE))
    value_rows = low(low_back(jnp.dot(attn_in, w_value, precision=PRECISE)))
    query = low(low_back(rotate(rms_scaled(query_pre, gain_query).reshape(SEQ_LEN, HEADS, HEAD_DIM), positions)))
    key_rows = low(low_back(rotate(rms_scaled(key_pre, gain_key).reshape(SEQ_LEN, HEADS, HEAD_DIM), positions)))
    attended = low(low_back(attend_sequence(query, key_rows, value_rows.reshape(SEQ_LEN, HEADS, HEAD_DIM), length)))
    hidden = tokens + low_back(jnp.dot(attended, w_output, precision=PRECISE))
    normed = low(rms_scaled(hidden, gain_mlp))
    logits = jnp.dot(normed, router, precision=PRECISE)
    gate_probs = jax.nn.softmax(jnp.take_along_axis(logits, routes, axis=1), axis=-1)
    return hidden + mix_experts(normed, gate_probs, routes, w_gate, w_up, w_down)

def reference(tokens, cotangent, lengths, routes, w_query, w_key, w_value, w_output, router, gain_attn, gain_query, gain_key, gain_mlp, w_gate, w_up, w_down):
    params = (w_query, w_key, w_value, w_output, router, gain_attn, gain_query, gain_key, gain_mlp, w_gate, w_up, w_down)

    def forward(inputs, weight_set):
        rounded = tuple((low(weight) for weight in weight_set))

        def per_sequence(state_in, pieces):
            return (state_in, one_sequence(pieces[0], pieces[1], pieces[2], rounded))
        unused, outputs = lax.scan(per_sequence, jnp.zeros((), jnp.float32), (inputs, lengths, routes))
        return outputs
    output, pullback = jax.vjp(forward, tokens.astype(jnp.float32), params)
    grad_tokens, weight_grads = pullback(cotangent.astype(jnp.float32))
    return (output.astype(jnp.bfloat16), grad_tokens.astype(jnp.bfloat16), weight_grads[0], weight_grads[1], weight_grads[2], weight_grads[3], weight_grads[4], weight_grads[5], weight_grads[6], weight_grads[7], weight_grads[8], weight_grads[9], weight_grads[10], weight_grads[11])
```

```python
import jax
import jax.numpy as jnp
from jax import lax
from jax.sharding import PartitionSpec as P

HEAD_DIM = 128
TOP = 8


PRECISE = lax.Precision.HIGHEST
EPSILON = 1e-05
ROPE_BASE = 10000.0
MASKED = -1e30


def rms_parts(values, gain):
    factor = lax.rsqrt(jnp.mean(values * values, axis=-1, keepdims=True) + EPSILON)
    normal = values * factor
    return (normal * gain, normal, factor)


def rms_back(upstream, normal, factor, gain):
    scaled = upstream * gain
    inner_mean = jnp.mean(scaled * normal, axis=-1, keepdims=True)
    return (factor * (scaled - normal * inner_mean), jnp.sum(upstream * normal, axis=0))


def rope_tables(positions):
    half_dim = HEAD_DIM // 2
    frequency = ROPE_BASE ** (-2.0 * jnp.arange(half_dim).astype(jnp.float32) / HEAD_DIM)
    angles = positions.astype(jnp.float32)[:, None] * frequency[None, :]
    return (jnp.cos(angles)[:, None, :], jnp.sin(angles)[:, None, :])


def rotate(values, cosine, sine_part, direction):
    half_dim = values.shape[-1] // 2
    front_half = values[..., :half_dim]
    behind = values[..., half_dim:]
    return jnp.concatenate(
        [
            front_half * cosine - direction * behind * sine_part,
            behind * cosine + direction * front_half * sine_part,
        ],
        axis=-1,
    )


def contract_rows(left_side, right_side):
    return lax.dot_general(
        left_side, right_side, (((0,), (0,)), ((), ())), preferred_element_type=jnp.float32
    )


def times_transpose(left_side, right_side):
    return lax.dot_general(
        left_side, right_side, (((1,), (1,)), ((), ())), preferred_element_type=jnp.float32
    )


def score_grads(
    query_heads,
    key_heads,
    value_heads,
    grad_heads,
    log_total,
    row_delta,
    query_place,
    key_place,
    length,
):
    factor = HEAD_DIM ** (-0.5)
    scores = (
        jnp.einsum("qhd,khd->hqk", query_heads, key_heads, preferred_element_type=jnp.float32)
        * factor
    )
    allowed = (key_place[None, :] <= query_place[:, None]) & (key_place[None, :] < length)
    weights_full = jnp.where(allowed[None], jnp.exp(scores - log_total[:, :, None]), 0.0)
    grad_weights = jnp.einsum(
        "qhd,khd->hqk", grad_heads, value_heads, preferred_element_type=jnp.float32
    )
    grad_scores = (weights_full * (grad_weights - row_delta[:, :, None])).astype(jnp.bfloat16)
    return (weights_full.astype(jnp.bfloat16), grad_scores)


def per_device(
    tokens,
    cotangent,
    lengths,
    routes,
    w_query,
    w_key,
    w_value,
    w_output,
    router,
    gain_attn,
    gain_query,
    gain_key,
    gain_mlp,
    w_gate,
    w_up,
    w_down,
):
    tok_rows = tokens.shape[1]
    model_width = tokens.shape[2]
    head_count = model_width // HEAD_DIM
    groups = lax.axis_size("expert")
    seq_len = tok_rows * groups
    length = lengths[0]
    factor = HEAD_DIM ** (-0.5)
    gathered = (
        lax.all_gather(w_query.astype(jnp.bfloat16), ("dp", "expert"), axis=0, tiled=True),
        lax.all_gather(w_key.astype(jnp.bfloat16), ("dp", "expert"), axis=0, tiled=True),
        lax.all_gather(w_value.astype(jnp.bfloat16), ("dp", "expert"), axis=0, tiled=True),
        lax.all_gather(w_output.astype(jnp.bfloat16), ("dp", "expert"), axis=0, tiled=True),
        lax.all_gather(router.astype(jnp.bfloat16), ("dp", "expert"), axis=0, tiled=True),
        lax.all_gather(gain_attn.astype(jnp.bfloat16), ("dp", "expert"), axis=0, tiled=True),
        lax.all_gather(gain_query.astype(jnp.bfloat16), ("dp", "expert"), axis=0, tiled=True),
        lax.all_gather(gain_key.astype(jnp.bfloat16), ("dp", "expert"), axis=0, tiled=True),
        lax.all_gather(gain_mlp.astype(jnp.bfloat16), ("dp", "expert"), axis=0, tiled=True),
    )
    query_weight, key_weight, value_weight, output_weight, router_weight = (
        gathered[0],
        gathered[1],
        gathered[2],
        gathered[3],
        gathered[4],
    )
    attn_gain = gathered[5].astype(jnp.float32)
    query_gain = gathered[6].astype(jnp.float32)
    key_gain = gathered[7].astype(jnp.float32)
    mlp_gain = gathered[8].astype(jnp.float32)
    gate_weight, up_weight, down_weight = (
        lax.all_gather(w_gate.astype(jnp.bfloat16), "dp", axis=2, tiled=True),
        lax.all_gather(w_up.astype(jnp.bfloat16), "dp", axis=2, tiled=True),
        lax.all_gather(w_down.astype(jnp.bfloat16), "dp", axis=1, tiled=True),
    )
    token_rows = tokens[0].astype(jnp.float32)
    attn_in, attn_normal, attn_factor = rms_parts(token_rows, attn_gain)
    attn_low = attn_in.astype(jnp.bfloat16)
    query_pre = jnp.dot(attn_low, query_weight, preferred_element_type=jnp.float32)
    key_pre = jnp.dot(attn_low, key_weight, preferred_element_type=jnp.float32)
    value_low = jnp.dot(attn_low, value_weight, preferred_element_type=jnp.float32).astype(
        jnp.bfloat16
    )
    query_norm, query_normal, query_factor = rms_parts(query_pre, query_gain)
    key_norm, key_normal, key_factor = rms_parts(key_pre, key_gain)
    positions = lax.axis_index("expert") * tok_rows + jnp.arange(tok_rows)
    cosine, sine_part = rope_tables(positions)
    query_low = rotate(
        query_norm.reshape(tok_rows, head_count, HEAD_DIM), cosine, sine_part, 1.0
    ).astype(jnp.bfloat16)
    key_low = (
        rotate(key_norm.reshape(tok_rows, head_count, HEAD_DIM), cosine, sine_part, 1.0)
        .astype(jnp.bfloat16)
        .reshape(tok_rows, model_width)
    )
    whole_keys, whole_values = (
        lax.all_gather(key_low, "expert", axis=0, tiled=True),
        lax.all_gather(value_low, "expert", axis=0, tiled=True),
    )
    all_keys = whole_keys.reshape(seq_len, head_count, HEAD_DIM)
    all_values = whole_values.reshape(seq_len, head_count, HEAD_DIM)
    key_place = jnp.arange(seq_len)
    allowed = (key_place[None, :] <= positions[:, None]) & (key_place[None, :] < length)
    scores = (
        jnp.einsum("qhd,khd->hqk", query_low, all_keys, preferred_element_type=jnp.float32) * factor
    )
    scores = jnp.where(allowed[None], scores, MASKED)
    log_total = jax.nn.logsumexp(scores, axis=-1)
    weights_low = jnp.where(allowed[None], jnp.exp(scores - log_total[:, :, None]), 0.0).astype(
        jnp.bfloat16
    )
    attended = jnp.einsum(
        "hqk,khd->qhd", weights_low, all_values, preferred_element_type=jnp.float32
    ).reshape(tok_rows, model_width)
    attended_low = attended.astype(jnp.bfloat16)
    hidden = token_rows + jnp.dot(attended_low, output_weight, preferred_element_type=jnp.float32)
    mlp_in, mlp_normal, mlp_factor = rms_parts(hidden, mlp_gain)
    mlp_low = mlp_in.astype(jnp.bfloat16)
    logits = jnp.dot(mlp_low, router_weight, preferred_element_type=jnp.float32)
    route_ids = routes[0]
    gate_probs = jax.nn.softmax(jnp.take_along_axis(logits, route_ids, axis=1), axis=-1)
    experts = router_weight.shape[1]
    slot_cap = 2 * tok_rows * TOP // experts
    local_count = experts // groups
    pair_count = tok_rows * TOP
    flat_routes = route_ids.reshape(-1)
    expert_ids = jnp.arange(experts)
    hit_table = (flat_routes[:, None] == expert_ids[None, :]).astype(jnp.int32)
    slot_rank = jnp.sum((jnp.cumsum(hit_table, axis=0) - hit_table) * hit_table, axis=1)
    counts = jnp.sum(hit_table, axis=0)
    slot_ids = flat_routes * slot_cap + slot_rank
    slot_pair = (
        jnp.zeros((experts * slot_cap,), jnp.int32)
        .at[slot_ids]
        .set(jnp.arange(pair_count, dtype=jnp.int32))
    )
    send_rows = mlp_low[slot_pair // TOP].reshape(groups, local_count, slot_cap, model_width)
    send_counts = counts.reshape(groups, local_count).astype(jnp.bfloat16)
    arrived_rows, arrived_counts = (
        lax.all_to_all(send_rows, "expert", split_axis=0, concat_axis=0, tiled=True),
        lax.all_to_all(send_counts, "expert", split_axis=0, concat_axis=0, tiled=True),
    )
    living = (jnp.arange(slot_cap)[None, None, :] < arrived_counts.astype(jnp.int32)[:, :, None])[
        ..., None
    ]
    gate_pre = jnp.einsum(
        "nemd,edf->nemf", arrived_rows, gate_weight, preferred_element_type=jnp.float32
    )
    up_pre = jnp.einsum(
        "nemd,edf->nemf", arrived_rows, up_weight, preferred_element_type=jnp.float32
    )
    gate_sigmoid = jax.nn.sigmoid(gate_pre)
    activity = (gate_pre * gate_sigmoid * up_pre).astype(jnp.bfloat16)
    expert_out = jnp.einsum(
        "nemf,efd->nemd", activity, down_weight, preferred_element_type=jnp.float32
    ).astype(jnp.bfloat16)
    returned = lax.all_to_all(expert_out, "expert", split_axis=0, concat_axis=0, tiled=True)
    pair_out = (
        returned.reshape(experts * slot_cap, model_width)[slot_ids]
        .reshape(tok_rows, TOP, model_width)
        .astype(jnp.float32)
    )
    output = hidden + jnp.sum(gate_probs[:, :, None] * pair_out, axis=1)
    grad_out = cotangent[0].astype(jnp.float32)
    grad_gates = jnp.sum(grad_out[:, None, :] * pair_out, axis=-1)
    pair_grad = (
        (gate_probs[:, :, None] * grad_out[:, None, :])
        .astype(jnp.bfloat16)
        .reshape(pair_count, model_width)
    )
    send_grad = pair_grad[slot_pair].reshape(groups, local_count, slot_cap, model_width)
    arrived_grad = lax.all_to_all(send_grad, "expert", split_axis=0, concat_axis=0, tiled=True)
    arrived_grad = jnp.where(living, arrived_grad, jnp.zeros((), jnp.bfloat16))
    grad_activity = jnp.einsum(
        "nemd,efd->nemf", arrived_grad, down_weight, preferred_element_type=jnp.float32
    )
    grad_gate_pre = (
        grad_activity * up_pre * gate_sigmoid * (1.0 + gate_pre * (1.0 - gate_sigmoid))
    ).astype(jnp.bfloat16)
    grad_up_pre = (grad_activity * gate_pre * gate_sigmoid).astype(jnp.bfloat16)
    grad_down = jnp.einsum(
        "nemf,nemd->efd", activity, arrived_grad, preferred_element_type=jnp.float32
    )
    grad_gate = jnp.einsum(
        "nemd,nemf->edf", arrived_rows, grad_gate_pre, preferred_element_type=jnp.float32
    )
    grad_up = jnp.einsum(
        "nemd,nemf->edf", arrived_rows, grad_up_pre, preferred_element_type=jnp.float32
    )
    input_grad = (
        jnp.einsum("nemf,edf->nemd", grad_gate_pre, gate_weight, preferred_element_type=jnp.float32)
        + jnp.einsum("nemf,edf->nemd", grad_up_pre, up_weight, preferred_element_type=jnp.float32)
    ).astype(jnp.bfloat16)
    sent_back = lax.all_to_all(input_grad, "expert", split_axis=0, concat_axis=0, tiled=True)
    grad_mlp_in = jnp.sum(
        sent_back.reshape(experts * slot_cap, model_width)[slot_ids]
        .reshape(tok_rows, TOP, model_width)
        .astype(jnp.float32),
        axis=1,
    )
    grad_chosen = gate_probs * (
        grad_gates - jnp.sum(gate_probs * grad_gates, axis=-1, keepdims=True)
    )
    route_table = (route_ids[:, :, None] == expert_ids[None, None, :]).astype(jnp.float32)
    grad_logits = jnp.sum(grad_chosen[:, :, None] * route_table, axis=1)
    grad_router = jnp.einsum(
        "td,te->de", mlp_low.astype(jnp.float32), grad_logits, precision=PRECISE
    )
    grad_mlp_in = grad_mlp_in + jnp.einsum(
        "te,de->td", grad_logits, router_weight.astype(jnp.float32), precision=PRECISE
    )
    grad_hidden_norm, grad_gain_mlp = rms_back(grad_mlp_in, mlp_normal, mlp_factor, mlp_gain)
    grad_hidden = grad_out + grad_hidden_norm
    grad_attn_low = grad_hidden.astype(jnp.bfloat16)
    grad_w_out = contract_rows(attended_low, grad_attn_low)
    grad_attended = times_transpose(grad_attn_low, output_weight).astype(jnp.bfloat16)
    row_delta = jnp.sum(
        (grad_attended.astype(jnp.float32) * attended).reshape(tok_rows, head_count, HEAD_DIM),
        axis=-1,
    ).T
    grad_heads = grad_attended.reshape(tok_rows, head_count, HEAD_DIM)
    block_rows = min(512, seq_len)
    block_total = seq_len // block_rows

    def key_part(number):
        offset = number * block_rows
        block_keys = lax.dynamic_slice_in_dim(all_keys, offset, block_rows, 0)
        block_values = lax.dynamic_slice_in_dim(all_values, offset, block_rows, 0)
        weights_part, grad_scores = score_grads(
            query_low,
            block_keys,
            block_values,
            grad_heads,
            log_total,
            row_delta,
            positions,
            offset + jnp.arange(block_rows),
            length,
        )
        grad_query_part = (
            jnp.einsum("hqk,khd->qhd", grad_scores, block_keys, preferred_element_type=jnp.float32)
            * factor
        )
        grad_key_part = (
            jnp.einsum("hqk,qhd->khd", grad_scores, query_low, preferred_element_type=jnp.float32)
            * factor
        )
        grad_value_part = jnp.einsum(
            "hqk,qhd->khd", weights_part, grad_heads, preferred_element_type=jnp.float32
        )
        return (
            grad_query_part,
            grad_key_part.reshape(block_rows, model_width),
            grad_value_part.reshape(block_rows, model_width),
        )

    query_parts, key_parts, value_parts = lax.map(
        lambda number: key_part(number), jnp.arange(block_total)
    )
    grad_query = jnp.sum(query_parts, axis=0).reshape(tok_rows, model_width)
    grad_key, grad_value = (
        lax.psum_scatter(
            key_parts.reshape(seq_len, model_width).astype(jnp.bfloat16),
            "expert",
            scatter_dimension=0,
            tiled=True,
        ).astype(jnp.float32),
        lax.psum_scatter(
            value_parts.reshape(seq_len, model_width).astype(jnp.bfloat16),
            "expert",
            scatter_dimension=0,
            tiled=True,
        ).astype(jnp.float32),
    )
    grad_value_low = grad_value.astype(jnp.bfloat16)
    grad_query_rot = (
        grad_query.astype(jnp.bfloat16).astype(jnp.float32).reshape(tok_rows, head_count, HEAD_DIM)
    )
    grad_key_rot = (
        grad_key.astype(jnp.bfloat16).astype(jnp.float32).reshape(tok_rows, head_count, HEAD_DIM)
    )
    grad_query_norm = rotate(grad_query_rot, cosine, sine_part, -1.0).reshape(tok_rows, model_width)
    grad_key_norm = rotate(grad_key_rot, cosine, sine_part, -1.0).reshape(tok_rows, model_width)
    grad_query_pre, grad_gain_query = rms_back(
        grad_query_norm, query_normal, query_factor, query_gain
    )
    grad_key_pre, grad_gain_key = rms_back(grad_key_norm, key_normal, key_factor, key_gain)
    grad_query_low = grad_query_pre.astype(jnp.bfloat16)
    grad_key_low = grad_key_pre.astype(jnp.bfloat16)
    grad_wq = contract_rows(attn_low, grad_query_low)
    grad_wk = contract_rows(attn_low, grad_key_low)
    grad_wv = contract_rows(attn_low, grad_value_low)
    grad_attn_in = (
        times_transpose(grad_query_low, query_weight)
        + times_transpose(grad_key_low, key_weight)
        + times_transpose(grad_value_low, value_weight)
    )
    grad_attn_x, grad_gain_attn = rms_back(grad_attn_in, attn_normal, attn_factor, attn_gain)
    grad_tokens = (grad_hidden + grad_attn_x).astype(jnp.bfloat16)
    summed_grads = (
        lax.psum_scatter(grad_wq, ("dp", "expert"), scatter_dimension=0, tiled=True),
        lax.psum_scatter(grad_wk, ("dp", "expert"), scatter_dimension=0, tiled=True),
        lax.psum_scatter(grad_wv, ("dp", "expert"), scatter_dimension=0, tiled=True),
        lax.psum_scatter(grad_w_out, ("dp", "expert"), scatter_dimension=0, tiled=True),
        lax.psum_scatter(grad_router, ("dp", "expert"), scatter_dimension=0, tiled=True),
        lax.psum_scatter(grad_gain_attn, ("dp", "expert"), scatter_dimension=0, tiled=True),
        lax.psum_scatter(grad_gain_query, ("dp", "expert"), scatter_dimension=0, tiled=True),
        lax.psum_scatter(grad_gain_key, ("dp", "expert"), scatter_dimension=0, tiled=True),
        lax.psum_scatter(grad_gain_mlp, ("dp", "expert"), scatter_dimension=0, tiled=True),
    )
    expert_grads = (
        lax.psum_scatter(
            grad_gate.astype(jnp.bfloat16), "dp", scatter_dimension=2, tiled=True
        ).astype(jnp.float32),
        lax.psum_scatter(
            grad_up.astype(jnp.bfloat16), "dp", scatter_dimension=2, tiled=True
        ).astype(jnp.float32),
        lax.psum_scatter(
            grad_down.astype(jnp.bfloat16), "dp", scatter_dimension=1, tiled=True
        ).astype(jnp.float32),
    )
    return (
        output.astype(jnp.bfloat16)[None],
        grad_tokens[None],
        summed_grads[0],
        summed_grads[1],
        summed_grads[2],
        summed_grads[3],
        summed_grads[4],
        summed_grads[5],
        summed_grads[6],
        summed_grads[7],
        summed_grads[8],
        expert_grads[0],
        expert_grads[1],
        expert_grads[2],
    )


FLIP = [(0, 1), (1, 0)]


def in_order(own, other, index):
    first = jnp.where(index == 0, own, other)
    second = jnp.where(index == 0, other, own)
    return jnp.stack([first, second])


def swap_x(block):
    return lax.ppermute(block, "dx", FLIP)


def swap_y(block):
    return lax.ppermute(block, "dy", FLIP)


def swap_core(block):
    groups = lax.axis_size("expert")
    return lax.ppermute(block, "expert", [(i, i ^ 1) for i in range(groups)])


def gather_quad(block):
    pair = in_order(block, swap_x(block), lax.axis_index("dx"))
    return in_order(pair, swap_y(pair), lax.axis_index("dy"))


def scatter_quad(blocks):
    column, row = lax.axis_index("dx"), lax.axis_index("dy")
    low = jnp.bfloat16
    sent = lax.dynamic_index_in_dim(blocks, 1 - column, 1, keepdims=False).astype(low)
    kept = lax.dynamic_index_in_dim(blocks, column, 1, keepdims=False).astype(jnp.float32)
    half = kept + swap_x(sent).astype(jnp.float32)
    sent = lax.dynamic_index_in_dim(half, 1 - row, 0, keepdims=False).astype(low)
    kept = lax.dynamic_index_in_dim(half, row, 0, keepdims=False)
    return kept + swap_y(sent).astype(jnp.float32)


def sum_experts(values):
    groups = lax.axis_size("expert")
    flat = values.reshape(-1, 128)
    spread = jnp.broadcast_to(flat[None], (groups,) + flat.shape)
    arrived = lax.all_to_all(spread, "expert", split_axis=0, concat_axis=0)
    return jnp.sum(arrived, axis=0).reshape(values.shape)


def dense_gates(logits, route_ids):
    columns = jnp.arange(logits.shape[-1])
    chosen = jnp.any(route_ids[:, :, None] == columns[None, None, :], axis=1)
    highest = jnp.max(jnp.where(chosen, logits, -jnp.inf), axis=-1, keepdims=True)
    weights = jnp.where(chosen, jnp.exp(logits - highest), 0.0)
    return weights / jnp.sum(weights, axis=-1, keepdims=True)


def expert_block(rows_in, grad_rows, gates, gate_w, up_w, down_w):
    wide = jnp.float32
    gate_pre = jnp.einsum("td,edf->etf", rows_in, gate_w, preferred_element_type=wide)
    up_pre = jnp.einsum("td,edf->etf", rows_in, up_w, preferred_element_type=wide)
    back = jnp.einsum("td,efd->etf", grad_rows, down_w, preferred_element_type=wide)
    sigmoid = jax.nn.sigmoid(gate_pre)
    silu = gate_pre * sigmoid
    activity = silu * up_pre
    gate_grads = jnp.sum(activity * back, axis=-1)
    weight = gates.T[:, :, None]
    scaled = (activity * weight).astype(jnp.bfloat16)
    back = back * weight
    grad_gate_pre = (back * up_pre * sigmoid * (1.0 + gate_pre * (1.0 - sigmoid))).astype(
        jnp.bfloat16
    )
    grad_up_pre = (back * silu).astype(jnp.bfloat16)
    grad_in = (
        jnp.einsum("etf,edf->td", grad_gate_pre, gate_w, preferred_element_type=wide)
        + jnp.einsum("etf,edf->td", grad_up_pre, up_w, preferred_element_type=wide)
    ).astype(jnp.bfloat16)
    mixed = jnp.einsum("etf,efd->td", scaled, down_w, preferred_element_type=wide).astype(
        jnp.bfloat16
    )
    return (grad_in, mixed, gate_grads, scaled, grad_gate_pre, grad_up_pre)


def per_device_by_heads(
    tokens,
    cotangent,
    lengths,
    routes,
    w_query,
    w_key,
    w_value,
    w_output,
    router,
    gain_attn,
    gain_query,
    gain_key,
    gain_mlp,
    w_gate,
    w_up,
    w_down,
):
    low, wide = jnp.bfloat16, jnp.float32
    everyone = ("dy", "dx", "expert")
    tok_rows, model_width = tokens.shape[1], tokens.shape[2]
    groups = lax.axis_size("expert")
    devices = 4 * groups
    chips = groups // 2
    seq_len = tok_rows * groups
    shard = w_query.shape[0]
    experts = router.shape[1]
    local_count = experts // groups
    group = lax.axis_index("expert")
    chip, core = group // 2, group % 2
    column, row = lax.axis_index("dx"), lax.axis_index("dy")
    length = lengths[0]
    factor = HEAD_DIM ** (-0.5)
    own_width = 2 * HEAD_DIM
    tok, cot = tokens[0], cotangent[0]

    packed = jnp.concatenate(
        [router.T, gain_attn[None], gain_query[None], gain_key[None], gain_mlp[None]], axis=0
    ).astype(low)
    pack_rows = experts + 4
    packed = packed.reshape(-1, 128)
    packed = lax.all_to_all(
        jnp.broadcast_to(packed[None], (devices,) + packed.shape),
        everyone,
        split_axis=0,
        concat_axis=0,
    )
    packed = (
        packed.reshape(devices, pack_rows, shard).transpose(1, 0, 2).reshape(pack_rows, model_width)
    )
    router_t = packed[:experts]
    attn_gain, query_gain, key_gain, mlp_gain = (
        packed[experts + i].astype(wide) for i in range(4)
    )

    def own_heads(vector):
        blocks = vector.reshape(2, 2, chips, HEAD_DIM)
        blocks = lax.dynamic_index_in_dim(blocks, core, 0, keepdims=False)
        return lax.dynamic_index_in_dim(blocks, chip, 1, keepdims=False).reshape(own_width)

    def spread_heads(vector):
        at_core = (jnp.arange(2) == core)[:, None, None, None]
        at_chip = (jnp.arange(chips) == chip)[None, None, :, None]
        return jnp.where(
            at_core & at_chip, vector.reshape(1, 2, 1, HEAD_DIM), 0.0
        ).reshape(model_width)

    def by_heads(weight):
        blocks = weight.astype(low).reshape(shard, 2, 2, chips, HEAD_DIM)
        return blocks.transpose(3, 1, 0, 2, 4).reshape(groups, shard, own_width)

    sent = jnp.concatenate([by_heads(w_query), by_heads(w_key), by_heads(w_value)], axis=2)
    arrived = lax.all_to_all(sent, "expert", split_axis=0, concat_axis=0)
    qkv_w = gather_quad(arrived.reshape(groups * shard, 3 * own_width)).reshape(
        model_width, 3 * own_width
    )
    tok_all = lax.all_gather(tok, "expert", axis=0, tiled=True)

    out_quad = gather_quad(w_output.astype(low))
    out_own = lax.dynamic_index_in_dim(out_quad, core, 0, keepdims=False)
    out_other = swap_core(lax.dynamic_index_in_dim(out_quad, 1 - core, 0, keepdims=False))
    out_w = jnp.moveaxis(in_order(out_own, out_other, core), 0, 1).reshape(own_width, model_width)

    gate_w, up_w, down_w = w_gate.astype(low), w_up.astype(low), w_down.astype(low)
    gate_w = jnp.concatenate([gate_w, swap_x(gate_w)], axis=2)
    up_w = jnp.concatenate([up_w, swap_x(up_w)], axis=2)
    down_w = jnp.concatenate([down_w, swap_x(down_w)], axis=1)
    block_width = w_gate.shape[2]

    route_pair = jnp.stack([routes[0], swap_y(routes[0])]).reshape(-1, 128)
    route_pair = lax.all_to_all(
        jnp.broadcast_to(route_pair[None], (groups,) + route_pair.shape),
        "expert",
        split_axis=0,
        concat_axis=0,
    ).reshape(groups, 2, tok_rows, TOP)
    cot_all = lax.all_gather(cot, "expert", axis=0, tiled=True)
    cot_near = lax.all_gather(swap_y(cot), "expert", axis=0, tiled=True)

    all_normal_in = tok_all.astype(wide)
    attn_in, attn_normal, _ = rms_parts(all_normal_in, attn_gain)
    attn_low = attn_in.astype(low)
    qkv = jnp.dot(attn_low, qkv_w, preferred_element_type=wide)
    query_pre, key_pre = qkv[:, :own_width], qkv[:, own_width : 2 * own_width]
    value_low = qkv[:, 2 * own_width :].astype(low)
    squares = jnp.stack([jnp.sum(query_pre * query_pre, axis=1), jnp.sum(key_pre * key_pre, axis=1)])
    squares = sum_experts(squares)
    factors = lax.rsqrt(squares / model_width + EPSILON)
    query_factor, key_factor = factors[0][:, None], factors[1][:, None]
    query_gain_own, key_gain_own = own_heads(query_gain), own_heads(key_gain)
    query_normal, key_normal = query_pre * query_factor, key_pre * key_factor
    positions = jnp.arange(seq_len)
    cosine, sine_part = rope_tables(positions)

    def turned(values, direction):
        return rotate(values.reshape(seq_len, 2, HEAD_DIM), cosine, sine_part, direction)

    query_low = turned(query_normal * query_gain_own, 1.0).astype(low)
    key_low = turned(key_normal * key_gain_own, 1.0).astype(low)
    values = value_low.reshape(seq_len, 2, HEAD_DIM)

    allowed = (positions[None, :] <= positions[:, None]) & (positions[None, :] < length)
    scores = jnp.einsum("qhd,khd->hqk", query_low, key_low, preferred_element_type=wide) * factor
    scores = jnp.where(allowed[None], scores, MASKED)
    log_total = jax.nn.logsumexp(scores, axis=-1)
    weights_low = jnp.where(allowed[None], jnp.exp(scores - log_total[:, :, None]), 0.0).astype(low)
    attended = jnp.einsum("hqk,khd->qhd", weights_low, values, preferred_element_type=wide).reshape(
        seq_len, own_width
    )
    attended_low = attended.astype(low)
    attn_part = jnp.dot(attended_low, out_w, preferred_element_type=wide).astype(low)
    attn_out = lax.psum_scatter(attn_part, "expert", scatter_dimension=0, tiled=True)
    hidden = tok.astype(wide) + attn_out.astype(wide)
    mlp_in, mlp_normal, mlp_factor = rms_parts(hidden, mlp_gain)
    mlp_low = mlp_in.astype(low)
    gates_own = dense_gates(times_transpose(mlp_low, router_t), routes[0])

    rows_own = lax.all_gather(mlp_low, "expert", axis=0, tiled=True)
    rows_near = lax.all_gather(swap_y(mlp_low), "expert", axis=0, tiled=True)

    def expert_part(rows_in, grad_rows, number):
        ids = route_pair[:, number].reshape(seq_len, TOP)
        gates = dense_gates(times_transpose(rows_in, router_t), ids)
        gates = lax.dynamic_slice_in_dim(gates, group * local_count, local_count, 1)
        return expert_block(rows_in, grad_rows, gates, gate_w, up_w, down_w)

    part_own = expert_part(rows_own, cot_all, 0)
    part_near = expert_part(rows_near, cot_near, 1)

    def home(own, near):
        own = lax.psum_scatter(own, "expert", scatter_dimension=0, tiled=True)
        near = lax.psum_scatter(near, "expert", scatter_dimension=0, tiled=True)
        return own.astype(wide) + swap_y(near).astype(wide)

    gate_grads = jnp.stack([part_own[2], part_near[2]])
    gate_grads = gate_grads.reshape(2, local_count, groups, tok_rows).transpose(2, 0, 1, 3)
    gate_grads = lax.all_to_all(gate_grads, "expert", split_axis=0, concat_axis=0)
    gate_grads = gate_grads.transpose(1, 3, 0, 2).reshape(2, tok_rows, experts)
    gate_grads = gate_grads[0] + swap_y(gate_grads[1])

    grad_mlp_in = home(part_own[0], part_near[0])
    grad_logits = gates_own * (gate_grads - jnp.sum(gates_own * gate_grads, axis=-1, keepdims=True))
    grad_router = jnp.einsum("te,td->ed", grad_logits, mlp_low.astype(wide), precision=PRECISE)
    grad_mlp_in = grad_mlp_in + jnp.einsum(
        "te,ed->td", grad_logits, router_t.astype(wide), precision=PRECISE
    )
    grad_out = cot.astype(wide)
    grad_hidden_norm, grad_gain_mlp = rms_back(grad_mlp_in, mlp_normal, mlp_factor, mlp_gain)
    grad_hidden = grad_out + grad_hidden_norm
    grad_attn_all = lax.all_gather(grad_hidden.astype(low), "expert", axis=0, tiled=True)

    grad_w_out = contract_rows(attended_low, grad_attn_all)
    grad_attended = times_transpose(grad_attn_all, out_w).astype(low)
    grad_heads = grad_attended.reshape(seq_len, 2, HEAD_DIM)
    row_delta = jnp.sum(
        grad_heads.astype(wide) * attended.reshape(seq_len, 2, HEAD_DIM), axis=-1
    ).T
    weights_part, grad_scores = score_grads(
        query_low,
        key_low,
        values,
        grad_heads,
        log_total,
        row_delta,
        positions,
        positions,
        length,
    )
    grad_query = (
        jnp.einsum("hqk,khd->qhd", grad_scores, key_low, preferred_element_type=wide) * factor
    ).astype(low)
    grad_key = (
        jnp.einsum("hqk,qhd->khd", grad_scores, query_low, preferred_element_type=wide) * factor
    ).astype(low)
    grad_value_low = (
        jnp.einsum("hqk,qhd->khd", weights_part, grad_heads, preferred_element_type=wide)
        .astype(low)
        .reshape(seq_len, own_width)
    )
    grad_query_norm = turned(grad_query.astype(wide), -1.0).reshape(seq_len, own_width)
    grad_key_norm = turned(grad_key.astype(wide), -1.0).reshape(seq_len, own_width)
    grad_gain_query = jnp.sum(grad_query_norm * query_normal, axis=0)
    grad_gain_key = jnp.sum(grad_key_norm * key_normal, axis=0)
    query_scaled, key_scaled = grad_query_norm * query_gain_own, grad_key_norm * key_gain_own
    inner = jnp.stack(
        [jnp.sum(query_scaled * query_normal, axis=1), jnp.sum(key_scaled * key_normal, axis=1)]
    )
    inner = sum_experts(inner) / model_width
    grad_query_low = (query_factor * (query_scaled - query_normal * inner[0][:, None])).astype(low)
    grad_key_low = (key_factor * (key_scaled - key_normal * inner[1][:, None])).astype(low)
    grad_qkv = jnp.concatenate([grad_query_low, grad_key_low, grad_value_low], axis=1)
    grad_in_part = times_transpose(grad_qkv, qkv_w)
    grad_attn_in = lax.psum_scatter(
        grad_in_part.astype(low), "expert", scatter_dimension=0, tiled=True
    ).astype(wide)
    grad_gain_attn = jnp.sum(grad_in_part * attn_normal, axis=0)
    _, own_normal, own_factor = rms_parts(tok.astype(wide), attn_gain)
    grad_attn_x, _ = rms_back(grad_attn_in, own_normal, own_factor, attn_gain)
    grad_tokens = (grad_hidden + grad_attn_x).astype(low)

    grad_w_qkv = contract_rows(attn_low, grad_qkv).reshape(2, 2, groups * shard, 3 * own_width)
    grad_w_qkv = scatter_quad(grad_w_qkv).astype(low).reshape(groups, shard, 3 * own_width)
    grad_w_qkv = lax.all_to_all(grad_w_qkv, "expert", split_axis=0, concat_axis=0)
    grad_w_qkv = grad_w_qkv.reshape(chips, 2, shard, 3, 2, HEAD_DIM).astype(wide)
    grad_w_qkv = grad_w_qkv.transpose(3, 2, 1, 4, 0, 5).reshape(3, shard, model_width)

    grad_w_out = grad_w_out.reshape(2, 2, shard, model_width)
    kept = lax.dynamic_index_in_dim(grad_w_out, core, 1, keepdims=False)
    given = lax.dynamic_index_in_dim(grad_w_out, 1 - core, 1, keepdims=False)
    grad_w_out = scatter_quad(in_order(kept.astype(low), swap_core(given.astype(low)), core))

    small = jnp.concatenate(
        [
            grad_router,
            grad_gain_attn[None],
            spread_heads(grad_gain_query)[None],
            spread_heads(grad_gain_key)[None],
            grad_gain_mlp[None],
        ],
        axis=0,
    )
    small = small.reshape(pack_rows, devices, shard).transpose(1, 0, 2).reshape(devices, -1, 128)
    small = lax.all_to_all(small, everyone, split_axis=0, concat_axis=0)
    small = jnp.sum(small, axis=0).reshape(pack_rows, shard)

    mix_part = home(part_own[1], part_near[1])
    output = (hidden + mix_part).astype(low)

    all_rows = jnp.concatenate([rows_own, rows_near], axis=0)
    all_cot = jnp.concatenate([cot_all, cot_near], axis=0)
    scaled, grad_gate_pre, grad_up_pre = (
        jnp.concatenate([part_own[i], part_near[i]], axis=1) for i in (3, 4, 5)
    )
    grad_down = jnp.einsum("etf,td->efd", scaled, all_cot, preferred_element_type=wide)
    grad_gate = jnp.einsum("td,etf->edf", all_rows, grad_gate_pre, preferred_element_type=wide)
    grad_up = jnp.einsum("td,etf->edf", all_rows, grad_up_pre, preferred_element_type=wide)
    grad_gate = grad_gate[:, :, :block_width] + swap_x(
        grad_gate[:, :, block_width:].astype(low)
    ).astype(wide)
    grad_up = grad_up[:, :, :block_width] + swap_x(grad_up[:, :, block_width:].astype(low)).astype(
        wide
    )
    grad_down = grad_down[:, :block_width] + swap_x(
        grad_down[:, block_width:].astype(low)
    ).astype(wide)
    return (
        output[None],
        grad_tokens[None],
        grad_w_qkv[0],
        grad_w_qkv[1],
        grad_w_qkv[2],
        grad_w_out,
        small[:experts].T,
        small[experts],
        small[experts + 1],
        small[experts + 2],
        small[experts + 3],
        grad_gate,
        grad_up,
        grad_down,
    )


def specs(dp):
    both = (dp, "expert") if isinstance(dp, str) else dp + ("expert",)
    rows, weight, vector = P(dp, "expert", None), P(both, None), P(both)
    columns, depth = P("expert", None, dp), P("expert", dp, None)
    taken = (rows, rows, P(dp), rows) + (weight,) * 5 + (vector,) * 4 + (columns, columns, depth)
    given = (rows, rows) + (weight,) * 5 + (vector,) * 4 + (columns, columns, depth)
    return (taken, given)


def solution(mesh):
    parts, groups = mesh.shape["dp"], mesh.shape["expert"]

    def whole(*args):
        model_width = args[0].shape[2]
        by_heads = (
            parts == 4
            and groups % 2 == 0
            and model_width == 2 * HEAD_DIM * groups
            and 2 * model_width == parts * groups * HEAD_DIM
        )
        if by_heads:
            used = jax.sharding.Mesh(
                mesh.devices.reshape(2, 2, groups), ("dy", "dx", "expert")
            )
            taken, given = specs(("dy", "dx"))
            body = per_device_by_heads
        else:
            used = mesh
            taken, given = specs("dp")
            body = per_device
        return jax.shard_map(
            body, mesh=used, in_specs=taken, out_specs=given, check_vma=False
        )(*args)

    return whole
```

```python
import functools

import jax
import jax.numpy as jnp
from jax import lax
from jax.experimental import pallas as pl
from jax.experimental.layout import Layout, with_layout_constraint
from jax.experimental.pallas import tpu as pltpu
from jax.sharding import PartitionSpec as P

HEAD_DIM = 128
TOP = 8


PRECISE = lax.Precision.HIGHEST
EPSILON = 1e-05
ROPE_BASE = 10000.0
MASKED = -1e30


def rms_parts(values, gain):
    factor = lax.rsqrt(jnp.mean(values * values, axis=-1, keepdims=True) + EPSILON)
    normal = values * factor
    return (normal * gain, normal, factor)


def rms_back(upstream, normal, factor, gain):
    scaled = upstream * gain
    inner_mean = jnp.mean(scaled * normal, axis=-1, keepdims=True)
    return (factor * (scaled - normal * inner_mean), jnp.sum(upstream * normal, axis=0))


def rope_tables(positions):
    half_dim = HEAD_DIM // 2
    frequency = ROPE_BASE ** (-2.0 * jnp.arange(half_dim).astype(jnp.float32) / HEAD_DIM)
    angles = positions.astype(jnp.float32)[:, None] * frequency[None, :]
    return (jnp.cos(angles)[:, None, :], jnp.sin(angles)[:, None, :])


def rotate(values, cosine, sine_part, direction):
    half_dim = values.shape[-1] // 2
    front_half = values[..., :half_dim]
    behind = values[..., half_dim:]
    return jnp.concatenate(
        [
            front_half * cosine - direction * behind * sine_part,
            behind * cosine + direction * front_half * sine_part,
        ],
        axis=-1,
    )


def contract_rows(left_side, right_side):
    return lax.dot_general(
        left_side, right_side, (((0,), (0,)), ((), ())), preferred_element_type=jnp.float32
    )


def times_transpose(left_side, right_side):
    return lax.dot_general(
        left_side, right_side, (((1,), (1,)), ((), ())), preferred_element_type=jnp.float32
    )


def score_grads(
    query_heads,
    key_heads,
    value_heads,
    grad_heads,
    log_total,
    row_delta,
    query_place,
    key_place,
    length,
):
    factor = HEAD_DIM ** (-0.5)
    scores = (
        jnp.einsum("qhd,khd->hqk", query_heads, key_heads, preferred_element_type=jnp.float32)
        * factor
    )
    allowed = (key_place[None, :] <= query_place[:, None]) & (key_place[None, :] < length)
    weights_full = jnp.where(allowed[None], jnp.exp(scores - log_total[:, :, None]), 0.0)
    grad_weights = jnp.einsum(
        "qhd,khd->hqk", grad_heads, value_heads, preferred_element_type=jnp.float32
    )
    grad_scores = (weights_full * (grad_weights - row_delta[:, :, None])).astype(jnp.bfloat16)
    return (weights_full.astype(jnp.bfloat16), grad_scores)


def per_device(
    tokens,
    cotangent,
    lengths,
    routes,
    w_query,
    w_key,
    w_value,
    w_output,
    router,
    gain_attn,
    gain_query,
    gain_key,
    gain_mlp,
    w_gate,
    w_up,
    w_down,
):
    tok_rows = tokens.shape[1]
    model_width = tokens.shape[2]
    head_count = model_width // HEAD_DIM
    groups = lax.axis_size("expert")
    seq_len = tok_rows * groups
    length = lengths[0]
    factor = HEAD_DIM ** (-0.5)
    gathered = (
        lax.all_gather(w_query.astype(jnp.bfloat16), ("dp", "expert"), axis=0, tiled=True),
        lax.all_gather(w_key.astype(jnp.bfloat16), ("dp", "expert"), axis=0, tiled=True),
        lax.all_gather(w_value.astype(jnp.bfloat16), ("dp", "expert"), axis=0, tiled=True),
        lax.all_gather(w_output.astype(jnp.bfloat16), ("dp", "expert"), axis=0, tiled=True),
        lax.all_gather(router.astype(jnp.bfloat16), ("dp", "expert"), axis=0, tiled=True),
        lax.all_gather(gain_attn.astype(jnp.bfloat16), ("dp", "expert"), axis=0, tiled=True),
        lax.all_gather(gain_query.astype(jnp.bfloat16), ("dp", "expert"), axis=0, tiled=True),
        lax.all_gather(gain_key.astype(jnp.bfloat16), ("dp", "expert"), axis=0, tiled=True),
        lax.all_gather(gain_mlp.astype(jnp.bfloat16), ("dp", "expert"), axis=0, tiled=True),
    )
    query_weight, key_weight, value_weight, output_weight, router_weight = (
        gathered[0],
        gathered[1],
        gathered[2],
        gathered[3],
        gathered[4],
    )
    attn_gain = gathered[5].astype(jnp.float32)
    query_gain = gathered[6].astype(jnp.float32)
    key_gain = gathered[7].astype(jnp.float32)
    mlp_gain = gathered[8].astype(jnp.float32)
    gate_weight, up_weight, down_weight = (
        lax.all_gather(w_gate.astype(jnp.bfloat16), "dp", axis=2, tiled=True),
        lax.all_gather(w_up.astype(jnp.bfloat16), "dp", axis=2, tiled=True),
        lax.all_gather(w_down.astype(jnp.bfloat16), "dp", axis=1, tiled=True),
    )
    token_rows = tokens[0].astype(jnp.float32)
    attn_in, attn_normal, attn_factor = rms_parts(token_rows, attn_gain)
    attn_low = attn_in.astype(jnp.bfloat16)
    query_pre = jnp.dot(attn_low, query_weight, preferred_element_type=jnp.float32)
    key_pre = jnp.dot(attn_low, key_weight, preferred_element_type=jnp.float32)
    value_low = jnp.dot(attn_low, value_weight, preferred_element_type=jnp.float32).astype(
        jnp.bfloat16
    )
    query_norm, query_normal, query_factor = rms_parts(query_pre, query_gain)
    key_norm, key_normal, key_factor = rms_parts(key_pre, key_gain)
    positions = lax.axis_index("expert") * tok_rows + jnp.arange(tok_rows)
    cosine, sine_part = rope_tables(positions)
    query_low = rotate(
        query_norm.reshape(tok_rows, head_count, HEAD_DIM), cosine, sine_part, 1.0
    ).astype(jnp.bfloat16)
    key_low = (
        rotate(key_norm.reshape(tok_rows, head_count, HEAD_DIM), cosine, sine_part, 1.0)
        .astype(jnp.bfloat16)
        .reshape(tok_rows, model_width)
    )
    whole_keys, whole_values = (
        lax.all_gather(key_low, "expert", axis=0, tiled=True),
        lax.all_gather(value_low, "expert", axis=0, tiled=True),
    )
    all_keys = whole_keys.reshape(seq_len, head_count, HEAD_DIM)
    all_values = whole_values.reshape(seq_len, head_count, HEAD_DIM)
    key_place = jnp.arange(seq_len)
    allowed = (key_place[None, :] <= positions[:, None]) & (key_place[None, :] < length)
    scores = (
        jnp.einsum("qhd,khd->hqk", query_low, all_keys, preferred_element_type=jnp.float32) * factor
    )
    scores = jnp.where(allowed[None], scores, MASKED)
    log_total = jax.nn.logsumexp(scores, axis=-1)
    weights_low = jnp.where(allowed[None], jnp.exp(scores - log_total[:, :, None]), 0.0).astype(
        jnp.bfloat16
    )
    attended = jnp.einsum(
        "hqk,khd->qhd", weights_low, all_values, preferred_element_type=jnp.float32
    ).reshape(tok_rows, model_width)
    attended_low = attended.astype(jnp.bfloat16)
    hidden = token_rows + jnp.dot(attended_low, output_weight, preferred_element_type=jnp.float32)
    mlp_in, mlp_normal, mlp_factor = rms_parts(hidden, mlp_gain)
    mlp_low = mlp_in.astype(jnp.bfloat16)
    logits = jnp.dot(mlp_low, router_weight, preferred_element_type=jnp.float32)
    route_ids = routes[0]
    gate_probs = jax.nn.softmax(jnp.take_along_axis(logits, route_ids, axis=1), axis=-1)
    experts = router_weight.shape[1]
    slot_cap = 2 * tok_rows * TOP // experts
    local_count = experts // groups
    pair_count = tok_rows * TOP
    flat_routes = route_ids.reshape(-1)
    expert_ids = jnp.arange(experts)
    hit_table = (flat_routes[:, None] == expert_ids[None, :]).astype(jnp.int32)
    slot_rank = jnp.sum((jnp.cumsum(hit_table, axis=0) - hit_table) * hit_table, axis=1)
    counts = jnp.sum(hit_table, axis=0)
    slot_ids = flat_routes * slot_cap + slot_rank
    slot_pair = (
        jnp.zeros((experts * slot_cap,), jnp.int32)
        .at[slot_ids]
        .set(jnp.arange(pair_count, dtype=jnp.int32))
    )
    send_rows = mlp_low[slot_pair // TOP].reshape(groups, local_count, slot_cap, model_width)
    send_counts = counts.reshape(groups, local_count).astype(jnp.bfloat16)
    arrived_rows, arrived_counts = (
        lax.all_to_all(send_rows, "expert", split_axis=0, concat_axis=0, tiled=True),
        lax.all_to_all(send_counts, "expert", split_axis=0, concat_axis=0, tiled=True),
    )
    living = (jnp.arange(slot_cap)[None, None, :] < arrived_counts.astype(jnp.int32)[:, :, None])[
        ..., None
    ]
    gate_pre = jnp.einsum(
        "nemd,edf->nemf", arrived_rows, gate_weight, preferred_element_type=jnp.float32
    )
    up_pre = jnp.einsum(
        "nemd,edf->nemf", arrived_rows, up_weight, preferred_element_type=jnp.float32
    )
    gate_sigmoid = jax.nn.sigmoid(gate_pre)
    activity = (gate_pre * gate_sigmoid * up_pre).astype(jnp.bfloat16)
    expert_out = jnp.einsum(
        "nemf,efd->nemd", activity, down_weight, preferred_element_type=jnp.float32
    ).astype(jnp.bfloat16)
    returned = lax.all_to_all(expert_out, "expert", split_axis=0, concat_axis=0, tiled=True)
    pair_out = (
        returned.reshape(experts * slot_cap, model_width)[slot_ids]
        .reshape(tok_rows, TOP, model_width)
        .astype(jnp.float32)
    )
    output = hidden + jnp.sum(gate_probs[:, :, None] * pair_out, axis=1)
    grad_out = cotangent[0].astype(jnp.float32)
    grad_gates = jnp.sum(grad_out[:, None, :] * pair_out, axis=-1)
    pair_grad = (
        (gate_probs[:, :, None] * grad_out[:, None, :])
        .astype(jnp.bfloat16)
        .reshape(pair_count, model_width)
    )
    send_grad = pair_grad[slot_pair].reshape(groups, local_count, slot_cap, model_width)
    arrived_grad = lax.all_to_all(send_grad, "expert", split_axis=0, concat_axis=0, tiled=True)
    arrived_grad = jnp.where(living, arrived_grad, jnp.zeros((), jnp.bfloat16))
    grad_activity = jnp.einsum(
        "nemd,efd->nemf", arrived_grad, down_weight, preferred_element_type=jnp.float32
    )
    grad_gate_pre = (
        grad_activity * up_pre * gate_sigmoid * (1.0 + gate_pre * (1.0 - gate_sigmoid))
    ).astype(jnp.bfloat16)
    grad_up_pre = (grad_activity * gate_pre * gate_sigmoid).astype(jnp.bfloat16)
    grad_down = jnp.einsum(
        "nemf,nemd->efd", activity, arrived_grad, preferred_element_type=jnp.float32
    )
    grad_gate = jnp.einsum(
        "nemd,nemf->edf", arrived_rows, grad_gate_pre, preferred_element_type=jnp.float32
    )
    grad_up = jnp.einsum(
        "nemd,nemf->edf", arrived_rows, grad_up_pre, preferred_element_type=jnp.float32
    )
    input_grad = (
        jnp.einsum("nemf,edf->nemd", grad_gate_pre, gate_weight, preferred_element_type=jnp.float32)
        + jnp.einsum("nemf,edf->nemd", grad_up_pre, up_weight, preferred_element_type=jnp.float32)
    ).astype(jnp.bfloat16)
    sent_back = lax.all_to_all(input_grad, "expert", split_axis=0, concat_axis=0, tiled=True)
    grad_mlp_in = jnp.sum(
        sent_back.reshape(experts * slot_cap, model_width)[slot_ids]
        .reshape(tok_rows, TOP, model_width)
        .astype(jnp.float32),
        axis=1,
    )
    grad_chosen = gate_probs * (
        grad_gates - jnp.sum(gate_probs * grad_gates, axis=-1, keepdims=True)
    )
    route_table = (route_ids[:, :, None] == expert_ids[None, None, :]).astype(jnp.float32)
    grad_logits = jnp.sum(grad_chosen[:, :, None] * route_table, axis=1)
    grad_router = jnp.einsum(
        "td,te->de", mlp_low.astype(jnp.float32), grad_logits, precision=PRECISE
    )
    grad_mlp_in = grad_mlp_in + jnp.einsum(
        "te,de->td", grad_logits, router_weight.astype(jnp.float32), precision=PRECISE
    )
    grad_hidden_norm, grad_gain_mlp = rms_back(grad_mlp_in, mlp_normal, mlp_factor, mlp_gain)
    grad_hidden = grad_out + grad_hidden_norm
    grad_attn_low = grad_hidden.astype(jnp.bfloat16)
    grad_w_out = contract_rows(attended_low, grad_attn_low)
    grad_attended = times_transpose(grad_attn_low, output_weight).astype(jnp.bfloat16)
    row_delta = jnp.sum(
        (grad_attended.astype(jnp.float32) * attended).reshape(tok_rows, head_count, HEAD_DIM),
        axis=-1,
    ).T
    grad_heads = grad_attended.reshape(tok_rows, head_count, HEAD_DIM)
    block_rows = min(512, seq_len)
    block_total = seq_len // block_rows

    def key_part(number):
        offset = number * block_rows
        block_keys = lax.dynamic_slice_in_dim(all_keys, offset, block_rows, 0)
        block_values = lax.dynamic_slice_in_dim(all_values, offset, block_rows, 0)
        weights_part, grad_scores = score_grads(
            query_low,
            block_keys,
            block_values,
            grad_heads,
            log_total,
            row_delta,
            positions,
            offset + jnp.arange(block_rows),
            length,
        )
        grad_query_part = (
            jnp.einsum("hqk,khd->qhd", grad_scores, block_keys, preferred_element_type=jnp.float32)
            * factor
        )
        grad_key_part = (
            jnp.einsum("hqk,qhd->khd", grad_scores, query_low, preferred_element_type=jnp.float32)
            * factor
        )
        grad_value_part = jnp.einsum(
            "hqk,qhd->khd", weights_part, grad_heads, preferred_element_type=jnp.float32
        )
        return (
            grad_query_part,
            grad_key_part.reshape(block_rows, model_width),
            grad_value_part.reshape(block_rows, model_width),
        )

    query_parts, key_parts, value_parts = lax.map(
        lambda number: key_part(number), jnp.arange(block_total)
    )
    grad_query = jnp.sum(query_parts, axis=0).reshape(tok_rows, model_width)
    grad_key, grad_value = (
        lax.psum_scatter(
            key_parts.reshape(seq_len, model_width).astype(jnp.bfloat16),
            "expert",
            scatter_dimension=0,
            tiled=True,
        ).astype(jnp.float32),
        lax.psum_scatter(
            value_parts.reshape(seq_len, model_width).astype(jnp.bfloat16),
            "expert",
            scatter_dimension=0,
            tiled=True,
        ).astype(jnp.float32),
    )
    grad_value_low = grad_value.astype(jnp.bfloat16)
    grad_query_rot = (
        grad_query.astype(jnp.bfloat16).astype(jnp.float32).reshape(tok_rows, head_count, HEAD_DIM)
    )
    grad_key_rot = (
        grad_key.astype(jnp.bfloat16).astype(jnp.float32).reshape(tok_rows, head_count, HEAD_DIM)
    )
    grad_query_norm = rotate(grad_query_rot, cosine, sine_part, -1.0).reshape(tok_rows, model_width)
    grad_key_norm = rotate(grad_key_rot, cosine, sine_part, -1.0).reshape(tok_rows, model_width)
    grad_query_pre, grad_gain_query = rms_back(
        grad_query_norm, query_normal, query_factor, query_gain
    )
    grad_key_pre, grad_gain_key = rms_back(grad_key_norm, key_normal, key_factor, key_gain)
    grad_query_low = grad_query_pre.astype(jnp.bfloat16)
    grad_key_low = grad_key_pre.astype(jnp.bfloat16)
    grad_wq = contract_rows(attn_low, grad_query_low)
    grad_wk = contract_rows(attn_low, grad_key_low)
    grad_wv = contract_rows(attn_low, grad_value_low)
    grad_attn_in = (
        times_transpose(grad_query_low, query_weight)
        + times_transpose(grad_key_low, key_weight)
        + times_transpose(grad_value_low, value_weight)
    )
    grad_attn_x, grad_gain_attn = rms_back(grad_attn_in, attn_normal, attn_factor, attn_gain)
    grad_tokens = (grad_hidden + grad_attn_x).astype(jnp.bfloat16)
    summed_grads = (
        lax.psum_scatter(grad_wq, ("dp", "expert"), scatter_dimension=0, tiled=True),
        lax.psum_scatter(grad_wk, ("dp", "expert"), scatter_dimension=0, tiled=True),
        lax.psum_scatter(grad_wv, ("dp", "expert"), scatter_dimension=0, tiled=True),
        lax.psum_scatter(grad_w_out, ("dp", "expert"), scatter_dimension=0, tiled=True),
        lax.psum_scatter(grad_router, ("dp", "expert"), scatter_dimension=0, tiled=True),
        lax.psum_scatter(grad_gain_attn, ("dp", "expert"), scatter_dimension=0, tiled=True),
        lax.psum_scatter(grad_gain_query, ("dp", "expert"), scatter_dimension=0, tiled=True),
        lax.psum_scatter(grad_gain_key, ("dp", "expert"), scatter_dimension=0, tiled=True),
        lax.psum_scatter(grad_gain_mlp, ("dp", "expert"), scatter_dimension=0, tiled=True),
    )
    expert_grads = (
        lax.psum_scatter(
            grad_gate.astype(jnp.bfloat16), "dp", scatter_dimension=2, tiled=True
        ).astype(jnp.float32),
        lax.psum_scatter(
            grad_up.astype(jnp.bfloat16), "dp", scatter_dimension=2, tiled=True
        ).astype(jnp.float32),
        lax.psum_scatter(
            grad_down.astype(jnp.bfloat16), "dp", scatter_dimension=1, tiled=True
        ).astype(jnp.float32),
    )
    return (
        output.astype(jnp.bfloat16)[None],
        grad_tokens[None],
        summed_grads[0],
        summed_grads[1],
        summed_grads[2],
        summed_grads[3],
        summed_grads[4],
        summed_grads[5],
        summed_grads[6],
        summed_grads[7],
        summed_grads[8],
        expert_grads[0],
        expert_grads[1],
        expert_grads[2],
    )


FLIP = [(0, 1), (1, 0)]


def in_order(own, other, index):
    first = jnp.where(index == 0, own, other)
    second = jnp.where(index == 0, other, own)
    return jnp.stack([first, second])


def swap_x(block):
    return lax.ppermute(block, "dx", FLIP)


def swap_y(block):
    return lax.ppermute(block, "dy", FLIP)


def swap_core(block):
    groups = lax.axis_size("expert")
    return lax.ppermute(block, "expert", [(i, i ^ 1) for i in range(groups)])


def row_major(value):
    return with_layout_constraint(value, Layout(major_to_minor=tuple(range(value.ndim))))


def together(*values):
    return lax.optimization_barrier(values)


def gather_first(block):
    return (block, swap_x(block), swap_y(block))


def gather_second(block, beside, below):
    half = block.shape[0] // 2
    return (block, beside, below, swap_x(below[:half]), swap_y(beside[half:]))


def gather_last(block, beside, below, upper, under):
    column, row = lax.axis_index("dx"), lax.axis_index("dy")
    across = jnp.concatenate([upper, under], axis=0)
    return in_order(in_order(block, beside, column), in_order(below, across, column), row)


def scatter_first(blocks):
    column, row = lax.axis_index("dx"), lax.axis_index("dy")
    low = jnp.bfloat16

    def pick(at_row, at_column):
        line = lax.dynamic_index_in_dim(blocks, at_row, 0, keepdims=False)
        return lax.dynamic_index_in_dim(line, at_column, 0, keepdims=False)

    half = blocks.shape[2] // 2
    across = pick(1 - row, 1 - column).astype(low)
    beside, below = pick(row, 1 - column), pick(1 - row, column)
    return (
        pick(row, column),
        beside[:half],
        below[half:],
        swap_x(beside[half:].astype(low)),
        swap_y(below[:half].astype(low)),
        swap_y(across[:half]),
        swap_x(across[half:]),
    )


def scatter_ready(kept, beside, below, from_beside, from_below, far_below, far_beside):
    low, wide = jnp.bfloat16, jnp.float32
    beside = (beside + far_below.astype(wide)).astype(low)
    below = (below + far_beside.astype(wide)).astype(low)
    return (kept, beside, below, from_beside, from_below)


def scatter_last(kept, beside, below, from_beside, from_below):
    wide = jnp.float32
    added = jnp.concatenate(
        [
            swap_x(beside).astype(wide) + from_below.astype(wide),
            from_beside.astype(wide) + swap_y(below).astype(wide),
        ]
    )
    return kept + added


def sum_experts(values):
    groups = lax.axis_size("expert")
    flat = values.reshape(-1, 128)
    spread = jnp.broadcast_to(flat[None], (groups,) + flat.shape)
    arrived = lax.all_to_all(spread, "expert", split_axis=0, concat_axis=0)
    return jnp.sum(arrived, axis=0).reshape(values.shape)


def dense_gates(logits, route_ids):
    columns = jnp.arange(logits.shape[-1])
    chosen = jnp.any(route_ids[:, :, None] == columns[None, None, :], axis=1)
    highest = jnp.max(jnp.where(chosen, logits, -jnp.inf), axis=-1, keepdims=True)
    weights = jnp.where(chosen, jnp.exp(logits - highest), 0.0)
    return weights / jnp.sum(weights, axis=-1, keepdims=True)


def mul_nn(left_side, right_side):
    return jnp.dot(left_side, right_side, preferred_element_type=jnp.float32)


VMEM_BYTES = 56 * 1024 * 1024
ROWS = 256


def whole_blocks(count):
    return [pl.BlockSpec(memory_space=pltpu.VMEM)] * count


def turn(values, cosine, signed_sine):
    return values * cosine + pltpu.roll(values, HEAD_DIM // 2, 1) * signed_sine


def allowed_block(first_row, rows, columns, length):
    at_row = first_row + lax.broadcasted_iota(jnp.int32, (rows, columns), 0)
    at_column = lax.broadcasted_iota(jnp.int32, (rows, columns), 1)
    return (at_column <= at_row) & (at_column < length)


def attend_kernel(
    length_ref,
    qkv_ref,
    query_factor_ref,
    key_factor_ref,
    query_gain_ref,
    key_gain_ref,
    cosine_ref,
    sine_ref,
    out_w_ref,
    query_ref,
    key_ref,
    value_ref,
    attended_ref,
    total_ref,
    part_ref,
):
    low = jnp.bfloat16
    seq_len, heads = qkv_ref.shape[0], 2
    length = length_ref[0]
    width = heads * HEAD_DIM
    factor = HEAD_DIM ** (-0.5)

    @pl.loop(0, seq_len // ROWS)
    def _(number):
        rows = pl.ds(pl.multiple_of(number * ROWS, ROWS), ROWS)
        cosine, sine_part = cosine_ref[rows, :], sine_ref[rows, :]
        for head in range(heads):
            part = slice(head * HEAD_DIM, (head + 1) * HEAD_DIM)
            later = slice(width + head * HEAD_DIM, width + (head + 1) * HEAD_DIM)
            query = qkv_ref[rows, part] * query_factor_ref[rows, :] * query_gain_ref[:, part]
            key = qkv_ref[rows, later] * key_factor_ref[rows, :] * key_gain_ref[:, part]
            query_ref[rows, part] = turn(query, cosine, sine_part).astype(low)
            key_ref[rows, part] = turn(key, cosine, sine_part).astype(low)
        value_ref[rows, :] = qkv_ref[rows, 2 * width :].astype(low)

    for number in range(seq_len // ROWS):
        first, end = number * ROWS, (number + 1) * ROWS
        allowed = allowed_block(first, ROWS, end, length)
        done = []
        for head in range(heads):
            part = slice(head * HEAD_DIM, (head + 1) * HEAD_DIM)
            scores = times_transpose(query_ref[first:end, part], key_ref[:end, part]) * factor
            scores = jnp.where(allowed, scores, MASKED)
            highest = jnp.max(scores, axis=1, keepdims=True)
            weights = jnp.exp(scores - highest)
            total = jnp.sum(weights, axis=1, keepdims=True)
            weights = (weights * (1.0 / total)).astype(low)
            total_ref[head, first:end, :] = highest + jnp.log(total)
            attended = mul_nn(weights, value_ref[:end, part])
            attended_ref[first:end, part] = attended
            done.append(attended.astype(low))
        part_ref[first:end, :] = mul_nn(jnp.concatenate(done, axis=1), out_w_ref[...]).astype(low)


def attend(length, qkv, query_factor, key_factor, query_gain, key_gain, cosine, sine_part, out_w):
    seq_len, width, model_width = qkv.shape[0], qkv.shape[1] // 3, out_w.shape[1]
    low, wide = jnp.bfloat16, jnp.float32
    rows = jax.ShapeDtypeStruct((seq_len, width), low)
    return pl.pallas_call(
        attend_kernel,
        in_specs=[pl.BlockSpec(memory_space=pltpu.SMEM)] + whole_blocks(8),
        out_specs=whole_blocks(6),
        out_shape=[
            rows,
            rows,
            rows,
            jax.ShapeDtypeStruct((seq_len, width), wide),
            jax.ShapeDtypeStruct((2, seq_len, 1), wide),
            jax.ShapeDtypeStruct((seq_len, model_width), low),
        ],
        compiler_params=pltpu.CompilerParams(vmem_limit_bytes=VMEM_BYTES),
        cost_estimate=pl.CostEstimate(
            flops=2 * seq_len * width * (seq_len + model_width),
            bytes_accessed=14 * seq_len * width + 2 * seq_len * model_width,
            transcendentals=seq_len * seq_len,
        ),
    )(length, qkv, query_factor, key_factor, query_gain, key_gain, cosine, sine_part, out_w)


def attend_back_kernel(
    length_ref,
    upstream_ref,
    out_w_ref,
    attended_ref,
    total_ref,
    query_ref,
    key_ref,
    value_ref,
    qkv_ref,
    query_factor_ref,
    key_factor_ref,
    query_gain_ref,
    key_gain_ref,
    cosine_ref,
    sine_ref,
    grad_value_ref,
    query_scaled_ref,
    key_scaled_ref,
    query_inner_ref,
    key_inner_ref,
    query_gain_grad_ref,
    key_gain_grad_ref,
    key_sum_ref,
    value_sum_ref,
):
    low, wide = jnp.bfloat16, jnp.float32
    seq_len, heads = qkv_ref.shape[0], 2
    length = length_ref[0]
    width = heads * HEAD_DIM
    factor = HEAD_DIM ** (-0.5)
    blocks = seq_len // ROWS

    def norm_back(sums, rows, head, offset, factor_ref, gain_ref, scaled_ref, inner_ref, grad_ref, fresh):
        part = slice(head * HEAD_DIM, (head + 1) * HEAD_DIM)
        place = slice(offset + head * HEAD_DIM, offset + (head + 1) * HEAD_DIM)
        upstream = turn(sums.astype(low).astype(wide), cosine_ref[rows, :], -sine_ref[rows, :])
        normal = qkv_ref[rows, place] * factor_ref[rows, :]
        gain_part = jnp.sum(upstream * normal, axis=0, keepdims=True)
        scaled = upstream * gain_ref[:, part]
        scaled_ref[rows, part] = scaled
        inner = jnp.sum(scaled * normal, axis=1, keepdims=True)
        if head == 0:
            inner_ref[rows, :] = inner
        else:
            inner_ref[rows, :] += inner
        if fresh:
            grad_ref[:, part] = gain_part
        else:
            grad_ref[:, part] += gain_part

    for number in reversed(range(blocks)):
        first, end = number * ROWS, (number + 1) * ROWS
        allowed = allowed_block(first, ROWS, end, length)
        rows = slice(first, end)
        grads = times_transpose(upstream_ref[rows, :], out_w_ref[...]).astype(low)
        for head in range(heads):
            part = slice(head * HEAD_DIM, (head + 1) * HEAD_DIM)
            query, keys = query_ref[rows, part], key_ref[:end, part]
            grad = grads[:, part]
            delta = jnp.sum(grad.astype(wide) * attended_ref[rows, part], axis=1, keepdims=True)
            scores = times_transpose(query, keys) * factor
            weights = jnp.where(allowed, jnp.exp(scores - total_ref[head, rows, :]), 0.0)
            grad_weights = times_transpose(grad, value_ref[:end, part])
            grad_scores = (weights * (grad_weights - delta)).astype(low)
            query_sum = mul_nn(grad_scores, keys) * factor
            key_sum = contract_rows(grad_scores, query)
            value_sum = contract_rows(weights.astype(low), grad)
            if number == blocks - 1:
                key_sum_ref[:, part] = key_sum
                value_sum_ref[:, part] = value_sum
            else:
                key_sum_ref[:end, part] += key_sum
                value_sum_ref[:end, part] += value_sum
            norm_back(
                query_sum,
                rows,
                head,
                0,
                query_factor_ref,
                query_gain_ref,
                query_scaled_ref,
                query_inner_ref,
                query_gain_grad_ref,
                number == blocks - 1,
            )
    for number in range(blocks):
        rows = slice(number * ROWS, (number + 1) * ROWS)
        grad_value_ref[rows, :] = value_sum_ref[rows, :].astype(low)
        for head in range(heads):
            part = slice(head * HEAD_DIM, (head + 1) * HEAD_DIM)
            norm_back(
                key_sum_ref[rows, part] * factor,
                rows,
                head,
                width,
                key_factor_ref,
                key_gain_ref,
                key_scaled_ref,
                key_inner_ref,
                key_gain_grad_ref,
                number == 0,
            )


def attend_back(length, upstream, out_w, attended, total, query, key, value, qkv, *rest):
    seq_len, width = attended.shape
    low, wide = jnp.bfloat16, jnp.float32
    shape = jax.ShapeDtypeStruct
    return pl.pallas_call(
        attend_back_kernel,
        in_specs=[pl.BlockSpec(memory_space=pltpu.SMEM)] + whole_blocks(14),
        out_specs=whole_blocks(7),
        out_shape=[
            shape((seq_len, width), low),
            shape((seq_len, width), wide),
            shape((seq_len, width), wide),
            shape((seq_len, 1), wide),
            shape((seq_len, 1), wide),
            shape((1, width), wide),
            shape((1, width), wide),
        ],
        scratch_shapes=[pltpu.VMEM((seq_len, width), wide), pltpu.VMEM((seq_len, width), wide)],
        compiler_params=pltpu.CompilerParams(vmem_limit_bytes=VMEM_BYTES),
        cost_estimate=pl.CostEstimate(
            flops=2 * seq_len * width * (3 * seq_len + upstream.shape[1]),
            bytes_accessed=30 * seq_len * width + 2 * upstream.size,
            transcendentals=seq_len * seq_len,
        ),
    )(length, upstream, out_w, attended, total, query, key, value, qkv, *rest)


def put_halves(outs, received, place, expert, axis, value):
    low, wide = jnp.bfloat16, jnp.float32
    length = value.shape[axis] // 2
    for half in range(2):
        span = slice(half * length, (half + 1) * length)
        at = (span, slice(None)) if axis == 0 else (slice(None), span)
        number = 2 * place + half
        if received is None:
            outs[number][...] = value[at].astype(low)
        else:
            outs[expert[0]][(expert[1],) + at] = value[at] + received[number][...].astype(wide)


def tall_kernel(count, adding, *refs):
    outs = refs[2 + (8 if adding else 4) * count :]
    received = refs[2 + 4 * count : 2 + 8 * count] if adding else None
    first, second = refs[0][...].T, refs[1][...].T
    for kind in range(2):
        for expert in range(count):
            place = count * kind + expert
            one, two = refs[2 + 2 * place], refs[3 + 2 * place]
            value = mul_nn(first, one[...]) + mul_nn(second, two[...])
            put_halves(outs, received, place, (kind, expert), 1, value)


def flat_kernel(count, adding, *refs):
    outs = refs[2 + (4 if adding else 2) * count : -1]
    received = refs[2 + 2 * count : 2 + 4 * count] if adding else None
    turned_ref = refs[-1]
    length, block = refs[2].shape

    @pl.when(pl.program_id(0) == 0)
    def _():
        for expert in range(count):
            for half in range(2):
                turned_ref[
                    expert * block : (expert + 1) * block, half * length : (half + 1) * length
                ] = refs[2 + 2 * expert + half][...].T

    for expert in range(count):
        span = slice(expert * block, (expert + 1) * block)
        value = mul_nn(turned_ref[span, :length], refs[0][...]) + mul_nn(
            turned_ref[span, length:], refs[1][...]
        )
        put_halves(outs, received, expert, (0, expert), 0, value)


def weight_grads(rows, sources, which, tall, received=None):
    length, model_width = rows[0].shape
    count, _, doubled = sources[0][0].shape
    block = doubled // 2
    tile = min(256, model_width)
    columns = pl.BlockSpec((length, tile), lambda i: (0, i))
    operands, in_specs = list(rows), [columns] * 2
    for pair in sources:
        for expert in range(count):
            operands += list(pair)
            in_specs += [
                pl.BlockSpec(
                    (None, length, block),
                    lambda i, expert=expert: (expert, 0, which),
                    pipeline_mode=pl.Buffered(1),
                )
            ] * 2
    kinds = len(sources)
    if tall:
        piece, shape = pl.BlockSpec((tile, block // 2), lambda i: (i, 0)), (model_width, block // 2)
        full = pl.BlockSpec((count, tile, block), lambda i: (0, i, 0))
        full_shape = (count, model_width, block)
    else:
        piece, shape = pl.BlockSpec((block // 2, tile), lambda i: (0, i)), (block // 2, model_width)
        full = pl.BlockSpec((count, block, tile), lambda i: (0, 0, i))
        full_shape = (count, block, model_width)
    pieces = 2 * count * kinds
    if received is None:
        out_specs, shapes, dtype = [piece] * pieces, [shape] * pieces, jnp.bfloat16
    else:
        operands += list(received)
        in_specs += [piece] * pieces
        out_specs, shapes, dtype = [full] * kinds, [full_shape] * kinds, jnp.float32
    scratch = [] if tall else [pltpu.VMEM((count * block, 2 * length), jnp.bfloat16)]
    return pl.pallas_call(
        functools.partial(tall_kernel if tall else flat_kernel, count, received is not None),
        grid=(model_width // tile,),
        in_specs=in_specs,
        out_specs=out_specs,
        out_shape=[jax.ShapeDtypeStruct(shape, dtype) for shape in shapes],
        scratch_shapes=scratch,
        compiler_params=pltpu.CompilerParams(vmem_limit_bytes=VMEM_BYTES),
        cost_estimate=pl.CostEstimate(
            flops=4 * length * model_width * count * block * kinds,
            bytes_accessed=4 * length * model_width + 6 * count * model_width * block * kinds,
            transcendentals=0,
        ),
    )(*operands)


def expert_block(gate_pre, up_pre, grad_rows, gates, gate_w, up_w, down_w):
    wide = jnp.float32
    back = jnp.einsum("td,efd->etf", grad_rows, down_w, preferred_element_type=wide)
    sigmoid = jax.nn.sigmoid(gate_pre)
    silu = gate_pre * sigmoid
    activity = silu * up_pre
    gate_grads = jnp.sum(activity * back, axis=-1)
    weight = gates.T[:, :, None]
    scaled = (activity * weight).astype(jnp.bfloat16)
    back = back * weight
    grad_gate_pre = (back * up_pre * sigmoid * (1.0 + gate_pre * (1.0 - sigmoid))).astype(
        jnp.bfloat16
    )
    grad_up_pre = (back * silu).astype(jnp.bfloat16)
    grad_in = (
        jnp.einsum("etf,edf->td", grad_gate_pre, gate_w, preferred_element_type=wide)
        + jnp.einsum("etf,edf->td", grad_up_pre, up_w, preferred_element_type=wide)
    ).astype(jnp.bfloat16)
    return (grad_in, gate_grads, scaled, grad_gate_pre, grad_up_pre)


def per_device_by_heads(
    tokens,
    cotangent,
    lengths,
    routes,
    w_query,
    w_key,
    w_value,
    w_output,
    router,
    gain_attn,
    gain_query,
    gain_key,
    gain_mlp,
    w_gate,
    w_up,
    w_down,
):
    low, wide = jnp.bfloat16, jnp.float32
    everyone = ("dy", "dx", "expert")
    tok_rows, model_width = tokens.shape[1], tokens.shape[2]
    groups = lax.axis_size("expert")
    devices = 4 * groups
    chips = groups // 2
    seq_len = tok_rows * groups
    shard = w_query.shape[0]
    experts = router.shape[1]
    local_count = experts // groups
    group = lax.axis_index("expert")
    chip, core = group // 2, group % 2
    column, row = lax.axis_index("dx"), lax.axis_index("dy")
    length = lengths[0]
    factor = HEAD_DIM ** (-0.5)
    own_width = 2 * HEAD_DIM
    tok, cot = tokens[0], cotangent[0]

    def own_heads(vector):
        blocks = vector.reshape(2, 2, chips, HEAD_DIM)
        blocks = lax.dynamic_index_in_dim(blocks, core, 0, keepdims=False)
        return lax.dynamic_index_in_dim(blocks, chip, 1, keepdims=False).reshape(own_width)

    def spread_heads(vector):
        at_core = (jnp.arange(2) == core)[:, None, None, None]
        at_chip = (jnp.arange(chips) == chip)[None, None, :, None]
        return jnp.where(
            at_core & at_chip, vector.reshape(1, 2, 1, HEAD_DIM), 0.0
        ).reshape(model_width)

    def by_heads(weight):
        blocks = weight.astype(low).reshape(shard, 2, 2, chips, HEAD_DIM)
        return blocks.transpose(3, 1, 0, 2, 4).reshape(groups, shard, own_width)

    sent = jnp.concatenate([by_heads(w_query), by_heads(w_key), by_heads(w_value)], axis=2)
    packed = jnp.concatenate(
        [router.T, gain_attn[None], gain_query[None], gain_key[None], gain_mlp[None]], axis=0
    ).astype(low)
    pack_rows = experts + 4
    packed = packed.reshape(-1, 128)
    sent, packed, out_rows, gate_own = together(
        sent, packed, w_output.astype(low), row_major(w_gate.astype(low))
    )
    arrived = lax.all_to_all(sent, "expert", split_axis=0, concat_axis=0)
    gate_far = [swap_x(gate_own[0])]
    up_own, down_own = row_major(w_up.astype(low)), row_major(w_down.astype(low))
    held = together(
        arrived, packed, gate_far[0], gate_own, up_own, down_own, cot, *gather_first(out_rows)
    )
    arrived, packed, gate_far[0], gate_own, up_own, down_own, cot = held[:7]
    out_parts = held[7:]
    packed = lax.all_to_all(
        jnp.broadcast_to(packed[None], (devices,) + packed.shape),
        everyone,
        split_axis=0,
        concat_axis=0,
    )
    qkv_parts = gather_first(arrived.reshape(groups * shard, 3 * own_width))
    held = together(packed, *qkv_parts, *gather_second(*out_parts))
    packed, qkv_parts, out_parts = held[0], held[1:4], held[4:]
    packed = (
        packed.reshape(devices, pack_rows, shard).transpose(1, 0, 2).reshape(pack_rows, model_width)
    )
    router_t = packed[:experts]
    attn_gain, query_gain, key_gain, mlp_gain = (
        packed[experts + i].astype(wide) for i in range(4)
    )
    tok_all = lax.all_gather(tok, "expert", axis=0, tiled=True)
    attn_in, attn_normal, _ = rms_parts(tok_all.astype(wide), attn_gain)
    held = together(attn_in.astype(low), *gather_second(*qkv_parts))
    attn_low, qkv_parts = held[0], held[1:]
    qkv_w = gather_last(*qkv_parts).reshape(model_width, 3 * own_width)

    cot_all = lax.all_gather(cot, "expert", axis=0, tiled=True)
    cot_half = lax.dynamic_slice_in_dim(cot_all, core * (seq_len // 2), seq_len // 2, 0)
    cot_half = swap_y(cot_half)

    qkv = jnp.dot(attn_low, qkv_w, preferred_element_type=wide)
    qkv, *out_parts = together(qkv, *out_parts)
    out_quad = gather_last(*out_parts)
    out_own = lax.dynamic_index_in_dim(out_quad, core, 0, keepdims=False)
    out_other = swap_core(lax.dynamic_index_in_dim(out_quad, 1 - core, 0, keepdims=False))
    out_w = jnp.moveaxis(in_order(out_own, out_other, core), 0, 1).reshape(own_width, model_width)
    query_pre, key_pre = qkv[:, :own_width], qkv[:, own_width : 2 * own_width]
    squares = jnp.stack([jnp.sum(query_pre * query_pre, axis=1), jnp.sum(key_pre * key_pre, axis=1)])
    squares = sum_experts(squares)
    factors = lax.rsqrt(squares / model_width + EPSILON)
    near_routes = swap_y(routes[0])
    factors, near_routes = together(factors, near_routes)
    query_factor, key_factor = factors[0][:, None], factors[1][:, None]
    query_gain_own, key_gain_own = own_heads(query_gain), own_heads(key_gain)
    cosine, sine_part = rope_tables(jnp.arange(seq_len))
    cosine = jnp.concatenate([cosine[:, 0], cosine[:, 0]], axis=1)
    sine_part = jnp.concatenate([-sine_part[:, 0], sine_part[:, 0]], axis=1)
    norm_args = (
        query_factor,
        key_factor,
        query_gain_own[None],
        key_gain_own[None],
        cosine,
        sine_part,
    )
    query_low, key_low, value_low, attended, log_total, attn_part = attend(
        lengths, qkv, *norm_args, out_w
    )
    attended_low = attended.astype(low)
    attn_part, cot_all, gate_own, up_own, down_own = together(
        attn_part, cot_all, gate_own, up_own, down_own
    )
    attn_out = lax.psum_scatter(attn_part, "expert", scatter_dimension=0, tiled=True)
    gate_far += [swap_x(gate_own[i]) for i in range(1, local_count)]
    up_far = [swap_x(up_own[0])]
    route_pair = jnp.stack([routes[0], near_routes]).reshape(-1, 128)
    route_pair = lax.all_to_all(
        jnp.broadcast_to(route_pair[None], (groups,) + route_pair.shape),
        "expert",
        split_axis=0,
        concat_axis=0,
    ).reshape(groups, 2, tok_rows, TOP)
    held = together(attn_out, cot_half, route_pair, up_far[0], up_own, down_own, *gate_far)
    attn_out, cot_half, route_pair, up_far[0], up_own, down_own = held[:6]
    gate_far = held[6:]
    up_far += [swap_x(up_own[i]) for i in range(1, local_count)]
    down_far = [swap_x(down_own[0])]
    cot_near = in_order(cot_half, swap_core(cot_half), core).reshape(seq_len, model_width)
    hidden = tok.astype(wide) + attn_out.astype(wide)
    mlp_in, mlp_normal, mlp_factor = rms_parts(hidden, mlp_gain)
    mlp_low = mlp_in.astype(low)
    gates_own = dense_gates(times_transpose(mlp_low, router_t), routes[0])

    rows_own = lax.all_gather(mlp_low, "expert", axis=0, tiled=True)
    mlp_near = swap_y(mlp_low)
    gate_w = jnp.concatenate([gate_own, jnp.stack(gate_far)], axis=2)
    cot_near, *up_far = together(cot_near, *up_far)
    up_w = jnp.concatenate([up_own, jnp.stack(up_far)], axis=2)
    held = together(rows_own, mlp_near, cot_near, gate_w, up_w, down_far[0], down_own)
    rows_own, mlp_near, cot_near, gate_w, up_w, down_far[0], down_own = held
    down_far += [swap_x(down_own[i]) for i in range(1, local_count)]
    block_width = w_gate.shape[2]
    rows_near = lax.all_gather(mlp_near, "expert", axis=0, tiled=True)

    def gates_of(rows_in, number):
        ids = route_pair[:, number].reshape(seq_len, TOP)
        gates = dense_gates(times_transpose(rows_in, router_t), ids)
        return lax.dynamic_slice_in_dim(gates, group * local_count, local_count, 1)

    def into(rows_in, weight):
        return jnp.einsum("td,edf->etf", rows_in, weight, preferred_element_type=wide)

    own_gates, own_up_pre = gates_of(rows_own, 0), into(rows_own, up_w)
    held = together(own_gates, own_up_pre, *down_far)
    own_gates, own_up_pre, down_far = held[0], held[1], held[2:]
    down_w = jnp.concatenate([down_own, jnp.stack(down_far)], axis=1)
    part_own = expert_block(
        into(rows_own, gate_w), own_up_pre, cot_all, own_gates, gate_w, up_w, down_w
    )
    rows_near, *part_own = together(rows_near, *part_own)
    part_near = expert_block(
        into(rows_near, gate_w),
        into(rows_near, up_w),
        cot_near,
        gates_of(rows_near, 1),
        gate_w,
        up_w,
        down_w,
    )

    grad_in_own = lax.psum_scatter(part_own[0], "expert", scatter_dimension=0, tiled=True)
    near_in, grad_in_own = together(part_near[0], grad_in_own)
    grad_in_near = lax.psum_scatter(near_in, "expert", scatter_dimension=0, tiled=True)

    tall_sources = [(part_own[i], part_near[i]) for i in (3, 4)]
    flat_sources = [(part_own[2], part_near[2])]
    rows_pair, cot_pair = (rows_own, rows_near), (cot_all, cot_near)
    far = list(weight_grads(rows_pair, tall_sources, 1, True))
    chunks = []
    for size in (1, 1, 1, 4, 1):
        chunks.append(far[: size * local_count // 2])
        far = far[size * local_count // 2 :]

    def send(number):
        chunks[number] = [swap_x(piece) for piece in chunks[number]]

    def tied(values, *numbers):
        held = together(*values, *[piece for i in numbers for piece in chunks[i]])
        place = len(values)
        for i in numbers:
            chunks[i] = list(held[place : place + len(chunks[i])])
            place += len(chunks[i])
        return held[: len(values)]

    cot_pair = (cot_all, tied((cot_near,), 0)[0])
    send(0)
    far = list(weight_grads(cot_pair, flat_sources, 1, False))
    for size in (2, 2):
        chunks.append(far[: size * local_count // 2])
        far = far[size * local_count // 2 :]
    (near_scaled,) = tied((part_near[2],), 0, 1, 5, 6)

    def mix(scaled):
        return jnp.einsum("etf,efd->td", scaled, down_w, preferred_element_type=wide).astype(low)

    gate_grads = jnp.stack([part_own[1], part_near[1]])
    gate_grads = gate_grads.reshape(2, local_count, groups, tok_rows).transpose(2, 0, 1, 3)
    gate_grads = lax.all_to_all(gate_grads, "expert", split_axis=0, concat_axis=0)
    own_mixed, near_mixed = mix(part_own[2]), mix(near_scaled)
    send(1)
    own_mixed, near_mixed, gate_grads = tied((own_mixed, near_mixed, gate_grads), 1)
    half_rows = seq_len // 2
    mixed_kept = lax.dynamic_slice_in_dim(near_mixed, core * half_rows, half_rows, 0)
    mixed_sent = lax.dynamic_slice_in_dim(near_mixed, (1 - core) * half_rows, half_rows, 0)
    mixed_half = (mixed_kept.astype(wide) + swap_core(mixed_sent).astype(wide)).astype(low)

    gate_grads = gate_grads.transpose(1, 3, 0, 2).reshape(2, tok_rows, experts)
    gate_grads = gate_grads[0] + swap_y(gate_grads[1])
    grad_in_near, gate_grads = tied((grad_in_near, gate_grads), 2)
    send(2)
    grad_mlp_in = grad_in_own.astype(wide) + swap_y(grad_in_near).astype(wide)
    grad_logits = gates_own * (gate_grads - jnp.sum(gates_own * gate_grads, axis=-1, keepdims=True))
    grad_router = jnp.einsum("te,td->ed", grad_logits, mlp_low.astype(wide), precision=PRECISE)
    grad_mlp_in = grad_mlp_in + jnp.einsum(
        "te,ed->td", grad_logits, router_t.astype(wide), precision=PRECISE
    )
    grad_out = cot.astype(wide)
    grad_hidden_norm, grad_gain_mlp = rms_back(grad_mlp_in, mlp_normal, mlp_factor, mlp_gain)
    grad_hidden = grad_out + grad_hidden_norm
    grad_attn_low, mixed_half = tied((grad_hidden.astype(low), mixed_half), 2, 3)
    grad_attn_all = lax.all_gather(grad_attn_low, "expert", axis=0, tiled=True)
    mixed_half = swap_y(mixed_half)
    send(3)

    grad_attn_all, mixed_half = tied((grad_attn_all, mixed_half), 3, 4)
    send(4)
    mixed = own_mixed.astype(wide)
    half_own = lax.dynamic_slice_in_dim(mixed, core * half_rows, half_rows, 0)
    mixed = lax.dynamic_update_slice_in_dim(
        own_mixed, (half_own + mixed_half.astype(wide)).astype(low), core * half_rows, 0
    )
    mixed = lax.psum_scatter(mixed, "expert", scatter_dimension=0, tiled=True)
    grad_value_low, query_scaled, key_scaled, query_inner, key_inner, *gain_grads = attend_back(
        lengths,
        grad_attn_all,
        out_w,
        attended,
        log_total,
        query_low,
        key_low,
        value_low,
        qkv,
        *norm_args,
    )
    held = tied(
        (grad_value_low, query_scaled, key_scaled, query_inner, key_inner, grad_attn_all), 4
    )
    grad_value_low, query_scaled, key_scaled, query_inner, key_inner, grad_attn_all = held
    grad_w_out = contract_rows(attended_low, grad_attn_all).reshape(2, 2, shard, model_width)
    kept = lax.dynamic_index_in_dim(grad_w_out, core, 1, keepdims=False)
    given = lax.dynamic_index_in_dim(grad_w_out, 1 - core, 1, keepdims=False)
    grad_w_out = in_order(kept.astype(low), swap_core(given.astype(low)), core)
    grad_gain_query, grad_gain_key = gain_grads[0][0], gain_grads[1][0]

    def by_parts(upstream):
        return contract_rows(attn_low, upstream).reshape(2, 2, groups * shard, -1)

    query_normal, key_normal = query_pre * query_factor, key_pre * key_factor
    inner = jnp.stack([query_inner[:, 0], key_inner[:, 0]])
    inner = sum_experts(inner)
    inner, grad_w_out = tied((inner, grad_w_out), 5)
    send(5)
    out_parts = scatter_first(grad_w_out)
    inner = inner / model_width
    grad_query_low = (query_factor * (query_scaled - query_normal * inner[0][:, None])).astype(low)
    grad_key_low = (key_factor * (key_scaled - key_normal * inner[1][:, None])).astype(low)
    grad_qkv = jnp.concatenate([grad_query_low, grad_key_low, grad_value_low], axis=1)
    grad_qkv, mixed = together(grad_qkv, mixed)
    qkv_w_grad = by_parts(grad_qkv)
    grad_qkv, qkv_w_grad = together(grad_qkv, qkv_w_grad)
    qkv_parts = scatter_first(qkv_w_grad)
    grad_in_part = times_transpose(grad_qkv, qkv_w)
    grad_in_low, *qkv_parts = tied((grad_in_part.astype(low), *qkv_parts), 5)
    grad_attn_in = lax.psum_scatter(grad_in_low, "expert", scatter_dimension=0, tiled=True)
    grad_attn_in = grad_attn_in.astype(wide)
    grad_gain_attn = jnp.sum(grad_in_part * attn_normal, axis=0)
    _, own_normal, own_factor = rms_parts(tok.astype(wide), attn_gain)
    grad_attn_x, _ = rms_back(grad_attn_in, own_normal, own_factor, attn_gain)
    grad_tokens = (grad_hidden + grad_attn_x).astype(low)

    small = jnp.concatenate(
        [
            grad_router,
            grad_gain_attn[None],
            spread_heads(grad_gain_query)[None],
            spread_heads(grad_gain_key)[None],
            grad_gain_mlp[None],
        ],
        axis=0,
    )
    small = small.reshape(pack_rows, devices, shard).transpose(1, 0, 2).reshape(devices, -1, 128)
    held = tied((*scatter_ready(*qkv_parts), *scatter_ready(*out_parts), small, *rows_pair), 4)
    qkv_parts, out_parts, small, rows_pair = held[:5], held[5:10], held[10], held[11:]
    small = lax.all_to_all(small, everyone, split_axis=0, concat_axis=0)
    small = jnp.sum(small, axis=0).reshape(pack_rows, shard)
    grad_gate, grad_up = weight_grads(
        rows_pair,
        tall_sources,
        0,
        True,
        received=[piece for chunk in chunks[:5] for piece in chunk],
    )
    grad_w_qkv = scatter_last(*qkv_parts).astype(low)
    grad_w_out = scatter_last(*out_parts)
    small, grad_w_qkv, grad_w_out, grad_gate, grad_up = tied(
        (small, grad_w_qkv, grad_w_out, grad_gate, grad_up), 6
    )
    send(6)
    grad_w_qkv = grad_w_qkv.reshape(groups, shard, 3 * own_width)
    grad_w_qkv = lax.all_to_all(grad_w_qkv, "expert", split_axis=0, concat_axis=0)
    (grad_down,) = weight_grads(
        cot_pair,
        flat_sources,
        0,
        False,
        received=[piece for chunk in chunks[5:] for piece in chunk],
    )
    grad_w_qkv, grad_down, grad_tokens = together(grad_w_qkv, grad_down, grad_tokens)
    grad_w_qkv = grad_w_qkv.reshape(chips, 2, shard, 3, 2, HEAD_DIM).astype(wide)
    grad_w_qkv = grad_w_qkv.transpose(3, 2, 1, 4, 0, 5).reshape(3, shard, model_width)

    output = (hidden + mixed.astype(wide)).astype(low)
    return (
        output[None],
        grad_tokens[None],
        grad_w_qkv[0],
        grad_w_qkv[1],
        grad_w_qkv[2],
        grad_w_out,
        small[:experts].T,
        small[experts],
        small[experts + 1],
        small[experts + 2],
        small[experts + 3],
        grad_gate,
        grad_up,
        grad_down,
    )


def specs(dp):
    both = (dp, "expert") if isinstance(dp, str) else dp + ("expert",)
    rows, weight, vector = P(dp, "expert", None), P(both, None), P(both)
    columns, depth = P("expert", None, dp), P("expert", dp, None)
    taken = (rows, rows, P(dp), rows) + (weight,) * 5 + (vector,) * 4 + (columns, columns, depth)
    given = (rows, rows) + (weight,) * 5 + (vector,) * 4 + (columns, columns, depth)
    return (taken, given)


def solution(mesh):
    parts, groups = mesh.shape["dp"], mesh.shape["expert"]

    def whole(*args):
        model_width = args[0].shape[2]
        by_heads = (
            parts == 4
            and groups % 2 == 0
            and model_width == 2 * HEAD_DIM * groups
            and 2 * model_width == parts * groups * HEAD_DIM
        )
        if by_heads:
            used = jax.sharding.Mesh(
                mesh.devices.reshape(2, 2, groups), ("dy", "dx", "expert")
            )
            taken, given = specs(("dy", "dx"))
            body = per_device_by_heads
        else:
            used = mesh
            taken, given = specs("dp")
            body = per_device
        return jax.shard_map(
            body, mesh=used, in_specs=taken, out_specs=given, check_vma=False
        )(*args)

    return whole
```

```python
import functools

import jax
import jax.numpy as jnp
from jax import lax
from jax.experimental import pallas as pl
from jax.experimental.layout import Layout, with_layout_constraint
from jax.experimental.pallas import tpu as pltpu
from jax.sharding import PartitionSpec as P

HEAD_DIM = 128
TOP = 8


PRECISE = lax.Precision.HIGHEST
EPSILON = 1e-05
ROPE_BASE = 10000.0
MASKED = -1e30


def rms_parts(values, gain):
    factor = lax.rsqrt(jnp.mean(values * values, axis=-1, keepdims=True) + EPSILON)
    normal = values * factor
    return (normal * gain, normal, factor)


def rms_back(upstream, normal, factor, gain):
    scaled = upstream * gain
    inner_mean = jnp.mean(scaled * normal, axis=-1, keepdims=True)
    return (factor * (scaled - normal * inner_mean), jnp.sum(upstream * normal, axis=0))


def rope_tables(positions):
    half_dim = HEAD_DIM // 2
    frequency = ROPE_BASE ** (-2.0 * jnp.arange(half_dim).astype(jnp.float32) / HEAD_DIM)
    angles = positions.astype(jnp.float32)[:, None] * frequency[None, :]
    return (jnp.cos(angles)[:, None, :], jnp.sin(angles)[:, None, :])


def rotate(values, cosine, sine_part, direction):
    half_dim = values.shape[-1] // 2
    front_half = values[..., :half_dim]
    behind = values[..., half_dim:]
    return jnp.concatenate(
        [
            front_half * cosine - direction * behind * sine_part,
            behind * cosine + direction * front_half * sine_part,
        ],
        axis=-1,
    )


def contract_rows(left_side, right_side):
    return lax.dot_general(
        left_side, right_side, (((0,), (0,)), ((), ())), preferred_element_type=jnp.float32
    )


def times_transpose(left_side, right_side):
    return lax.dot_general(
        left_side, right_side, (((1,), (1,)), ((), ())), preferred_element_type=jnp.float32
    )


def score_grads(
    query_heads,
    key_heads,
    value_heads,
    grad_heads,
    log_total,
    row_delta,
    query_place,
    key_place,
    length,
):
    factor = HEAD_DIM ** (-0.5)
    scores = (
        jnp.einsum("qhd,khd->hqk", query_heads, key_heads, preferred_element_type=jnp.float32)
        * factor
    )
    allowed = (key_place[None, :] <= query_place[:, None]) & (key_place[None, :] < length)
    weights_full = jnp.where(allowed[None], jnp.exp(scores - log_total[:, :, None]), 0.0)
    grad_weights = jnp.einsum(
        "qhd,khd->hqk", grad_heads, value_heads, preferred_element_type=jnp.float32
    )
    grad_scores = (weights_full * (grad_weights - row_delta[:, :, None])).astype(jnp.bfloat16)
    return (weights_full.astype(jnp.bfloat16), grad_scores)


def per_device(
    tokens,
    cotangent,
    lengths,
    routes,
    w_query,
    w_key,
    w_value,
    w_output,
    router,
    gain_attn,
    gain_query,
    gain_key,
    gain_mlp,
    w_gate,
    w_up,
    w_down,
):
    tok_rows = tokens.shape[1]
    model_width = tokens.shape[2]
    head_count = model_width // HEAD_DIM
    groups = lax.axis_size("expert")
    seq_len = tok_rows * groups
    length = lengths[0]
    factor = HEAD_DIM ** (-0.5)
    gathered = (
        lax.all_gather(w_query.astype(jnp.bfloat16), ("dp", "expert"), axis=0, tiled=True),
        lax.all_gather(w_key.astype(jnp.bfloat16), ("dp", "expert"), axis=0, tiled=True),
        lax.all_gather(w_value.astype(jnp.bfloat16), ("dp", "expert"), axis=0, tiled=True),
        lax.all_gather(w_output.astype(jnp.bfloat16), ("dp", "expert"), axis=0, tiled=True),
        lax.all_gather(router.astype(jnp.bfloat16), ("dp", "expert"), axis=0, tiled=True),
        lax.all_gather(gain_attn.astype(jnp.bfloat16), ("dp", "expert"), axis=0, tiled=True),
        lax.all_gather(gain_query.astype(jnp.bfloat16), ("dp", "expert"), axis=0, tiled=True),
        lax.all_gather(gain_key.astype(jnp.bfloat16), ("dp", "expert"), axis=0, tiled=True),
        lax.all_gather(gain_mlp.astype(jnp.bfloat16), ("dp", "expert"), axis=0, tiled=True),
    )
    query_weight, key_weight, value_weight, output_weight, router_weight = (
        gathered[0],
        gathered[1],
        gathered[2],
        gathered[3],
        gathered[4],
    )
    attn_gain = gathered[5].astype(jnp.float32)
    query_gain = gathered[6].astype(jnp.float32)
    key_gain = gathered[7].astype(jnp.float32)
    mlp_gain = gathered[8].astype(jnp.float32)
    gate_weight, up_weight, down_weight = (
        lax.all_gather(w_gate.astype(jnp.bfloat16), "dp", axis=2, tiled=True),
        lax.all_gather(w_up.astype(jnp.bfloat16), "dp", axis=2, tiled=True),
        lax.all_gather(w_down.astype(jnp.bfloat16), "dp", axis=1, tiled=True),
    )
    token_rows = tokens[0].astype(jnp.float32)
    attn_in, attn_normal, attn_factor = rms_parts(token_rows, attn_gain)
    attn_low = attn_in.astype(jnp.bfloat16)
    query_pre = jnp.dot(attn_low, query_weight, preferred_element_type=jnp.float32)
    key_pre = jnp.dot(attn_low, key_weight, preferred_element_type=jnp.float32)
    value_low = jnp.dot(attn_low, value_weight, preferred_element_type=jnp.float32).astype(
        jnp.bfloat16
    )
    query_norm, query_normal, query_factor = rms_parts(query_pre, query_gain)
    key_norm, key_normal, key_factor = rms_parts(key_pre, key_gain)
    positions = lax.axis_index("expert") * tok_rows + jnp.arange(tok_rows)
    cosine, sine_part = rope_tables(positions)
    query_low = rotate(
        query_norm.reshape(tok_rows, head_count, HEAD_DIM), cosine, sine_part, 1.0
    ).astype(jnp.bfloat16)
    key_low = (
        rotate(key_norm.reshape(tok_rows, head_count, HEAD_DIM), cosine, sine_part, 1.0)
        .astype(jnp.bfloat16)
        .reshape(tok_rows, model_width)
    )
    whole_keys, whole_values = (
        lax.all_gather(key_low, "expert", axis=0, tiled=True),
        lax.all_gather(value_low, "expert", axis=0, tiled=True),
    )
    all_keys = whole_keys.reshape(seq_len, head_count, HEAD_DIM)
    all_values = whole_values.reshape(seq_len, head_count, HEAD_DIM)
    key_place = jnp.arange(seq_len)
    allowed = (key_place[None, :] <= positions[:, None]) & (key_place[None, :] < length)
    scores = (
        jnp.einsum("qhd,khd->hqk", query_low, all_keys, preferred_element_type=jnp.float32) * factor
    )
    scores = jnp.where(allowed[None], scores, MASKED)
    log_total = jax.nn.logsumexp(scores, axis=-1)
    weights_low = jnp.where(allowed[None], jnp.exp(scores - log_total[:, :, None]), 0.0).astype(
        jnp.bfloat16
    )
    attended = jnp.einsum(
        "hqk,khd->qhd", weights_low, all_values, preferred_element_type=jnp.float32
    ).reshape(tok_rows, model_width)
    attended_low = attended.astype(jnp.bfloat16)
    hidden = token_rows + jnp.dot(attended_low, output_weight, preferred_element_type=jnp.float32)
    mlp_in, mlp_normal, mlp_factor = rms_parts(hidden, mlp_gain)
    mlp_low = mlp_in.astype(jnp.bfloat16)
    logits = jnp.dot(mlp_low, router_weight, preferred_element_type=jnp.float32)
    route_ids = routes[0]
    gate_probs = jax.nn.softmax(jnp.take_along_axis(logits, route_ids, axis=1), axis=-1)
    experts = router_weight.shape[1]
    slot_cap = 2 * tok_rows * TOP // experts
    local_count = experts // groups
    pair_count = tok_rows * TOP
    flat_routes = route_ids.reshape(-1)
    expert_ids = jnp.arange(experts)
    hit_table = (flat_routes[:, None] == expert_ids[None, :]).astype(jnp.int32)
    slot_rank = jnp.sum((jnp.cumsum(hit_table, axis=0) - hit_table) * hit_table, axis=1)
    counts = jnp.sum(hit_table, axis=0)
    slot_ids = flat_routes * slot_cap + slot_rank
    slot_pair = (
        jnp.zeros((experts * slot_cap,), jnp.int32)
        .at[slot_ids]
        .set(jnp.arange(pair_count, dtype=jnp.int32))
    )
    send_rows = mlp_low[slot_pair // TOP].reshape(groups, local_count, slot_cap, model_width)
    send_counts = counts.reshape(groups, local_count).astype(jnp.bfloat16)
    arrived_rows, arrived_counts = (
        lax.all_to_all(send_rows, "expert", split_axis=0, concat_axis=0, tiled=True),
        lax.all_to_all(send_counts, "expert", split_axis=0, concat_axis=0, tiled=True),
    )
    living = (jnp.arange(slot_cap)[None, None, :] < arrived_counts.astype(jnp.int32)[:, :, None])[
        ..., None
    ]
    gate_pre = jnp.einsum(
        "nemd,edf->nemf", arrived_rows, gate_weight, preferred_element_type=jnp.float32
    )
    up_pre = jnp.einsum(
        "nemd,edf->nemf", arrived_rows, up_weight, preferred_element_type=jnp.float32
    )
    gate_sigmoid = jax.nn.sigmoid(gate_pre)
    activity = (gate_pre * gate_sigmoid * up_pre).astype(jnp.bfloat16)
    expert_out = jnp.einsum(
        "nemf,efd->nemd", activity, down_weight, preferred_element_type=jnp.float32
    ).astype(jnp.bfloat16)
    returned = lax.all_to_all(expert_out, "expert", split_axis=0, concat_axis=0, tiled=True)
    pair_out = (
        returned.reshape(experts * slot_cap, model_width)[slot_ids]
        .reshape(tok_rows, TOP, model_width)
        .astype(jnp.float32)
    )
    output = hidden + jnp.sum(gate_probs[:, :, None] * pair_out, axis=1)
    grad_out = cotangent[0].astype(jnp.float32)
    grad_gates = jnp.sum(grad_out[:, None, :] * pair_out, axis=-1)
    pair_grad = (
        (gate_probs[:, :, None] * grad_out[:, None, :])
        .astype(jnp.bfloat16)
        .reshape(pair_count, model_width)
    )
    send_grad = pair_grad[slot_pair].reshape(groups, local_count, slot_cap, model_width)
    arrived_grad = lax.all_to_all(send_grad, "expert", split_axis=0, concat_axis=0, tiled=True)
    arrived_grad = jnp.where(living, arrived_grad, jnp.zeros((), jnp.bfloat16))
    grad_activity = jnp.einsum(
        "nemd,efd->nemf", arrived_grad, down_weight, preferred_element_type=jnp.float32
    )
    grad_gate_pre = (
        grad_activity * up_pre * gate_sigmoid * (1.0 + gate_pre * (1.0 - gate_sigmoid))
    ).astype(jnp.bfloat16)
    grad_up_pre = (grad_activity * gate_pre * gate_sigmoid).astype(jnp.bfloat16)
    grad_down = jnp.einsum(
        "nemf,nemd->efd", activity, arrived_grad, preferred_element_type=jnp.float32
    )
    grad_gate = jnp.einsum(
        "nemd,nemf->edf", arrived_rows, grad_gate_pre, preferred_element_type=jnp.float32
    )
    grad_up = jnp.einsum(
        "nemd,nemf->edf", arrived_rows, grad_up_pre, preferred_element_type=jnp.float32
    )
    input_grad = (
        jnp.einsum("nemf,edf->nemd", grad_gate_pre, gate_weight, preferred_element_type=jnp.float32)
        + jnp.einsum("nemf,edf->nemd", grad_up_pre, up_weight, preferred_element_type=jnp.float32)
    ).astype(jnp.bfloat16)
    sent_back = lax.all_to_all(input_grad, "expert", split_axis=0, concat_axis=0, tiled=True)
    grad_mlp_in = jnp.sum(
        sent_back.reshape(experts * slot_cap, model_width)[slot_ids]
        .reshape(tok_rows, TOP, model_width)
        .astype(jnp.float32),
        axis=1,
    )
    grad_chosen = gate_probs * (
        grad_gates - jnp.sum(gate_probs * grad_gates, axis=-1, keepdims=True)
    )
    route_table = (route_ids[:, :, None] == expert_ids[None, None, :]).astype(jnp.float32)
    grad_logits = jnp.sum(grad_chosen[:, :, None] * route_table, axis=1)
    grad_router = jnp.einsum(
        "td,te->de", mlp_low.astype(jnp.float32), grad_logits, precision=PRECISE
    )
    grad_mlp_in = grad_mlp_in + jnp.einsum(
        "te,de->td", grad_logits, router_weight.astype(jnp.float32), precision=PRECISE
    )
    grad_hidden_norm, grad_gain_mlp = rms_back(grad_mlp_in, mlp_normal, mlp_factor, mlp_gain)
    grad_hidden = grad_out + grad_hidden_norm
    grad_attn_low = grad_hidden.astype(jnp.bfloat16)
    grad_w_out = contract_rows(attended_low, grad_attn_low)
    grad_attended = times_transpose(grad_attn_low, output_weight).astype(jnp.bfloat16)
    row_delta = jnp.sum(
        (grad_attended.astype(jnp.float32) * attended).reshape(tok_rows, head_count, HEAD_DIM),
        axis=-1,
    ).T
    grad_heads = grad_attended.reshape(tok_rows, head_count, HEAD_DIM)
    block_rows = min(512, seq_len)
    block_total = seq_len // block_rows

    def key_part(number):
        offset = number * block_rows
        block_keys = lax.dynamic_slice_in_dim(all_keys, offset, block_rows, 0)
        block_values = lax.dynamic_slice_in_dim(all_values, offset, block_rows, 0)
        weights_part, grad_scores = score_grads(
            query_low,
            block_keys,
            block_values,
            grad_heads,
            log_total,
            row_delta,
            positions,
            offset + jnp.arange(block_rows),
            length,
        )
        grad_query_part = (
            jnp.einsum("hqk,khd->qhd", grad_scores, block_keys, preferred_element_type=jnp.float32)
            * factor
        )
        grad_key_part = (
            jnp.einsum("hqk,qhd->khd", grad_scores, query_low, preferred_element_type=jnp.float32)
            * factor
        )
        grad_value_part = jnp.einsum(
            "hqk,qhd->khd", weights_part, grad_heads, preferred_element_type=jnp.float32
        )
        return (
            grad_query_part,
            grad_key_part.reshape(block_rows, model_width),
            grad_value_part.reshape(block_rows, model_width),
        )

    query_parts, key_parts, value_parts = lax.map(
        lambda number: key_part(number), jnp.arange(block_total)
    )
    grad_query = jnp.sum(query_parts, axis=0).reshape(tok_rows, model_width)
    grad_key, grad_value = (
        lax.psum_scatter(
            key_parts.reshape(seq_len, model_width).astype(jnp.bfloat16),
            "expert",
            scatter_dimension=0,
            tiled=True,
        ).astype(jnp.float32),
        lax.psum_scatter(
            value_parts.reshape(seq_len, model_width).astype(jnp.bfloat16),
            "expert",
            scatter_dimension=0,
            tiled=True,
        ).astype(jnp.float32),
    )
    grad_value_low = grad_value.astype(jnp.bfloat16)
    grad_query_rot = (
        grad_query.astype(jnp.bfloat16).astype(jnp.float32).reshape(tok_rows, head_count, HEAD_DIM)
    )
    grad_key_rot = (
        grad_key.astype(jnp.bfloat16).astype(jnp.float32).reshape(tok_rows, head_count, HEAD_DIM)
    )
    grad_query_norm = rotate(grad_query_rot, cosine, sine_part, -1.0).reshape(tok_rows, model_width)
    grad_key_norm = rotate(grad_key_rot, cosine, sine_part, -1.0).reshape(tok_rows, model_width)
    grad_query_pre, grad_gain_query = rms_back(
        grad_query_norm, query_normal, query_factor, query_gain
    )
    grad_key_pre, grad_gain_key = rms_back(grad_key_norm, key_normal, key_factor, key_gain)
    grad_query_low = grad_query_pre.astype(jnp.bfloat16)
    grad_key_low = grad_key_pre.astype(jnp.bfloat16)
    grad_wq = contract_rows(attn_low, grad_query_low)
    grad_wk = contract_rows(attn_low, grad_key_low)
    grad_wv = contract_rows(attn_low, grad_value_low)
    grad_attn_in = (
        times_transpose(grad_query_low, query_weight)
        + times_transpose(grad_key_low, key_weight)
        + times_transpose(grad_value_low, value_weight)
    )
    grad_attn_x, grad_gain_attn = rms_back(grad_attn_in, attn_normal, attn_factor, attn_gain)
    grad_tokens = (grad_hidden + grad_attn_x).astype(jnp.bfloat16)
    summed_grads = (
        lax.psum_scatter(grad_wq, ("dp", "expert"), scatter_dimension=0, tiled=True),
        lax.psum_scatter(grad_wk, ("dp", "expert"), scatter_dimension=0, tiled=True),
        lax.psum_scatter(grad_wv, ("dp", "expert"), scatter_dimension=0, tiled=True),
        lax.psum_scatter(grad_w_out, ("dp", "expert"), scatter_dimension=0, tiled=True),
        lax.psum_scatter(grad_router, ("dp", "expert"), scatter_dimension=0, tiled=True),
        lax.psum_scatter(grad_gain_attn, ("dp", "expert"), scatter_dimension=0, tiled=True),
        lax.psum_scatter(grad_gain_query, ("dp", "expert"), scatter_dimension=0, tiled=True),
        lax.psum_scatter(grad_gain_key, ("dp", "expert"), scatter_dimension=0, tiled=True),
        lax.psum_scatter(grad_gain_mlp, ("dp", "expert"), scatter_dimension=0, tiled=True),
    )
    expert_grads = (
        lax.psum_scatter(
            grad_gate.astype(jnp.bfloat16), "dp", scatter_dimension=2, tiled=True
        ).astype(jnp.float32),
        lax.psum_scatter(
            grad_up.astype(jnp.bfloat16), "dp", scatter_dimension=2, tiled=True
        ).astype(jnp.float32),
        lax.psum_scatter(
            grad_down.astype(jnp.bfloat16), "dp", scatter_dimension=1, tiled=True
        ).astype(jnp.float32),
    )
    return (
        output.astype(jnp.bfloat16)[None],
        grad_tokens[None],
        summed_grads[0],
        summed_grads[1],
        summed_grads[2],
        summed_grads[3],
        summed_grads[4],
        summed_grads[5],
        summed_grads[6],
        summed_grads[7],
        summed_grads[8],
        expert_grads[0],
        expert_grads[1],
        expert_grads[2],
    )


FLIP = [(0, 1), (1, 0)]


def in_order(own, other, index):
    first = jnp.where(index == 0, own, other)
    second = jnp.where(index == 0, other, own)
    return jnp.stack([first, second])


def swap_x(block):
    return lax.ppermute(block, "dx", FLIP)


def swap_y(block):
    return lax.ppermute(block, "dy", FLIP)


def swap_core(block):
    groups = lax.axis_size("expert")
    return lax.ppermute(block, "expert", [(i, i ^ 1) for i in range(groups)])


def row_major(value):
    return with_layout_constraint(value, Layout(major_to_minor=tuple(range(value.ndim))))


def together(*values):
    return lax.optimization_barrier(values)


def gather_first(block):
    return (block, swap_x(block), swap_y(block))


def gather_second(block, beside, below):
    half = block.shape[0] // 2
    return (block, beside, below, swap_x(below[:half]), swap_y(beside[half:]))


def gather_last(block, beside, below, upper, under):
    column, row = lax.axis_index("dx"), lax.axis_index("dy")
    across = jnp.concatenate([upper, under], axis=0)
    return in_order(in_order(block, beside, column), in_order(below, across, column), row)


def scatter_first(blocks):
    column, row = lax.axis_index("dx"), lax.axis_index("dy")
    low = jnp.bfloat16

    def pick(at_row, at_column):
        line = lax.dynamic_index_in_dim(blocks, at_row, 0, keepdims=False)
        return lax.dynamic_index_in_dim(line, at_column, 0, keepdims=False)

    half = blocks.shape[2] // 2
    across = pick(1 - row, 1 - column).astype(low)
    beside, below = pick(row, 1 - column), pick(1 - row, column)
    return (
        pick(row, column),
        beside[:half],
        below[half:],
        beside[half:].astype(low),
        below[:half].astype(low),
        swap_y(across[:half]),
        swap_x(across[half:]),
    )


def scatter_ready(kept, beside, below, beside_rest, below_rest, far_below, far_beside):
    low, wide = jnp.bfloat16, jnp.float32
    beside = (beside + far_below.astype(wide)).astype(low)
    below = (below + far_beside.astype(wide)).astype(low)
    return (kept, beside, below, beside_rest, below_rest)


def scatter_last(kept, beside, below, beside_rest, below_rest):
    wide = jnp.float32
    added = jnp.concatenate(
        [
            swap_x(beside).astype(wide) + swap_y(below_rest).astype(wide),
            swap_x(beside_rest).astype(wide) + swap_y(below).astype(wide),
        ]
    )
    return kept + added


def sum_experts(values):
    groups = lax.axis_size("expert")
    flat = values.reshape(-1, 128)
    spread = jnp.broadcast_to(flat[None], (groups,) + flat.shape)
    arrived = lax.all_to_all(spread, "expert", split_axis=0, concat_axis=0)
    return jnp.sum(arrived, axis=0).reshape(values.shape)


def dense_gates(logits, route_ids):
    columns = jnp.arange(logits.shape[-1])
    chosen = jnp.any(route_ids[:, :, None] == columns[None, None, :], axis=1)
    highest = jnp.max(jnp.where(chosen, logits, -jnp.inf), axis=-1, keepdims=True)
    weights = jnp.where(chosen, jnp.exp(logits - highest), 0.0)
    return weights / jnp.sum(weights, axis=-1, keepdims=True)


def mul_nn(left_side, right_side):
    return jnp.dot(left_side, right_side, preferred_element_type=jnp.float32)


VMEM_BYTES = 56 * 1024 * 1024
ROWS = 256


def whole_blocks(count):
    return [pl.BlockSpec(memory_space=pltpu.VMEM)] * count


def turn(values, cosine, signed_sine):
    return values * cosine + pltpu.roll(values, HEAD_DIM // 2, 1) * signed_sine


def allowed_block(first_row, rows, columns, length):
    at_row = first_row + lax.broadcasted_iota(jnp.int32, (rows, columns), 0)
    at_column = lax.broadcasted_iota(jnp.int32, (rows, columns), 1)
    return (at_column <= at_row) & (at_column < length)


def attend_kernel(
    length_ref,
    qkv_ref,
    query_factor_ref,
    key_factor_ref,
    query_gain_ref,
    key_gain_ref,
    cosine_ref,
    sine_ref,
    out_w_ref,
    query_ref,
    key_ref,
    value_ref,
    attended_ref,
    total_ref,
    part_ref,
):
    low = jnp.bfloat16
    seq_len, heads = qkv_ref.shape[0], 2
    length = length_ref[0]
    width = heads * HEAD_DIM
    factor = HEAD_DIM ** (-0.5)

    @pl.loop(0, seq_len // ROWS)
    def _(number):
        rows = pl.ds(pl.multiple_of(number * ROWS, ROWS), ROWS)
        cosine, sine_part = cosine_ref[rows, :], sine_ref[rows, :]
        for head in range(heads):
            part = slice(head * HEAD_DIM, (head + 1) * HEAD_DIM)
            later = slice(width + head * HEAD_DIM, width + (head + 1) * HEAD_DIM)
            query = qkv_ref[rows, part] * query_factor_ref[rows, :] * query_gain_ref[:, part]
            key = qkv_ref[rows, later] * key_factor_ref[rows, :] * key_gain_ref[:, part]
            query_ref[rows, part] = turn(query, cosine, sine_part).astype(low)
            key_ref[rows, part] = turn(key, cosine, sine_part).astype(low)
        value_ref[rows, :] = qkv_ref[rows, 2 * width :].astype(low)

    for number in range(seq_len // ROWS):
        first, end = number * ROWS, (number + 1) * ROWS
        allowed = allowed_block(first, ROWS, end, length)
        done = []
        for head in range(heads):
            part = slice(head * HEAD_DIM, (head + 1) * HEAD_DIM)
            scores = times_transpose(query_ref[first:end, part], key_ref[:end, part]) * factor
            scores = jnp.where(allowed, scores, MASKED)
            highest = jnp.max(scores, axis=1, keepdims=True)
            weights = jnp.exp(scores - highest)
            total = jnp.sum(weights, axis=1, keepdims=True)
            weights = (weights * (1.0 / total)).astype(low)
            total_ref[head, first:end, :] = highest + jnp.log(total)
            attended = mul_nn(weights, value_ref[:end, part])
            attended_ref[first:end, part] = attended
            done.append(attended.astype(low))
        part_ref[first:end, :] = mul_nn(jnp.concatenate(done, axis=1), out_w_ref[...]).astype(low)


def attend(length, qkv, query_factor, key_factor, query_gain, key_gain, cosine, sine_part, out_w):
    seq_len, width, model_width = qkv.shape[0], qkv.shape[1] // 3, out_w.shape[1]
    low, wide = jnp.bfloat16, jnp.float32
    rows = jax.ShapeDtypeStruct((seq_len, width), low)
    return pl.pallas_call(
        attend_kernel,
        in_specs=[pl.BlockSpec(memory_space=pltpu.SMEM)] + whole_blocks(8),
        out_specs=whole_blocks(6),
        out_shape=[
            rows,
            rows,
            rows,
            jax.ShapeDtypeStruct((seq_len, width), wide),
            jax.ShapeDtypeStruct((2, seq_len, 1), wide),
            jax.ShapeDtypeStruct((seq_len, model_width), low),
        ],
        compiler_params=pltpu.CompilerParams(vmem_limit_bytes=VMEM_BYTES),
        cost_estimate=pl.CostEstimate(
            flops=2 * seq_len * width * (seq_len + model_width),
            bytes_accessed=14 * seq_len * width + 2 * seq_len * model_width,
            transcendentals=seq_len * seq_len,
        ),
    )(length, qkv, query_factor, key_factor, query_gain, key_gain, cosine, sine_part, out_w)


def attend_back_kernel(
    length_ref,
    upstream_ref,
    out_w_ref,
    attended_ref,
    total_ref,
    query_ref,
    key_ref,
    value_ref,
    qkv_ref,
    query_factor_ref,
    key_factor_ref,
    query_gain_ref,
    key_gain_ref,
    cosine_ref,
    sine_ref,
    grad_value_ref,
    query_scaled_ref,
    key_scaled_ref,
    query_inner_ref,
    key_inner_ref,
    query_gain_grad_ref,
    key_gain_grad_ref,
    key_sum_ref,
    value_sum_ref,
):
    low, wide = jnp.bfloat16, jnp.float32
    seq_len, heads = qkv_ref.shape[0], 2
    length = length_ref[0]
    width = heads * HEAD_DIM
    factor = HEAD_DIM ** (-0.5)
    blocks = seq_len // ROWS

    def norm_back(sums, rows, head, offset, factor_ref, gain_ref, scaled_ref, inner_ref, grad_ref, fresh):
        part = slice(head * HEAD_DIM, (head + 1) * HEAD_DIM)
        place = slice(offset + head * HEAD_DIM, offset + (head + 1) * HEAD_DIM)
        upstream = turn(sums.astype(low).astype(wide), cosine_ref[rows, :], -sine_ref[rows, :])
        normal = qkv_ref[rows, place] * factor_ref[rows, :]
        gain_part = jnp.sum(upstream * normal, axis=0, keepdims=True)
        scaled = upstream * gain_ref[:, part]
        scaled_ref[rows, part] = scaled
        inner = jnp.sum(scaled * normal, axis=1, keepdims=True)
        if head == 0:
            inner_ref[rows, :] = inner
        else:
            inner_ref[rows, :] += inner
        if fresh:
            grad_ref[:, part] = gain_part
        else:
            grad_ref[:, part] += gain_part

    for number in reversed(range(blocks)):
        first, end = number * ROWS, (number + 1) * ROWS
        allowed = allowed_block(first, ROWS, end, length)
        rows = slice(first, end)
        grads = times_transpose(upstream_ref[rows, :], out_w_ref[...]).astype(low)
        for head in range(heads):
            part = slice(head * HEAD_DIM, (head + 1) * HEAD_DIM)
            query, keys = query_ref[rows, part], key_ref[:end, part]
            grad = grads[:, part]
            delta = jnp.sum(grad.astype(wide) * attended_ref[rows, part], axis=1, keepdims=True)
            scores = times_transpose(query, keys) * factor
            weights = jnp.where(allowed, jnp.exp(scores - total_ref[head, rows, :]), 0.0)
            grad_weights = times_transpose(grad, value_ref[:end, part])
            grad_scores = (weights * (grad_weights - delta)).astype(low)
            query_sum = mul_nn(grad_scores, keys) * factor
            key_sum = contract_rows(grad_scores, query)
            value_sum = contract_rows(weights.astype(low), grad)
            if number == blocks - 1:
                key_sum_ref[:, part] = key_sum
                value_sum_ref[:, part] = value_sum
            else:
                key_sum_ref[:end, part] += key_sum
                value_sum_ref[:end, part] += value_sum
            norm_back(
                query_sum,
                rows,
                head,
                0,
                query_factor_ref,
                query_gain_ref,
                query_scaled_ref,
                query_inner_ref,
                query_gain_grad_ref,
                number == blocks - 1,
            )
    for number in range(blocks):
        rows = slice(number * ROWS, (number + 1) * ROWS)
        grad_value_ref[rows, :] = value_sum_ref[rows, :].astype(low)
        for head in range(heads):
            part = slice(head * HEAD_DIM, (head + 1) * HEAD_DIM)
            norm_back(
                key_sum_ref[rows, part] * factor,
                rows,
                head,
                width,
                key_factor_ref,
                key_gain_ref,
                key_scaled_ref,
                key_inner_ref,
                key_gain_grad_ref,
                number == 0,
            )


def attend_back(length, upstream, out_w, attended, total, query, key, value, qkv, *rest):
    seq_len, width = attended.shape
    low, wide = jnp.bfloat16, jnp.float32
    shape = jax.ShapeDtypeStruct
    return pl.pallas_call(
        attend_back_kernel,
        in_specs=[pl.BlockSpec(memory_space=pltpu.SMEM)] + whole_blocks(14),
        out_specs=whole_blocks(7),
        out_shape=[
            shape((seq_len, width), low),
            shape((seq_len, width), wide),
            shape((seq_len, width), wide),
            shape((seq_len, 1), wide),
            shape((seq_len, 1), wide),
            shape((1, width), wide),
            shape((1, width), wide),
        ],
        scratch_shapes=[pltpu.VMEM((seq_len, width), wide), pltpu.VMEM((seq_len, width), wide)],
        compiler_params=pltpu.CompilerParams(vmem_limit_bytes=VMEM_BYTES),
        cost_estimate=pl.CostEstimate(
            flops=2 * seq_len * width * (3 * seq_len + upstream.shape[1]),
            bytes_accessed=30 * seq_len * width + 2 * upstream.size,
            transcendentals=seq_len * seq_len,
        ),
    )(length, upstream, out_w, attended, total, query, key, value, qkv, *rest)


def put_halves(outs, place, expert, axis, value):
    if len(outs[0].shape) == 3:
        outs[expert[0]][expert[1]] = value
        return
    length = value.shape[axis] // 2
    for half in range(2):
        span = slice(half * length, (half + 1) * length)
        at = (span, slice(None)) if axis == 0 else (slice(None), span)
        outs[2 * place + half][...] = value[at].astype(jnp.bfloat16)


def tall_kernel(count, *refs):
    outs = refs[2 + 4 * count :]
    first, second = refs[0][...].T, refs[1][...].T
    for kind in range(2):
        for expert in range(count):
            place = count * kind + expert
            one, two = refs[2 + 2 * place], refs[3 + 2 * place]
            value = mul_nn(first, one[...]) + mul_nn(second, two[...])
            put_halves(outs, place, (kind, expert), 1, value)


def flat_kernel(count, *refs):
    outs = refs[2 + 2 * count : -1]
    turned_ref = refs[-1]
    length, block = refs[2].shape

    @pl.when(pl.program_id(0) == 0)
    def _():
        for expert in range(count):
            for half in range(2):
                turned_ref[
                    expert * block : (expert + 1) * block, half * length : (half + 1) * length
                ] = refs[2 + 2 * expert + half][...].T

    for expert in range(count):
        span = slice(expert * block, (expert + 1) * block)
        value = mul_nn(turned_ref[span, :length], refs[0][...]) + mul_nn(
            turned_ref[span, length:], refs[1][...]
        )
        put_halves(outs, expert, (0, expert), 0, value)


def weight_grads(rows, sources, which, tall):
    length, model_width = rows[0].shape
    count, _, doubled = sources[0][0].shape
    block = doubled // 2
    tile = min(256, model_width)
    columns = pl.BlockSpec((length, tile), lambda i: (0, i))
    operands, in_specs = list(rows), [columns] * 2
    for pair in sources:
        for expert in range(count):
            operands += list(pair)
            in_specs += [
                pl.BlockSpec(
                    (None, length, block),
                    lambda i, expert=expert: (expert, 0, which),
                    pipeline_mode=pl.Buffered(1),
                )
            ] * 2
    kinds = len(sources)
    if which == 0:
        number, dtype = kinds, jnp.float32
        if tall:
            spec, shape = pl.BlockSpec((count, tile, block), lambda i: (0, i, 0)), (model_width, block)
        else:
            spec, shape = pl.BlockSpec((count, block, tile), lambda i: (0, 0, i)), (block, model_width)
        shape = (count,) + shape
    else:
        number, dtype = 2 * count * kinds, jnp.bfloat16
        if tall:
            spec, shape = pl.BlockSpec((tile, block // 2), lambda i: (i, 0)), (model_width, block // 2)
        else:
            spec, shape = pl.BlockSpec((block // 2, tile), lambda i: (0, i)), (block // 2, model_width)
    scratch = [] if tall else [pltpu.VMEM((count * block, 2 * length), jnp.bfloat16)]
    return pl.pallas_call(
        functools.partial(tall_kernel if tall else flat_kernel, count),
        grid=(model_width // tile,),
        in_specs=in_specs,
        out_specs=[spec] * number,
        out_shape=[jax.ShapeDtypeStruct(shape, dtype)] * number,
        scratch_shapes=scratch,
        compiler_params=pltpu.CompilerParams(vmem_limit_bytes=VMEM_BYTES),
        cost_estimate=pl.CostEstimate(
            flops=4 * length * model_width * count * block * kinds,
            bytes_accessed=4 * length * model_width + 6 * count * model_width * block * kinds,
            transcendentals=0,
        ),
    )(*operands)


def add_kernel(axis, own_ref, *refs):
    out_ref = refs[-1]
    for expert in range(out_ref.shape[0]):
        pair = [ref[...].astype(jnp.float32) for ref in refs[2 * expert : 2 * expert + 2]]
        out_ref[expert] = own_ref[expert] + jnp.concatenate(pair, axis=axis)


def add_pieces(own, pieces, axis):
    count, rows, columns = own.shape
    tile = min(512, rows if axis else columns)
    if axis:
        full = pl.BlockSpec((count, tile, columns), lambda i: (0, i, 0))
        piece = pl.BlockSpec((tile, columns // 2), lambda i: (i, 0))
    else:
        full = pl.BlockSpec((count, rows, tile), lambda i: (0, 0, i))
        piece = pl.BlockSpec((rows // 2, tile), lambda i: (0, i))
    return pl.pallas_call(
        functools.partial(add_kernel, axis),
        grid=((rows if axis else columns) // tile,),
        in_specs=[full] + [piece] * len(pieces),
        out_specs=full,
        out_shape=jax.ShapeDtypeStruct(own.shape, own.dtype),
        input_output_aliases={0: 0},
        compiler_params=pltpu.CompilerParams(vmem_limit_bytes=VMEM_BYTES),
        cost_estimate=pl.CostEstimate(
            flops=own.size, bytes_accessed=10 * own.size, transcendentals=0
        ),
    )(own, *pieces)


def expert_block(gate_pre, up_pre, grad_rows, gates, gate_w, up_w, down_w):
    wide = jnp.float32
    back = jnp.einsum("td,efd->etf", grad_rows, down_w, preferred_element_type=wide)
    sigmoid = jax.nn.sigmoid(gate_pre)
    silu = gate_pre * sigmoid
    activity = silu * up_pre
    gate_grads = jnp.sum(activity * back, axis=-1)
    weight = gates
    scaled = (activity * weight).astype(jnp.bfloat16)
    back = back * weight
    grad_gate_pre = (back * up_pre * sigmoid * (1.0 + gate_pre * (1.0 - sigmoid))).astype(
        jnp.bfloat16
    )
    grad_up_pre = (back * silu).astype(jnp.bfloat16)
    grad_in = (
        jnp.einsum("etf,edf->td", grad_gate_pre, gate_w, preferred_element_type=wide)
        + jnp.einsum("etf,edf->td", grad_up_pre, up_w, preferred_element_type=wide)
    ).astype(jnp.bfloat16)
    return (grad_in, gate_grads, scaled, grad_gate_pre, grad_up_pre)


def per_device_by_heads(
    tokens,
    cotangent,
    lengths,
    routes,
    w_query,
    w_key,
    w_value,
    w_output,
    router,
    gain_attn,
    gain_query,
    gain_key,
    gain_mlp,
    w_gate,
    w_up,
    w_down,
):
    low, wide = jnp.bfloat16, jnp.float32
    everyone = ("dy", "dx", "expert")
    tok_rows, model_width = tokens.shape[1], tokens.shape[2]
    groups = lax.axis_size("expert")
    devices = 4 * groups
    chips = groups // 2
    seq_len = tok_rows * groups
    shard = w_query.shape[0]
    experts = router.shape[1]
    local_count = experts // groups
    group = lax.axis_index("expert")
    chip, core = group // 2, group % 2
    column, row = lax.axis_index("dx"), lax.axis_index("dy")
    length = lengths[0]
    factor = HEAD_DIM ** (-0.5)
    own_width = 2 * HEAD_DIM
    tok, cot = tokens[0], cotangent[0]

    def own_heads(vector):
        blocks = vector.reshape(2, 2, chips, HEAD_DIM)
        blocks = lax.dynamic_index_in_dim(blocks, core, 0, keepdims=False)
        return lax.dynamic_index_in_dim(blocks, chip, 1, keepdims=False).reshape(own_width)

    def spread_heads(vector):
        at_core = (jnp.arange(2) == core)[:, None, None, None]
        at_chip = (jnp.arange(chips) == chip)[None, None, :, None]
        return jnp.where(
            at_core & at_chip, vector.reshape(1, 2, 1, HEAD_DIM), 0.0
        ).reshape(model_width)

    def by_heads(weight):
        blocks = weight.astype(low).reshape(shard, 2, 2, chips, HEAD_DIM)
        return blocks.transpose(3, 1, 0, 2, 4).reshape(groups, shard, own_width)

    sent = jnp.concatenate([by_heads(w_query), by_heads(w_key), by_heads(w_value)], axis=2)
    packed = jnp.concatenate(
        [router.T, gain_attn[None], gain_query[None], gain_key[None], gain_mlp[None]], axis=0
    ).astype(low)
    pack_rows = experts + 4
    packed = packed.reshape(-1, 128)
    numbers = range(local_count)

    def experts_low(weight):
        pieces = [weight[0]]
        for i in numbers[1:]:
            pieces += jnp.split(weight[i], 2)
        return [row_major(piece.astype(low)) for piece in pieces]

    def joined(pieces):
        return [pieces[0]] + [
            jnp.concatenate(pieces[i : i + 2]) for i in range(1, len(pieces), 2)
        ]

    many = 2 * local_count - 1

    cosine, sine_part = rope_tables(jnp.arange(seq_len))
    cosine = jnp.concatenate([cosine[:, 0], cosine[:, 0]], axis=1)
    sine_part = jnp.concatenate([-sine_part[:, 0], sine_part[:, 0]], axis=1)
    sent, packed, out_rows, *gate_own = together(
        sent, packed, w_output.astype(low), *experts_low(w_gate)
    )
    up_own, down_own = experts_low(w_up), experts_low(w_down)
    out_rows, up_own[0], *gate_own = together(out_rows, up_own[0], *gate_own)
    arrived = lax.all_to_all(sent, "expert", split_axis=0, concat_axis=0)
    gate_far = [swap_x(piece) for piece in gate_own[:-1]]
    held = together(
        arrived,
        packed,
        cot,
        cosine,
        sine_part,
        *gather_first(out_rows),
        *gate_far,
        gate_own[-1],
        *up_own,
        *down_own,
    )
    arrived, packed, cot, cosine, sine_part = held[:5]
    out_parts, held = held[5:8], held[8:]
    gate_far, gate_last, held = list(held[: many - 1]), held[many - 1], held[many:]
    up_own, down_own = held[:many], held[many:]
    packed = lax.all_to_all(
        jnp.broadcast_to(packed[None], (devices,) + packed.shape),
        everyone,
        split_axis=0,
        concat_axis=0,
    )
    qkv_parts = gather_first(arrived.reshape(groups * shard, 3 * own_width))
    held = together(packed, *qkv_parts, *gather_second(*out_parts))
    packed, qkv_parts, out_parts = held[0], held[1:4], held[4:]
    packed = (
        packed.reshape(devices, pack_rows, shard).transpose(1, 0, 2).reshape(pack_rows, model_width)
    )
    router_t = packed[:experts]
    attn_gain, query_gain, key_gain, mlp_gain = (
        packed[experts + i].astype(wide) for i in range(4)
    )
    tok_all = lax.all_gather(tok, "expert", axis=0, tiled=True)
    attn_in, attn_normal, _ = rms_parts(tok_all.astype(wide), attn_gain)
    held = together(attn_in.astype(low), *gather_second(*qkv_parts))
    attn_low, qkv_parts = held[0], held[1:]
    qkv_w = gather_last(*qkv_parts).reshape(model_width, 3 * own_width)

    cot_all = lax.all_gather(cot, "expert", axis=0, tiled=True)
    cot_half = lax.dynamic_slice_in_dim(cot_all, core * (seq_len // 2), seq_len // 2, 0)
    cot_half = swap_y(cot_half)

    qkv = jnp.dot(attn_low, qkv_w, preferred_element_type=wide)
    qkv, *out_parts = together(qkv, *out_parts)
    out_quad = gather_last(*out_parts)
    out_first = lax.dynamic_index_in_dim(out_quad, core, 0, keepdims=False)
    out_other = swap_core(lax.dynamic_index_in_dim(out_quad, 1 - core, 0, keepdims=False))
    out_w = jnp.moveaxis(in_order(out_first, out_other, core), 0, 1)
    out_w = out_w.reshape(own_width, model_width)
    query_pre, key_pre = qkv[:, :own_width], qkv[:, own_width : 2 * own_width]
    squares = jnp.stack([jnp.sum(query_pre * query_pre, axis=1), jnp.sum(key_pre * key_pre, axis=1)])
    squares = sum_experts(squares)
    factors = lax.rsqrt(squares / model_width + EPSILON)
    query_factor, key_factor = factors[0][:, None], factors[1][:, None]
    query_gain_own, key_gain_own = own_heads(query_gain), own_heads(key_gain)
    norm_args = (
        query_factor,
        key_factor,
        query_gain_own[None],
        key_gain_own[None],
        cosine,
        sine_part,
    )
    query_low, key_low, value_low, attended, log_total, attn_part = attend(
        lengths, qkv, *norm_args, out_w
    )
    attended_low = attended.astype(low)
    held = together(attn_part, cot_all, gate_last, *up_own, *down_own)
    attn_part, cot_all, gate_last, held = held[0], held[1], held[2], held[3:]
    up_own, down_own = held[:many], held[many:]
    attn_out = lax.psum_scatter(attn_part, "expert", scatter_dimension=0, tiled=True)
    gate_far.append(swap_x(gate_last))
    up_far = [swap_x(piece) for piece in up_own[:-1]]
    held = together(attn_out, cot_half, *gate_far, *up_far, up_own[-1], *down_own)
    attn_out, cot_half, held = held[0], held[1], held[2:]
    gate_far, held = list(held[:many]), held[many:]
    up_far, down_own = list(held[: many - 1]), held[many:]
    up_own = [*up_own[:-1], held[many - 1]]
    up_far.append(swap_x(up_own[-1]))
    down_far = [swap_x(piece) for piece in down_own[:-1]]
    cot_near = in_order(cot_half, swap_core(cot_half), core).reshape(seq_len, model_width)
    hidden = tok.astype(wide) + attn_out.astype(wide)
    mlp_in, mlp_normal, mlp_factor = rms_parts(hidden, mlp_gain)
    mlp_low = mlp_in.astype(low)
    gates_own = dense_gates(times_transpose(mlp_low, router_t), routes[0])

    rows_own = lax.all_gather(mlp_low, "expert", axis=0, tiled=True)
    mlp_near = swap_y(mlp_low)

    def doubled(own, far, axis):
        return jnp.stack(
            [jnp.concatenate(pair, axis=axis) for pair in zip(joined(own), joined(far))]
        )

    gates_sent = jnp.stack([gates_own, swap_y(gates_own)])
    gates_sent = gates_sent.reshape(2, tok_rows, groups, local_count).transpose(2, 0, 3, 1)
    gates_sent = lax.all_to_all(gates_sent, "expert", split_axis=0, concat_axis=0)
    gate_w = doubled(gate_own, gate_far, 1)
    cot_near, *up_far = together(cot_near, *up_far)
    up_w = doubled(up_own, up_far, 1)
    held = together(
        rows_own, mlp_near, cot_near, gate_w, up_w, gates_sent, *down_far, down_own[-1]
    )
    rows_own, mlp_near, cot_near, gate_w, up_w, gates_sent = held[:6]
    down_far, down_own = list(held[6:-1]), [*down_own[:-1], held[-1]]
    gates_all = gates_sent.transpose(1, 2, 0, 3).reshape(2, local_count, seq_len, 1)
    down_far.append(swap_x(down_own[-1]))
    rows_near = lax.all_gather(mlp_near, "expert", axis=0, tiled=True)

    def into(rows_in, weight):
        return jnp.einsum("td,edf->etf", rows_in, weight, preferred_element_type=wide)

    own_up_pre = into(rows_own, up_w)
    own_up_pre, *down_far = together(own_up_pre, *down_far)
    down_w = doubled(down_own, down_far, 0)
    part_own = expert_block(
        into(rows_own, gate_w), own_up_pre, cot_all, gates_all[0], gate_w, up_w, down_w
    )
    rows_near, *part_own = together(rows_near, *part_own)
    part_near = expert_block(
        into(rows_near, gate_w),
        into(rows_near, up_w),
        cot_near,
        gates_all[1],
        gate_w,
        up_w,
        down_w,
    )

    grad_in_own = lax.psum_scatter(part_own[0], "expert", scatter_dimension=0, tiled=True)

    def mix(scaled):
        return jnp.einsum("etf,efd->td", scaled, down_w, preferred_element_type=wide).astype(low)

    near_in, grad_in_own, own_mixed, near_mixed = together(
        part_near[0], grad_in_own, mix(part_own[2]), mix(part_near[2])
    )
    grad_in_near = lax.psum_scatter(near_in, "expert", scatter_dimension=0, tiled=True)

    tall_sources = [(part_own[i], part_near[i]) for i in (3, 4)]
    flat_sources = [(part_own[2], part_near[2])]
    rows_pair, cot_pair = (rows_own, rows_near), (cot_all, cot_near)
    far = list(weight_grads(rows_pair, tall_sources, 1, True))
    chunks = []
    for size in (2, 1, 1, 4):
        chunks.append(far[: size * local_count // 2])
        far = far[size * local_count // 2 :]

    def send(number):
        chunks[number] = [swap_x(piece) for piece in chunks[number]]

    def tied(values, *numbers):
        held = together(*values, *[piece for i in numbers for piece in chunks[i]])
        place = len(values)
        for i in numbers:
            chunks[i] = list(held[place : place + len(chunks[i])])
            place += len(chunks[i])
        return held[: len(values)]

    held = tied((cot_near, near_mixed, part_own[1], part_near[1]), 0, 1, 2, 3)
    cot_pair, near_mixed, part_gates = (cot_all, held[0]), held[1], held[2:]
    send(0)
    far = list(weight_grads(cot_pair, flat_sources, 1, False))
    for size in (1, 3):
        chunks.append(far[: size * local_count // 2])
        far = far[size * local_count // 2 :]
    gate_grads = jnp.stack(part_gates)
    gate_grads = gate_grads.reshape(2, local_count, groups, tok_rows).transpose(2, 0, 1, 3)
    gate_grads = lax.all_to_all(gate_grads, "expert", split_axis=0, concat_axis=0)
    half_rows = seq_len // 2
    mixed_kept = lax.dynamic_slice_in_dim(near_mixed, core * half_rows, half_rows, 0)
    mixed_sent = lax.dynamic_slice_in_dim(near_mixed, (1 - core) * half_rows, half_rows, 0)
    mixed_half = (mixed_kept.astype(wide) + swap_core(mixed_sent).astype(wide)).astype(low)
    mixed_half, gate_grads = tied((mixed_half, gate_grads), 0, 1, 4, 5)
    send(1)

    gate_grads = gate_grads.transpose(1, 3, 0, 2).reshape(2, tok_rows, experts)
    gate_grads = gate_grads[0] + swap_y(gate_grads[1])
    grad_in_near, gate_grads = tied((grad_in_near, gate_grads), 1, 2)
    send(2)
    grad_mlp_in = grad_in_own.astype(wide) + swap_y(grad_in_near).astype(wide)
    grad_logits = gates_own * (gate_grads - jnp.sum(gates_own * gate_grads, axis=-1, keepdims=True))
    grad_router = jnp.einsum("te,td->ed", grad_logits, mlp_low.astype(wide), precision=PRECISE)
    grad_mlp_in = grad_mlp_in + jnp.einsum(
        "te,ed->td", grad_logits, router_t.astype(wide), precision=PRECISE
    )
    grad_out = cot.astype(wide)
    grad_hidden_norm, grad_gain_mlp = rms_back(grad_mlp_in, mlp_normal, mlp_factor, mlp_gain)
    grad_hidden = grad_out + grad_hidden_norm
    grad_attn_low, mixed_half = tied((grad_hidden.astype(low), mixed_half), 2, 3)
    grad_attn_all = lax.all_gather(grad_attn_low, "expert", axis=0, tiled=True)
    mixed_half = swap_y(mixed_half)
    send(3)

    grad_gate, grad_up = weight_grads(rows_pair, tall_sources, 0, True)
    (grad_down,) = weight_grads(cot_pair, flat_sources, 0, False)
    held = tied((grad_attn_all, mixed_half, grad_gate, grad_up, grad_down), 3, 4)
    grad_attn_all, mixed_half, grad_gate, grad_up, grad_down = held
    send(4)
    mixed = own_mixed.astype(wide)
    half_own = lax.dynamic_slice_in_dim(mixed, core * half_rows, half_rows, 0)
    mixed = lax.dynamic_update_slice_in_dim(
        own_mixed, (half_own + mixed_half.astype(wide)).astype(low), core * half_rows, 0
    )
    mixed = lax.psum_scatter(mixed, "expert", scatter_dimension=0, tiled=True)
    grad_value_low, query_scaled, key_scaled, query_inner, key_inner, *gain_grads = attend_back(
        lengths,
        grad_attn_all,
        out_w,
        attended,
        log_total,
        query_low,
        key_low,
        value_low,
        qkv,
        *norm_args,
    )
    held = tied(
        (grad_value_low, query_scaled, key_scaled, query_inner, key_inner, grad_attn_all), 4
    )
    grad_value_low, query_scaled, key_scaled, query_inner, key_inner, grad_attn_all = held
    grad_w_out = contract_rows(attended_low, grad_attn_all).reshape(2, 2, shard, model_width)
    kept = lax.dynamic_index_in_dim(grad_w_out, core, 1, keepdims=False)
    given = lax.dynamic_index_in_dim(grad_w_out, 1 - core, 1, keepdims=False)
    grad_w_out = in_order(kept.astype(low), swap_core(given.astype(low)), core)
    grad_gain_query, grad_gain_key = gain_grads[0][0], gain_grads[1][0]

    def by_parts(upstream):
        return contract_rows(attn_low, upstream).reshape(2, 2, groups * shard, -1)

    query_normal, key_normal = query_pre * query_factor, key_pre * key_factor
    inner = jnp.stack([query_inner[:, 0], key_inner[:, 0]])
    inner = sum_experts(inner)
    inner, grad_w_out = together(inner, grad_w_out)
    out_parts = scatter_first(grad_w_out)
    inner = inner / model_width
    grad_query_low = (query_factor * (query_scaled - query_normal * inner[0][:, None])).astype(low)
    grad_key_low = (key_factor * (key_scaled - key_normal * inner[1][:, None])).astype(low)
    grad_qkv = jnp.concatenate([grad_query_low, grad_key_low, grad_value_low], axis=1)
    qkv_w_grad = by_parts(grad_qkv)
    grad_qkv, qkv_w_grad = together(grad_qkv, qkv_w_grad)
    qkv_parts = scatter_first(qkv_w_grad)
    grad_in_part = times_transpose(grad_qkv, qkv_w)
    count = len(qkv_parts)
    held = together(grad_in_part.astype(low), mixed, *qkv_parts, *out_parts)
    grad_in_low, mixed, qkv_parts, out_parts = held[0], held[1], held[2 : 2 + count], held[2 + count :]
    grad_attn_in = lax.psum_scatter(grad_in_low, "expert", scatter_dimension=0, tiled=True)
    grad_attn_in = grad_attn_in.astype(wide)
    grad_gain_attn = jnp.sum(grad_in_part * attn_normal, axis=0)
    _, own_normal, own_factor = rms_parts(tok.astype(wide), attn_gain)
    grad_attn_x, _ = rms_back(grad_attn_in, own_normal, own_factor, attn_gain)
    grad_tokens = (grad_hidden + grad_attn_x).astype(low)

    small = jnp.concatenate(
        [
            grad_router,
            grad_gain_attn[None],
            spread_heads(grad_gain_query)[None],
            spread_heads(grad_gain_key)[None],
            grad_gain_mlp[None],
        ],
        axis=0,
    )
    small = small.reshape(pack_rows, devices, shard).transpose(1, 0, 2).reshape(devices, -1, 128)
    held = tied((*scatter_ready(*qkv_parts), *scatter_ready(*out_parts), small), 5)
    send(5)
    qkv_parts, out_parts, small = held[:5], held[5:10], held[10]
    small = lax.all_to_all(small, everyone, split_axis=0, concat_axis=0)
    small = jnp.sum(small, axis=0).reshape(pack_rows, shard)
    grad_w_qkv = scatter_last(*qkv_parts).astype(low)
    grad_w_out = scatter_last(*out_parts)
    small, grad_w_qkv, grad_w_out, grad_gate, grad_up = together(
        small, grad_w_qkv, grad_w_out, grad_gate, grad_up
    )
    pieces = [piece for chunk in chunks for piece in chunk]
    part = 2 * local_count
    grad_gate = add_pieces(grad_gate, pieces[:part], 1)
    grad_up = add_pieces(grad_up, pieces[part : 2 * part], 1)
    grad_w_qkv = grad_w_qkv.reshape(groups, shard, 3 * own_width)
    grad_w_qkv = lax.all_to_all(grad_w_qkv, "expert", split_axis=0, concat_axis=0)
    grad_w_qkv, grad_gate, grad_up, grad_tokens = together(
        grad_w_qkv, grad_gate, grad_up, grad_tokens
    )
    grad_w_qkv = grad_w_qkv.reshape(chips, 2, shard, 3, 2, HEAD_DIM).astype(wide)
    grad_w_qkv = grad_w_qkv.transpose(3, 2, 1, 4, 0, 5).reshape(3, shard, model_width)
    grad_down, grad_w_qkv, grad_tokens = together(grad_down, grad_w_qkv, grad_tokens)
    grad_down = add_pieces(grad_down, pieces[2 * part :], 0)

    output = (hidden + mixed.astype(wide)).astype(low)
    return (
        output[None],
        grad_tokens[None],
        grad_w_qkv[0],
        grad_w_qkv[1],
        grad_w_qkv[2],
        grad_w_out,
        small[:experts].T,
        small[experts],
        small[experts + 1],
        small[experts + 2],
        small[experts + 3],
        grad_gate,
        grad_up,
        grad_down,
    )


def specs(dp):
    both = (dp, "expert") if isinstance(dp, str) else dp + ("expert",)
    rows, weight, vector = P(dp, "expert", None), P(both, None), P(both)
    columns, depth = P("expert", None, dp), P("expert", dp, None)
    taken = (rows, rows, P(dp), rows) + (weight,) * 5 + (vector,) * 4 + (columns, columns, depth)
    given = (rows, rows) + (weight,) * 5 + (vector,) * 4 + (columns, columns, depth)
    return (taken, given)


def solution(mesh):
    parts, groups = mesh.shape["dp"], mesh.shape["expert"]

    def whole(*args):
        model_width = args[0].shape[2]
        by_heads = (
            parts == 4
            and groups % 2 == 0
            and model_width == 2 * HEAD_DIM * groups
            and 2 * model_width == parts * groups * HEAD_DIM
        )
        if by_heads:
            used = jax.sharding.Mesh(
                mesh.devices.reshape(2, 2, groups), ("dy", "dx", "expert")
            )
            taken, given = specs(("dy", "dx"))
            body = per_device_by_heads
        else:
            used = mesh
            taken, given = specs("dp")
            body = per_device
        return jax.shard_map(
            body, mesh=used, in_specs=taken, out_specs=given, check_vma=False
        )(*args)

    return whole
```

```python
import functools

import jax
import jax.numpy as jnp
from jax import lax
from jax.experimental import pallas as pl
from jax.experimental.layout import Layout, with_layout_constraint
from jax.experimental.pallas import tpu as pltpu
from jax.sharding import PartitionSpec as P

HEAD_DIM = 128
TOP = 8


PRECISE = lax.Precision.HIGHEST
EPSILON = 1e-05
ROPE_BASE = 10000.0
MASKED = -1e30


def rms_parts(values, gain):
    factor = lax.rsqrt(jnp.mean(values * values, axis=-1, keepdims=True) + EPSILON)
    normal = values * factor
    return (normal * gain, normal, factor)


def rms_back(upstream, normal, factor, gain):
    scaled = upstream * gain
    inner_mean = jnp.mean(scaled * normal, axis=-1, keepdims=True)
    return (factor * (scaled - normal * inner_mean), jnp.sum(upstream * normal, axis=0))


def rope_tables(positions):
    half_dim = HEAD_DIM // 2
    frequency = ROPE_BASE ** (-2.0 * jnp.arange(half_dim).astype(jnp.float32) / HEAD_DIM)
    angles = positions.astype(jnp.float32)[:, None] * frequency[None, :]
    return (jnp.cos(angles)[:, None, :], jnp.sin(angles)[:, None, :])


def rotate(values, cosine, sine_part, direction):
    half_dim = values.shape[-1] // 2
    front_half = values[..., :half_dim]
    behind = values[..., half_dim:]
    return jnp.concatenate(
        [
            front_half * cosine - direction * behind * sine_part,
            behind * cosine + direction * front_half * sine_part,
        ],
        axis=-1,
    )


def contract_rows(left_side, right_side):
    return lax.dot_general(
        left_side, right_side, (((0,), (0,)), ((), ())), preferred_element_type=jnp.float32
    )


def times_transpose(left_side, right_side):
    return lax.dot_general(
        left_side, right_side, (((1,), (1,)), ((), ())), preferred_element_type=jnp.float32
    )


def score_grads(
    query_heads,
    key_heads,
    value_heads,
    grad_heads,
    log_total,
    row_delta,
    query_place,
    key_place,
    length,
):
    factor = HEAD_DIM ** (-0.5)
    scores = (
        jnp.einsum("qhd,khd->hqk", query_heads, key_heads, preferred_element_type=jnp.float32)
        * factor
    )
    allowed = (key_place[None, :] <= query_place[:, None]) & (key_place[None, :] < length)
    weights_full = jnp.where(allowed[None], jnp.exp(scores - log_total[:, :, None]), 0.0)
    grad_weights = jnp.einsum(
        "qhd,khd->hqk", grad_heads, value_heads, preferred_element_type=jnp.float32
    )
    grad_scores = (weights_full * (grad_weights - row_delta[:, :, None])).astype(jnp.bfloat16)
    return (weights_full.astype(jnp.bfloat16), grad_scores)


def per_device(
    tokens,
    cotangent,
    lengths,
    routes,
    w_query,
    w_key,
    w_value,
    w_output,
    router,
    gain_attn,
    gain_query,
    gain_key,
    gain_mlp,
    w_gate,
    w_up,
    w_down,
):
    tok_rows = tokens.shape[1]
    model_width = tokens.shape[2]
    head_count = model_width // HEAD_DIM
    groups = lax.axis_size("expert")
    seq_len = tok_rows * groups
    length = lengths[0]
    factor = HEAD_DIM ** (-0.5)
    gathered = (
        lax.all_gather(w_query.astype(jnp.bfloat16), ("dp", "expert"), axis=0, tiled=True),
        lax.all_gather(w_key.astype(jnp.bfloat16), ("dp", "expert"), axis=0, tiled=True),
        lax.all_gather(w_value.astype(jnp.bfloat16), ("dp", "expert"), axis=0, tiled=True),
        lax.all_gather(w_output.astype(jnp.bfloat16), ("dp", "expert"), axis=0, tiled=True),
        lax.all_gather(router.astype(jnp.bfloat16), ("dp", "expert"), axis=0, tiled=True),
        lax.all_gather(gain_attn.astype(jnp.bfloat16), ("dp", "expert"), axis=0, tiled=True),
        lax.all_gather(gain_query.astype(jnp.bfloat16), ("dp", "expert"), axis=0, tiled=True),
        lax.all_gather(gain_key.astype(jnp.bfloat16), ("dp", "expert"), axis=0, tiled=True),
        lax.all_gather(gain_mlp.astype(jnp.bfloat16), ("dp", "expert"), axis=0, tiled=True),
    )
    query_weight, key_weight, value_weight, output_weight, router_weight = (
        gathered[0],
        gathered[1],
        gathered[2],
        gathered[3],
        gathered[4],
    )
    attn_gain = gathered[5].astype(jnp.float32)
    query_gain = gathered[6].astype(jnp.float32)
    key_gain = gathered[7].astype(jnp.float32)
    mlp_gain = gathered[8].astype(jnp.float32)
    gate_weight, up_weight, down_weight = (
        lax.all_gather(w_gate.astype(jnp.bfloat16), "dp", axis=2, tiled=True),
        lax.all_gather(w_up.astype(jnp.bfloat16), "dp", axis=2, tiled=True),
        lax.all_gather(w_down.astype(jnp.bfloat16), "dp", axis=1, tiled=True),
    )
    token_rows = tokens[0].astype(jnp.float32)
    attn_in, attn_normal, attn_factor = rms_parts(token_rows, attn_gain)
    attn_low = attn_in.astype(jnp.bfloat16)
    query_pre = jnp.dot(attn_low, query_weight, preferred_element_type=jnp.float32)
    key_pre = jnp.dot(attn_low, key_weight, preferred_element_type=jnp.float32)
    value_low = jnp.dot(attn_low, value_weight, preferred_element_type=jnp.float32).astype(
        jnp.bfloat16
    )
    query_norm, query_normal, query_factor = rms_parts(query_pre, query_gain)
    key_norm, key_normal, key_factor = rms_parts(key_pre, key_gain)
    positions = lax.axis_index("expert") * tok_rows + jnp.arange(tok_rows)
    cosine, sine_part = rope_tables(positions)
    query_low = rotate(
        query_norm.reshape(tok_rows, head_count, HEAD_DIM), cosine, sine_part, 1.0
    ).astype(jnp.bfloat16)
    key_low = (
        rotate(key_norm.reshape(tok_rows, head_count, HEAD_DIM), cosine, sine_part, 1.0)
        .astype(jnp.bfloat16)
        .reshape(tok_rows, model_width)
    )
    whole_keys, whole_values = (
        lax.all_gather(key_low, "expert", axis=0, tiled=True),
        lax.all_gather(value_low, "expert", axis=0, tiled=True),
    )
    all_keys = whole_keys.reshape(seq_len, head_count, HEAD_DIM)
    all_values = whole_values.reshape(seq_len, head_count, HEAD_DIM)
    key_place = jnp.arange(seq_len)
    allowed = (key_place[None, :] <= positions[:, None]) & (key_place[None, :] < length)
    scores = (
        jnp.einsum("qhd,khd->hqk", query_low, all_keys, preferred_element_type=jnp.float32) * factor
    )
    scores = jnp.where(allowed[None], scores, MASKED)
    log_total = jax.nn.logsumexp(scores, axis=-1)
    weights_low = jnp.where(allowed[None], jnp.exp(scores - log_total[:, :, None]), 0.0).astype(
        jnp.bfloat16
    )
    attended = jnp.einsum(
        "hqk,khd->qhd", weights_low, all_values, preferred_element_type=jnp.float32
    ).reshape(tok_rows, model_width)
    attended_low = attended.astype(jnp.bfloat16)
    hidden = token_rows + jnp.dot(attended_low, output_weight, preferred_element_type=jnp.float32)
    mlp_in, mlp_normal, mlp_factor = rms_parts(hidden, mlp_gain)
    mlp_low = mlp_in.astype(jnp.bfloat16)
    logits = jnp.dot(mlp_low, router_weight, preferred_element_type=jnp.float32)
    route_ids = routes[0]
    gate_probs = jax.nn.softmax(jnp.take_along_axis(logits, route_ids, axis=1), axis=-1)
    experts = router_weight.shape[1]
    slot_cap = 2 * tok_rows * TOP // experts
    local_count = experts // groups
    pair_count = tok_rows * TOP
    flat_routes = route_ids.reshape(-1)
    expert_ids = jnp.arange(experts)
    hit_table = (flat_routes[:, None] == expert_ids[None, :]).astype(jnp.int32)
    slot_rank = jnp.sum((jnp.cumsum(hit_table, axis=0) - hit_table) * hit_table, axis=1)
    counts = jnp.sum(hit_table, axis=0)
    slot_ids = flat_routes * slot_cap + slot_rank
    slot_pair = (
        jnp.zeros((experts * slot_cap,), jnp.int32)
        .at[slot_ids]
        .set(jnp.arange(pair_count, dtype=jnp.int32))
    )
    send_rows = mlp_low[slot_pair // TOP].reshape(groups, local_count, slot_cap, model_width)
    send_counts = counts.reshape(groups, local_count).astype(jnp.bfloat16)
    arrived_rows, arrived_counts = (
        lax.all_to_all(send_rows, "expert", split_axis=0, concat_axis=0, tiled=True),
        lax.all_to_all(send_counts, "expert", split_axis=0, concat_axis=0, tiled=True),
    )
    living = (jnp.arange(slot_cap)[None, None, :] < arrived_counts.astype(jnp.int32)[:, :, None])[
        ..., None
    ]
    gate_pre = jnp.einsum(
        "nemd,edf->nemf", arrived_rows, gate_weight, preferred_element_type=jnp.float32
    )
    up_pre = jnp.einsum(
        "nemd,edf->nemf", arrived_rows, up_weight, preferred_element_type=jnp.float32
    )
    gate_sigmoid = jax.nn.sigmoid(gate_pre)
    activity = (gate_pre * gate_sigmoid * up_pre).astype(jnp.bfloat16)
    expert_out = jnp.einsum(
        "nemf,efd->nemd", activity, down_weight, preferred_element_type=jnp.float32
    ).astype(jnp.bfloat16)
    returned = lax.all_to_all(expert_out, "expert", split_axis=0, concat_axis=0, tiled=True)
    pair_out = (
        returned.reshape(experts * slot_cap, model_width)[slot_ids]
        .reshape(tok_rows, TOP, model_width)
        .astype(jnp.float32)
    )
    output = hidden + jnp.sum(gate_probs[:, :, None] * pair_out, axis=1)
    grad_out = cotangent[0].astype(jnp.float32)
    grad_gates = jnp.sum(grad_out[:, None, :] * pair_out, axis=-1)
    pair_grad = (
        (gate_probs[:, :, None] * grad_out[:, None, :])
        .astype(jnp.bfloat16)
        .reshape(pair_count, model_width)
    )
    send_grad = pair_grad[slot_pair].reshape(groups, local_count, slot_cap, model_width)
    arrived_grad = lax.all_to_all(send_grad, "expert", split_axis=0, concat_axis=0, tiled=True)
    arrived_grad = jnp.where(living, arrived_grad, jnp.zeros((), jnp.bfloat16))
    grad_activity = jnp.einsum(
        "nemd,efd->nemf", arrived_grad, down_weight, preferred_element_type=jnp.float32
    )
    grad_gate_pre = (
        grad_activity * up_pre * gate_sigmoid * (1.0 + gate_pre * (1.0 - gate_sigmoid))
    ).astype(jnp.bfloat16)
    grad_up_pre = (grad_activity * gate_pre * gate_sigmoid).astype(jnp.bfloat16)
    grad_down = jnp.einsum(
        "nemf,nemd->efd", activity, arrived_grad, preferred_element_type=jnp.float32
    )
    grad_gate = jnp.einsum(
        "nemd,nemf->edf", arrived_rows, grad_gate_pre, preferred_element_type=jnp.float32
    )
    grad_up = jnp.einsum(
        "nemd,nemf->edf", arrived_rows, grad_up_pre, preferred_element_type=jnp.float32
    )
    input_grad = (
        jnp.einsum("nemf,edf->nemd", grad_gate_pre, gate_weight, preferred_element_type=jnp.float32)
        + jnp.einsum("nemf,edf->nemd", grad_up_pre, up_weight, preferred_element_type=jnp.float32)
    ).astype(jnp.bfloat16)
    sent_back = lax.all_to_all(input_grad, "expert", split_axis=0, concat_axis=0, tiled=True)
    grad_mlp_in = jnp.sum(
        sent_back.reshape(experts * slot_cap, model_width)[slot_ids]
        .reshape(tok_rows, TOP, model_width)
        .astype(jnp.float32),
        axis=1,
    )
    grad_chosen = gate_probs * (
        grad_gates - jnp.sum(gate_probs * grad_gates, axis=-1, keepdims=True)
    )
    route_table = (route_ids[:, :, None] == expert_ids[None, None, :]).astype(jnp.float32)
    grad_logits = jnp.sum(grad_chosen[:, :, None] * route_table, axis=1)
    grad_router = jnp.einsum(
        "td,te->de", mlp_low.astype(jnp.float32), grad_logits, precision=PRECISE
    )
    grad_mlp_in = grad_mlp_in + jnp.einsum(
        "te,de->td", grad_logits, router_weight.astype(jnp.float32), precision=PRECISE
    )
    grad_hidden_norm, grad_gain_mlp = rms_back(grad_mlp_in, mlp_normal, mlp_factor, mlp_gain)
    grad_hidden = grad_out + grad_hidden_norm
    grad_attn_low = grad_hidden.astype(jnp.bfloat16)
    grad_w_out = contract_rows(attended_low, grad_attn_low)
    grad_attended = times_transpose(grad_attn_low, output_weight).astype(jnp.bfloat16)
    row_delta = jnp.sum(
        (grad_attended.astype(jnp.float32) * attended).reshape(tok_rows, head_count, HEAD_DIM),
        axis=-1,
    ).T
    grad_heads = grad_attended.reshape(tok_rows, head_count, HEAD_DIM)
    block_rows = min(512, seq_len)
    block_total = seq_len // block_rows

    def key_part(number):
        offset = number * block_rows
        block_keys = lax.dynamic_slice_in_dim(all_keys, offset, block_rows, 0)
        block_values = lax.dynamic_slice_in_dim(all_values, offset, block_rows, 0)
        weights_part, grad_scores = score_grads(
            query_low,
            block_keys,
            block_values,
            grad_heads,
            log_total,
            row_delta,
            positions,
            offset + jnp.arange(block_rows),
            length,
        )
        grad_query_part = (
            jnp.einsum("hqk,khd->qhd", grad_scores, block_keys, preferred_element_type=jnp.float32)
            * factor
        )
        grad_key_part = (
            jnp.einsum("hqk,qhd->khd", grad_scores, query_low, preferred_element_type=jnp.float32)
            * factor
        )
        grad_value_part = jnp.einsum(
            "hqk,qhd->khd", weights_part, grad_heads, preferred_element_type=jnp.float32
        )
        return (
            grad_query_part,
            grad_key_part.reshape(block_rows, model_width),
            grad_value_part.reshape(block_rows, model_width),
        )

    query_parts, key_parts, value_parts = lax.map(
        lambda number: key_part(number), jnp.arange(block_total)
    )
    grad_query = jnp.sum(query_parts, axis=0).reshape(tok_rows, model_width)
    grad_key, grad_value = (
        lax.psum_scatter(
            key_parts.reshape(seq_len, model_width).astype(jnp.bfloat16),
            "expert",
            scatter_dimension=0,
            tiled=True,
        ).astype(jnp.float32),
        lax.psum_scatter(
            value_parts.reshape(seq_len, model_width).astype(jnp.bfloat16),
            "expert",
            scatter_dimension=0,
            tiled=True,
        ).astype(jnp.float32),
    )
    grad_value_low = grad_value.astype(jnp.bfloat16)
    grad_query_rot = (
        grad_query.astype(jnp.bfloat16).astype(jnp.float32).reshape(tok_rows, head_count, HEAD_DIM)
    )
    grad_key_rot = (
        grad_key.astype(jnp.bfloat16).astype(jnp.float32).reshape(tok_rows, head_count, HEAD_DIM)
    )
    grad_query_norm = rotate(grad_query_rot, cosine, sine_part, -1.0).reshape(tok_rows, model_width)
    grad_key_norm = rotate(grad_key_rot, cosine, sine_part, -1.0).reshape(tok_rows, model_width)
    grad_query_pre, grad_gain_query = rms_back(
        grad_query_norm, query_normal, query_factor, query_gain
    )
    grad_key_pre, grad_gain_key = rms_back(grad_key_norm, key_normal, key_factor, key_gain)
    grad_query_low = grad_query_pre.astype(jnp.bfloat16)
    grad_key_low = grad_key_pre.astype(jnp.bfloat16)
    grad_wq = contract_rows(attn_low, grad_query_low)
    grad_wk = contract_rows(attn_low, grad_key_low)
    grad_wv = contract_rows(attn_low, grad_value_low)
    grad_attn_in = (
        times_transpose(grad_query_low, query_weight)
        + times_transpose(grad_key_low, key_weight)
        + times_transpose(grad_value_low, value_weight)
    )
    grad_attn_x, grad_gain_attn = rms_back(grad_attn_in, attn_normal, attn_factor, attn_gain)
    grad_tokens = (grad_hidden + grad_attn_x).astype(jnp.bfloat16)
    summed_grads = (
        lax.psum_scatter(grad_wq, ("dp", "expert"), scatter_dimension=0, tiled=True),
        lax.psum_scatter(grad_wk, ("dp", "expert"), scatter_dimension=0, tiled=True),
        lax.psum_scatter(grad_wv, ("dp", "expert"), scatter_dimension=0, tiled=True),
        lax.psum_scatter(grad_w_out, ("dp", "expert"), scatter_dimension=0, tiled=True),
        lax.psum_scatter(grad_router, ("dp", "expert"), scatter_dimension=0, tiled=True),
        lax.psum_scatter(grad_gain_attn, ("dp", "expert"), scatter_dimension=0, tiled=True),
        lax.psum_scatter(grad_gain_query, ("dp", "expert"), scatter_dimension=0, tiled=True),
        lax.psum_scatter(grad_gain_key, ("dp", "expert"), scatter_dimension=0, tiled=True),
        lax.psum_scatter(grad_gain_mlp, ("dp", "expert"), scatter_dimension=0, tiled=True),
    )
    expert_grads = (
        lax.psum_scatter(
            grad_gate.astype(jnp.bfloat16), "dp", scatter_dimension=2, tiled=True
        ).astype(jnp.float32),
        lax.psum_scatter(
            grad_up.astype(jnp.bfloat16), "dp", scatter_dimension=2, tiled=True
        ).astype(jnp.float32),
        lax.psum_scatter(
            grad_down.astype(jnp.bfloat16), "dp", scatter_dimension=1, tiled=True
        ).astype(jnp.float32),
    )
    return (
        output.astype(jnp.bfloat16)[None],
        grad_tokens[None],
        summed_grads[0],
        summed_grads[1],
        summed_grads[2],
        summed_grads[3],
        summed_grads[4],
        summed_grads[5],
        summed_grads[6],
        summed_grads[7],
        summed_grads[8],
        expert_grads[0],
        expert_grads[1],
        expert_grads[2],
    )


FLIP = [(0, 1), (1, 0)]


def in_order(own, other, index):
    first = jnp.where(index == 0, own, other)
    second = jnp.where(index == 0, other, own)
    return jnp.stack([first, second])


def swap_x(block):
    return lax.ppermute(block, "dx", FLIP)


def swap_y(block):
    return lax.ppermute(block, "dy", FLIP)


def swap_core(block):
    groups = lax.axis_size("expert")
    return lax.ppermute(block, "expert", [(i, i ^ 1) for i in range(groups)])


def row_major(value):
    return with_layout_constraint(value, Layout(major_to_minor=tuple(range(value.ndim))))


def together(*values):
    return lax.optimization_barrier(values)


def gather_first(block):
    return (block, swap_x(block), swap_y(block))


def gather_second(block, beside, below):
    half = block.shape[0] // 2
    return (block, beside, below, swap_x(below[:half]), swap_y(beside[half:]))


def gather_last(block, beside, below, upper, under):
    column, row = lax.axis_index("dx"), lax.axis_index("dy")
    across = jnp.concatenate([upper, under], axis=0)
    return in_order(in_order(block, beside, column), in_order(below, across, column), row)


def scatter_first(blocks):
    column, row = lax.axis_index("dx"), lax.axis_index("dy")
    low = jnp.bfloat16

    def pick(at_row, at_column):
        line = lax.dynamic_index_in_dim(blocks, at_row, 0, keepdims=False)
        return lax.dynamic_index_in_dim(line, at_column, 0, keepdims=False)

    half = blocks.shape[2] // 2
    across = pick(1 - row, 1 - column).astype(low)
    beside, below = pick(row, 1 - column), pick(1 - row, column)
    return (
        pick(row, column),
        beside[:half],
        below[half:],
        beside[half:].astype(low),
        below[:half].astype(low),
        swap_y(across[:half]),
        swap_x(across[half:]),
    )


def scatter_ready(kept, beside, below, beside_rest, below_rest, far_below, far_beside):
    low, wide = jnp.bfloat16, jnp.float32
    beside = (beside + far_below.astype(wide)).astype(low)
    below = (below + far_beside.astype(wide)).astype(low)
    return (kept, beside, below, beside_rest, below_rest)


def scatter_last(kept, beside, below, beside_rest, below_rest):
    wide = jnp.float32
    added = jnp.concatenate(
        [
            swap_x(beside).astype(wide) + swap_y(below_rest).astype(wide),
            swap_x(beside_rest).astype(wide) + swap_y(below).astype(wide),
        ]
    )
    return kept + added


def sum_experts(values):
    groups = lax.axis_size("expert")
    flat = values.reshape(-1, 128)
    spread = jnp.broadcast_to(flat[None], (groups,) + flat.shape)
    arrived = lax.all_to_all(spread, "expert", split_axis=0, concat_axis=0)
    return jnp.sum(arrived, axis=0).reshape(values.shape)


def dense_gates(logits, route_ids):
    columns = jnp.arange(logits.shape[-1])
    chosen = jnp.any(route_ids[:, :, None] == columns[None, None, :], axis=1)
    highest = jnp.max(jnp.where(chosen, logits, -jnp.inf), axis=-1, keepdims=True)
    weights = jnp.where(chosen, jnp.exp(logits - highest), 0.0)
    return weights / jnp.sum(weights, axis=-1, keepdims=True)


def mul_nn(left_side, right_side):
    return jnp.dot(left_side, right_side, preferred_element_type=jnp.float32)


VMEM_BYTES = 56 * 1024 * 1024
ROWS = 256


def whole_blocks(count):
    return [pl.BlockSpec(memory_space=pltpu.VMEM)] * count


def turn(values, cosine, signed_sine):
    return values * cosine + pltpu.roll(values, HEAD_DIM // 2, 1) * signed_sine


def allowed_block(first_row, rows, columns, length):
    at_row = first_row + lax.broadcasted_iota(jnp.int32, (rows, columns), 0)
    at_column = lax.broadcasted_iota(jnp.int32, (rows, columns), 1)
    return (at_column <= at_row) & (at_column < length)


def attend_kernel(
    length_ref,
    qkv_ref,
    query_factor_ref,
    key_factor_ref,
    query_gain_ref,
    key_gain_ref,
    cosine_ref,
    sine_ref,
    out_w_ref,
    query_ref,
    key_ref,
    value_ref,
    attended_ref,
    total_ref,
    part_ref,
):
    low = jnp.bfloat16
    seq_len, heads = qkv_ref.shape[0], 2
    length = length_ref[0]
    width = heads * HEAD_DIM
    factor = HEAD_DIM ** (-0.5)

    @pl.loop(0, seq_len // ROWS)
    def _(number):
        rows = pl.ds(pl.multiple_of(number * ROWS, ROWS), ROWS)
        cosine, sine_part = cosine_ref[rows, :], sine_ref[rows, :]
        for head in range(heads):
            part = slice(head * HEAD_DIM, (head + 1) * HEAD_DIM)
            later = slice(width + head * HEAD_DIM, width + (head + 1) * HEAD_DIM)
            query = qkv_ref[rows, part] * query_factor_ref[rows, :] * query_gain_ref[:, part]
            key = qkv_ref[rows, later] * key_factor_ref[rows, :] * key_gain_ref[:, part]
            query_ref[rows, part] = turn(query, cosine, sine_part).astype(low)
            key_ref[rows, part] = turn(key, cosine, sine_part).astype(low)
        value_ref[rows, :] = qkv_ref[rows, 2 * width :].astype(low)

    for number in range(seq_len // ROWS):
        first, end = number * ROWS, (number + 1) * ROWS
        allowed = allowed_block(first, ROWS, end, length)
        done = []
        for head in range(heads):
            part = slice(head * HEAD_DIM, (head + 1) * HEAD_DIM)
            scores = times_transpose(query_ref[first:end, part], key_ref[:end, part]) * factor
            scores = jnp.where(allowed, scores, MASKED)
            highest = jnp.max(scores, axis=1, keepdims=True)
            weights = jnp.exp(scores - highest)
            total = jnp.sum(weights, axis=1, keepdims=True)
            weights = (weights * (1.0 / total)).astype(low)
            total_ref[head, first:end, :] = highest + jnp.log(total)
            attended = mul_nn(weights, value_ref[:end, part])
            attended_ref[first:end, part] = attended
            done.append(attended.astype(low))
        part_ref[first:end, :] = mul_nn(jnp.concatenate(done, axis=1), out_w_ref[...]).astype(low)


def attend(length, qkv, query_factor, key_factor, query_gain, key_gain, cosine, sine_part, out_w):
    seq_len, width, model_width = qkv.shape[0], qkv.shape[1] // 3, out_w.shape[1]
    low, wide = jnp.bfloat16, jnp.float32
    rows = jax.ShapeDtypeStruct((seq_len, width), low)
    return pl.pallas_call(
        attend_kernel,
        in_specs=[pl.BlockSpec(memory_space=pltpu.SMEM)] + whole_blocks(8),
        out_specs=whole_blocks(6),
        out_shape=[
            rows,
            rows,
            rows,
            jax.ShapeDtypeStruct((seq_len, width), wide),
            jax.ShapeDtypeStruct((2, seq_len, 1), wide),
            jax.ShapeDtypeStruct((seq_len, model_width), low),
        ],
        compiler_params=pltpu.CompilerParams(vmem_limit_bytes=VMEM_BYTES),
        cost_estimate=pl.CostEstimate(
            flops=2 * seq_len * width * (seq_len + model_width),
            bytes_accessed=14 * seq_len * width + 2 * seq_len * model_width,
            transcendentals=seq_len * seq_len,
        ),
    )(length, qkv, query_factor, key_factor, query_gain, key_gain, cosine, sine_part, out_w)


def attend_back_kernel(
    length_ref,
    upstream_ref,
    out_w_ref,
    attended_ref,
    total_ref,
    query_ref,
    key_ref,
    value_ref,
    qkv_ref,
    query_factor_ref,
    key_factor_ref,
    query_gain_ref,
    key_gain_ref,
    cosine_ref,
    sine_ref,
    grad_value_ref,
    query_scaled_ref,
    key_scaled_ref,
    query_inner_ref,
    key_inner_ref,
    query_gain_grad_ref,
    key_gain_grad_ref,
    key_sum_ref,
    value_sum_ref,
):
    low, wide = jnp.bfloat16, jnp.float32
    seq_len, heads = qkv_ref.shape[0], 2
    length = length_ref[0]
    width = heads * HEAD_DIM
    factor = HEAD_DIM ** (-0.5)
    blocks = seq_len // ROWS

    def norm_back(sums, rows, head, offset, factor_ref, gain_ref, scaled_ref, inner_ref, grad_ref, fresh):
        part = slice(head * HEAD_DIM, (head + 1) * HEAD_DIM)
        place = slice(offset + head * HEAD_DIM, offset + (head + 1) * HEAD_DIM)
        upstream = turn(sums.astype(low).astype(wide), cosine_ref[rows, :], -sine_ref[rows, :])
        normal = qkv_ref[rows, place] * factor_ref[rows, :]
        gain_part = jnp.sum(upstream * normal, axis=0, keepdims=True)
        scaled = upstream * gain_ref[:, part]
        scaled_ref[rows, part] = scaled
        inner = jnp.sum(scaled * normal, axis=1, keepdims=True)
        if head == 0:
            inner_ref[rows, :] = inner
        else:
            inner_ref[rows, :] += inner
        if fresh:
            grad_ref[:, part] = gain_part
        else:
            grad_ref[:, part] += gain_part

    for number in reversed(range(blocks)):
        first, end = number * ROWS, (number + 1) * ROWS
        allowed = allowed_block(first, ROWS, end, length)
        rows = slice(first, end)
        grads = times_transpose(upstream_ref[rows, :], out_w_ref[...]).astype(low)
        for head in range(heads):
            part = slice(head * HEAD_DIM, (head + 1) * HEAD_DIM)
            query, keys = query_ref[rows, part], key_ref[:end, part]
            grad = grads[:, part]
            delta = jnp.sum(grad.astype(wide) * attended_ref[rows, part], axis=1, keepdims=True)
            scores = times_transpose(query, keys) * factor
            weights = jnp.where(allowed, jnp.exp(scores - total_ref[head, rows, :]), 0.0)
            grad_weights = times_transpose(grad, value_ref[:end, part])
            grad_scores = (weights * (grad_weights - delta)).astype(low)
            query_sum = mul_nn(grad_scores, keys) * factor
            key_sum = contract_rows(grad_scores, query)
            value_sum = contract_rows(weights.astype(low), grad)
            if number == blocks - 1:
                key_sum_ref[:, part] = key_sum
                value_sum_ref[:, part] = value_sum
            else:
                key_sum_ref[:end, part] += key_sum
                value_sum_ref[:end, part] += value_sum
            norm_back(
                query_sum,
                rows,
                head,
                0,
                query_factor_ref,
                query_gain_ref,
                query_scaled_ref,
                query_inner_ref,
                query_gain_grad_ref,
                number == blocks - 1,
            )
    for number in range(blocks):
        rows = slice(number * ROWS, (number + 1) * ROWS)
        grad_value_ref[rows, :] = value_sum_ref[rows, :].astype(low)
        for head in range(heads):
            part = slice(head * HEAD_DIM, (head + 1) * HEAD_DIM)
            norm_back(
                key_sum_ref[rows, part] * factor,
                rows,
                head,
                width,
                key_factor_ref,
                key_gain_ref,
                key_scaled_ref,
                key_inner_ref,
                key_gain_grad_ref,
                number == 0,
            )


def attend_back(length, upstream, out_w, attended, total, query, key, value, qkv, *rest):
    seq_len, width = attended.shape
    low, wide = jnp.bfloat16, jnp.float32
    shape = jax.ShapeDtypeStruct
    return pl.pallas_call(
        attend_back_kernel,
        in_specs=[pl.BlockSpec(memory_space=pltpu.SMEM)] + whole_blocks(14),
        out_specs=whole_blocks(7),
        out_shape=[
            shape((seq_len, width), low),
            shape((seq_len, width), wide),
            shape((seq_len, width), wide),
            shape((seq_len, 1), wide),
            shape((seq_len, 1), wide),
            shape((1, width), wide),
            shape((1, width), wide),
        ],
        scratch_shapes=[pltpu.VMEM((seq_len, width), wide), pltpu.VMEM((seq_len, width), wide)],
        compiler_params=pltpu.CompilerParams(vmem_limit_bytes=VMEM_BYTES),
        cost_estimate=pl.CostEstimate(
            flops=2 * seq_len * width * (3 * seq_len + upstream.shape[1]),
            bytes_accessed=30 * seq_len * width + 2 * upstream.size,
            transcendentals=seq_len * seq_len,
        ),
    )(length, upstream, out_w, attended, total, query, key, value, qkv, *rest)


def put_halves(outs, place, expert, axis, value):
    if len(outs[0].shape) == 3:
        outs[expert[0]][expert[1]] = value
        return
    length = value.shape[axis] // 2
    for half in range(2):
        span = slice(half * length, (half + 1) * length)
        at = (span, slice(None)) if axis == 0 else (slice(None), span)
        outs[2 * place + half][...] = value[at].astype(jnp.bfloat16)


def tall_kernel(count, *refs):
    outs = refs[2 + 4 * count :]
    first, second = refs[0][...].T, refs[1][...].T
    for kind in range(2):
        for expert in range(count):
            place = count * kind + expert
            one, two = refs[2 + 2 * place], refs[3 + 2 * place]
            value = mul_nn(first, one[...]) + mul_nn(second, two[...])
            put_halves(outs, place, (kind, expert), 1, value)


def flat_kernel(count, *refs):
    outs = refs[2 + 2 * count : -1]
    turned_ref = refs[-1]
    length, block = refs[2].shape

    @pl.when(pl.program_id(0) == 0)
    def _():
        for expert in range(count):
            for half in range(2):
                turned_ref[
                    expert * block : (expert + 1) * block, half * length : (half + 1) * length
                ] = refs[2 + 2 * expert + half][...].T

    for expert in range(count):
        span = slice(expert * block, (expert + 1) * block)
        value = mul_nn(turned_ref[span, :length], refs[0][...]) + mul_nn(
            turned_ref[span, length:], refs[1][...]
        )
        put_halves(outs, expert, (0, expert), 0, value)


def weight_grads(rows, sources, which, tall):
    length, model_width = rows[0].shape
    count, _, doubled = sources[0][0].shape
    block = doubled // 2
    tile = min(256, model_width)
    columns = pl.BlockSpec((length, tile), lambda i: (0, i))
    operands, in_specs = list(rows), [columns] * 2
    for pair in sources:
        for expert in range(count):
            operands += list(pair)
            in_specs += [
                pl.BlockSpec(
                    (None, length, block),
                    lambda i, expert=expert: (expert, 0, which),
                    pipeline_mode=pl.Buffered(1),
                )
            ] * 2
    kinds = len(sources)
    if which == 0:
        number, dtype = kinds, jnp.float32
        if tall:
            spec, shape = pl.BlockSpec((count, tile, block), lambda i: (0, i, 0)), (model_width, block)
        else:
            spec, shape = pl.BlockSpec((count, block, tile), lambda i: (0, 0, i)), (block, model_width)
        shape = (count,) + shape
    else:
        number, dtype = 2 * count * kinds, jnp.bfloat16
        if tall:
            spec, shape = pl.BlockSpec((tile, block // 2), lambda i: (i, 0)), (model_width, block // 2)
        else:
            spec, shape = pl.BlockSpec((block // 2, tile), lambda i: (0, i)), (block // 2, model_width)
    scratch = [] if tall else [pltpu.VMEM((count * block, 2 * length), jnp.bfloat16)]
    return pl.pallas_call(
        functools.partial(tall_kernel if tall else flat_kernel, count),
        grid=(model_width // tile,),
        in_specs=in_specs,
        out_specs=[spec] * number,
        out_shape=[jax.ShapeDtypeStruct(shape, dtype)] * number,
        scratch_shapes=scratch,
        compiler_params=pltpu.CompilerParams(vmem_limit_bytes=VMEM_BYTES),
        cost_estimate=pl.CostEstimate(
            flops=4 * length * model_width * count * block * kinds,
            bytes_accessed=4 * length * model_width + 6 * count * model_width * block * kinds,
            transcendentals=0,
        ),
    )(*operands)


def add_kernel(axis, own_ref, *refs):
    out_ref = refs[-1]
    for expert in range(out_ref.shape[0]):
        pair = [ref[...].astype(jnp.float32) for ref in refs[2 * expert : 2 * expert + 2]]
        out_ref[expert] = own_ref[expert] + jnp.concatenate(pair, axis=axis)


def add_pieces(own, pieces, axis):
    count, rows, columns = own.shape
    tile = min(512, rows if axis else columns)
    if axis:
        full = pl.BlockSpec((count, tile, columns), lambda i: (0, i, 0))
        piece = pl.BlockSpec((tile, columns // 2), lambda i: (i, 0))
    else:
        full = pl.BlockSpec((count, rows, tile), lambda i: (0, 0, i))
        piece = pl.BlockSpec((rows // 2, tile), lambda i: (0, i))
    return pl.pallas_call(
        functools.partial(add_kernel, axis),
        grid=((rows if axis else columns) // tile,),
        in_specs=[full] + [piece] * len(pieces),
        out_specs=full,
        out_shape=jax.ShapeDtypeStruct(own.shape, own.dtype),
        input_output_aliases={0: 0},
        compiler_params=pltpu.CompilerParams(vmem_limit_bytes=VMEM_BYTES),
        cost_estimate=pl.CostEstimate(
            flops=own.size, bytes_accessed=10 * own.size, transcendentals=0
        ),
    )(own, *pieces)


def expert_block(gate_pre, up_pre, grad_rows, gates, gate_w, up_w, down_w):
    wide = jnp.float32
    back = jnp.einsum("td,efd->etf", grad_rows, down_w, preferred_element_type=wide)
    sigmoid = jax.nn.sigmoid(gate_pre)
    silu = gate_pre * sigmoid
    activity = silu * up_pre
    gate_grads = jnp.sum(activity * back, axis=-1)
    weight = gates
    scaled = (activity * weight).astype(jnp.bfloat16)
    back = back * weight
    grad_gate_pre = (back * up_pre * sigmoid * (1.0 + gate_pre * (1.0 - sigmoid))).astype(
        jnp.bfloat16
    )
    grad_up_pre = (back * silu).astype(jnp.bfloat16)
    grad_in = (
        jnp.einsum("etf,edf->td", grad_gate_pre, gate_w, preferred_element_type=wide)
        + jnp.einsum("etf,edf->td", grad_up_pre, up_w, preferred_element_type=wide)
    ).astype(jnp.bfloat16)
    return (grad_in, gate_grads, scaled, grad_gate_pre, grad_up_pre)


def per_device_by_heads(
    tokens,
    cotangent,
    lengths,
    routes,
    w_query,
    w_key,
    w_value,
    w_output,
    router,
    gain_attn,
    gain_query,
    gain_key,
    gain_mlp,
    w_gate,
    w_up,
    w_down,
):
    low, wide = jnp.bfloat16, jnp.float32
    everyone = ("dy", "dx", "expert")
    tok_rows, model_width = tokens.shape[1], tokens.shape[2]
    groups = lax.axis_size("expert")
    devices = 4 * groups
    chips = groups // 2
    seq_len = tok_rows * groups
    shard = w_query.shape[0]
    experts = router.shape[1]
    local_count = experts // groups
    group = lax.axis_index("expert")
    chip, core = group // 2, group % 2
    column, row = lax.axis_index("dx"), lax.axis_index("dy")
    length = lengths[0]
    factor = HEAD_DIM ** (-0.5)
    own_width = 2 * HEAD_DIM
    tok, cot = tokens[0], cotangent[0]

    def own_heads(vector):
        blocks = vector.reshape(2, 2, chips, HEAD_DIM)
        blocks = lax.dynamic_index_in_dim(blocks, core, 0, keepdims=False)
        return lax.dynamic_index_in_dim(blocks, chip, 1, keepdims=False).reshape(own_width)

    def spread_heads(vector):
        at_core = (jnp.arange(2) == core)[:, None, None, None]
        at_chip = (jnp.arange(chips) == chip)[None, None, :, None]
        return jnp.where(
            at_core & at_chip, vector.reshape(1, 2, 1, HEAD_DIM), 0.0
        ).reshape(model_width)

    def by_heads(weight):
        blocks = weight.astype(low).reshape(shard, 2, 2, chips, HEAD_DIM)
        return blocks.transpose(3, 1, 0, 2, 4).reshape(groups, shard, own_width)

    sent = jnp.concatenate([by_heads(w_query), by_heads(w_key), by_heads(w_value)], axis=2)
    packed = jnp.concatenate(
        [router.T, gain_attn[None], gain_query[None], gain_key[None], gain_mlp[None]], axis=0
    ).astype(low)
    pack_rows = experts + 4
    packed = packed.reshape(-1, 128)
    numbers = range(local_count)

    def experts_low(weight):
        pieces = [weight[0]]
        for i in numbers[1:]:
            pieces += jnp.split(weight[i], 2)
        return [row_major(piece.astype(low)) for piece in pieces]

    def joined(pieces):
        return [pieces[0]] + [
            jnp.concatenate(pieces[i : i + 2]) for i in range(1, len(pieces), 2)
        ]

    many = 2 * local_count - 1

    cosine, sine_part = rope_tables(jnp.arange(seq_len))
    cosine = jnp.concatenate([cosine[:, 0], cosine[:, 0]], axis=1)
    sine_part = jnp.concatenate([-sine_part[:, 0], sine_part[:, 0]], axis=1)
    sent, packed, out_rows, *gate_own = together(
        sent, packed, w_output.astype(low), *experts_low(w_gate)
    )
    up_own, down_own = experts_low(w_up), experts_low(w_down)
    out_rows, *held = together(out_rows, *up_own, *down_own)
    up_own, down_own = held[:many], held[many:]
    arrived = lax.all_to_all(sent, "expert", split_axis=0, concat_axis=0)
    gate_far = [swap_x(piece) for piece in gate_own[:-1]]
    held = together(
        arrived,
        packed,
        cot,
        cosine,
        sine_part,
        *gather_first(out_rows),
        *gate_far,
        gate_own[-1],
        *up_own,
        *down_own,
    )
    arrived, packed, cot, cosine, sine_part = held[:5]
    out_parts, held = held[5:8], held[8:]
    gate_far, gate_last, held = list(held[: many - 1]), held[many - 1], held[many:]
    up_own, down_own = held[:many], held[many:]
    packed = lax.all_to_all(
        jnp.broadcast_to(packed[None], (devices,) + packed.shape),
        everyone,
        split_axis=0,
        concat_axis=0,
    )
    qkv_parts = gather_first(arrived.reshape(groups * shard, 3 * own_width))
    held = together(packed, *qkv_parts, *out_parts)
    packed, qkv_parts, out_parts = held[0], held[1:4], held[4:]
    packed = (
        packed.reshape(devices, pack_rows, shard).transpose(1, 0, 2).reshape(pack_rows, model_width)
    )
    router_t = packed[:experts]
    attn_gain, query_gain, key_gain, mlp_gain = (
        packed[experts + i].astype(wide) for i in range(4)
    )
    tok_all = lax.all_gather(tok, "expert", axis=0, tiled=True)
    attn_in, attn_normal, _ = rms_parts(tok_all.astype(wide), attn_gain)
    held = together(
        attn_in.astype(low), *gather_second(*qkv_parts), *gather_second(*out_parts)
    )
    attn_low, qkv_parts, out_parts = held[0], held[1:6], held[6:]
    qkv_w = gather_last(*qkv_parts).reshape(model_width, 3 * own_width)

    cot_all = lax.all_gather(cot, "expert", axis=0, tiled=True)
    cot_half = lax.dynamic_slice_in_dim(cot_all, core * (seq_len // 2), seq_len // 2, 0)
    cot_half = swap_y(cot_half)

    qkv = jnp.dot(attn_low, qkv_w, preferred_element_type=wide)
    qkv, gate_last, *out_parts = together(qkv, gate_last, *out_parts)
    gate_far.append(swap_x(gate_last))
    out_quad = gather_last(*out_parts)
    out_first = lax.dynamic_index_in_dim(out_quad, core, 0, keepdims=False)
    out_other = swap_core(lax.dynamic_index_in_dim(out_quad, 1 - core, 0, keepdims=False))
    out_w = jnp.moveaxis(in_order(out_first, out_other, core), 0, 1)
    out_w = out_w.reshape(own_width, model_width)
    query_pre, key_pre = qkv[:, :own_width], qkv[:, own_width : 2 * own_width]
    squares = jnp.stack([jnp.sum(query_pre * query_pre, axis=1), jnp.sum(key_pre * key_pre, axis=1)])
    squares = sum_experts(squares)
    factors = lax.rsqrt(squares / model_width + EPSILON)
    query_factor, key_factor = factors[0][:, None], factors[1][:, None]
    query_gain_own, key_gain_own = own_heads(query_gain), own_heads(key_gain)
    norm_args = (
        query_factor,
        key_factor,
        query_gain_own[None],
        key_gain_own[None],
        cosine,
        sine_part,
    )
    query_low, key_low, value_low, attended, log_total, attn_part = attend(
        lengths, qkv, *norm_args, out_w
    )
    attended_low = attended.astype(low)
    held = together(attn_part, cot_all, *gate_far, *up_own, *down_own)
    attn_part, cot_all, gate_far, held = held[0], held[1], held[2 : 2 + many], held[2 + many :]
    up_own, down_own = held[:many], held[many:]
    attn_out = lax.psum_scatter(attn_part, "expert", scatter_dimension=0, tiled=True)
    up_far = [swap_x(piece) for piece in up_own]
    held = together(attn_out, cot_half, *up_far, *down_own)
    attn_out, cot_half, up_far, down_own = held[0], held[1], held[2 : 2 + many], held[2 + many :]
    down_far = [swap_x(piece) for piece in down_own[:-1]]
    cot_near = in_order(cot_half, swap_core(cot_half), core).reshape(seq_len, model_width)
    hidden = tok.astype(wide) + attn_out.astype(wide)
    mlp_in, mlp_normal, mlp_factor = rms_parts(hidden, mlp_gain)
    mlp_low = mlp_in.astype(low)
    gates_own = dense_gates(times_transpose(mlp_low, router_t), routes[0])

    rows_own = lax.all_gather(mlp_low, "expert", axis=0, tiled=True)
    mlp_near = swap_y(mlp_low)

    def doubled(own, far, axis):
        return jnp.stack(
            [jnp.concatenate(pair, axis=axis) for pair in zip(joined(own), joined(far))]
        )

    gates_sent = jnp.stack([gates_own, swap_y(gates_own)])
    gates_sent = gates_sent.reshape(2, tok_rows, groups, local_count).transpose(2, 0, 3, 1)
    gates_sent = lax.all_to_all(gates_sent, "expert", split_axis=0, concat_axis=0)
    gate_w = doubled(gate_own, gate_far, 1)
    cot_near, *up_far = together(cot_near, *up_far)
    up_w = doubled(up_own, up_far, 1)
    held = together(
        rows_own, mlp_near, cot_near, gate_w, up_w, gates_sent, *down_far, down_own[-1]
    )
    rows_own, mlp_near, cot_near, gate_w, up_w, gates_sent = held[:6]
    down_far, down_own = list(held[6:-1]), [*down_own[:-1], held[-1]]
    gates_all = gates_sent.transpose(1, 2, 0, 3).reshape(2, local_count, seq_len, 1)
    down_far.append(swap_x(down_own[-1]))
    rows_near = lax.all_gather(mlp_near, "expert", axis=0, tiled=True)

    def into(rows_in, weight):
        return jnp.einsum("td,edf->etf", rows_in, weight, preferred_element_type=wide)

    own_up_pre = into(rows_own, up_w)
    own_up_pre, *down_far = together(own_up_pre, *down_far)
    down_w = doubled(down_own, down_far, 0)
    part_own = expert_block(
        into(rows_own, gate_w), own_up_pre, cot_all, gates_all[0], gate_w, up_w, down_w
    )
    rows_near, *part_own = together(rows_near, *part_own)
    part_near = expert_block(
        into(rows_near, gate_w),
        into(rows_near, up_w),
        cot_near,
        gates_all[1],
        gate_w,
        up_w,
        down_w,
    )

    grad_in_own = lax.psum_scatter(part_own[0], "expert", scatter_dimension=0, tiled=True)

    def mix(scaled):
        return jnp.einsum("etf,efd->td", scaled, down_w, preferred_element_type=wide).astype(low)

    tall_sources = [(part_own[i], part_near[i]) for i in (3, 4)]
    rows_pair = (rows_own, rows_near)
    far = list(weight_grads(rows_pair, tall_sources, 1, True))
    far[0] = swap_x(far[0])
    held = together(
        part_near[0],
        grad_in_own,
        part_own[1],
        part_near[1],
        part_own[2],
        part_near[2],
        cot_near,
        *far,
    )
    near_in, grad_in_own, part_gates, scaled_pair = held[0], held[1], held[2:4], held[4:6]
    cot_pair, far = (cot_all, held[6]), held[7:]
    flat_sources = [tuple(scaled_pair)]
    grad_in_near = lax.psum_scatter(near_in, "expert", scatter_dimension=0, tiled=True)
    chunks = []
    for size in (1, 2, 1, 4):
        chunks.append(list(far[: size * local_count // 2]))
        far = far[size * local_count // 2 :]

    def send(number):
        chunks[number] = [swap_x(piece) for piece in chunks[number]]

    def tied(values, *numbers):
        held = together(*values, *[piece for i in numbers for piece in chunks[i]])
        place = len(values)
        for i in numbers:
            chunks[i] = list(held[place : place + len(chunks[i])])
            place += len(chunks[i])
        return held[: len(values)]

    send(1)
    far = weight_grads(cot_pair, flat_sources, 1, False)
    for size in (1, 3):
        chunks.append(list(far[: size * local_count // 2]))
        far = far[size * local_count // 2 :]
    own_mixed, near_mixed = mix(scaled_pair[0]), mix(scaled_pair[1])
    gate_grads = jnp.stack(part_gates)
    gate_grads = gate_grads.reshape(2, local_count, groups, tok_rows).transpose(2, 0, 1, 3)
    gate_grads = lax.all_to_all(gate_grads, "expert", split_axis=0, concat_axis=0)
    half_rows = seq_len // 2
    mixed_kept = lax.dynamic_slice_in_dim(near_mixed, core * half_rows, half_rows, 0)
    mixed_sent = lax.dynamic_slice_in_dim(near_mixed, (1 - core) * half_rows, half_rows, 0)
    mixed_half = (mixed_kept.astype(wide) + swap_core(mixed_sent).astype(wide)).astype(low)
    mixed_half, own_mixed, gate_grads = tied((mixed_half, own_mixed, gate_grads), 1, 4, 5)

    gate_grads = gate_grads.transpose(1, 3, 0, 2).reshape(2, tok_rows, experts)
    gate_grads = gate_grads[0] + swap_y(gate_grads[1])
    grad_in_near, gate_grads = tied((grad_in_near, gate_grads), 2)
    send(2)
    grad_mlp_in = grad_in_own.astype(wide) + swap_y(grad_in_near).astype(wide)
    grad_logits = gates_own * (gate_grads - jnp.sum(gates_own * gate_grads, axis=-1, keepdims=True))
    grad_router = jnp.einsum("te,td->ed", grad_logits, mlp_low.astype(wide), precision=PRECISE)
    grad_mlp_in = grad_mlp_in + jnp.einsum(
        "te,ed->td", grad_logits, router_t.astype(wide), precision=PRECISE
    )
    grad_out = cot.astype(wide)
    grad_hidden_norm, grad_gain_mlp = rms_back(grad_mlp_in, mlp_normal, mlp_factor, mlp_gain)
    grad_hidden = grad_out + grad_hidden_norm
    grad_attn_low, mixed_half = tied((grad_hidden.astype(low), mixed_half), 2, 3)
    grad_attn_all = lax.all_gather(grad_attn_low, "expert", axis=0, tiled=True)
    mixed_half = swap_y(mixed_half)
    send(3)

    grad_gate, grad_up = weight_grads(rows_pair, tall_sources, 0, True)
    (grad_down,) = weight_grads(cot_pair, flat_sources, 0, False)
    held = tied((grad_attn_all, mixed_half, grad_gate, grad_up, grad_down), 3, 4)
    grad_attn_all, mixed_half, grad_gate, grad_up, grad_down = held
    send(4)
    mixed = own_mixed.astype(wide)
    half_own = lax.dynamic_slice_in_dim(mixed, core * half_rows, half_rows, 0)
    mixed = lax.dynamic_update_slice_in_dim(
        own_mixed, (half_own + mixed_half.astype(wide)).astype(low), core * half_rows, 0
    )
    mixed = lax.psum_scatter(mixed, "expert", scatter_dimension=0, tiled=True)
    grad_value_low, query_scaled, key_scaled, query_inner, key_inner, *gain_grads = attend_back(
        lengths,
        grad_attn_all,
        out_w,
        attended,
        log_total,
        query_low,
        key_low,
        value_low,
        qkv,
        *norm_args,
    )
    held = tied(
        (grad_value_low, query_scaled, key_scaled, query_inner, key_inner, grad_attn_all), 4
    )
    grad_value_low, query_scaled, key_scaled, query_inner, key_inner, grad_attn_all = held
    grad_w_out = contract_rows(attended_low, grad_attn_all).reshape(2, 2, shard, model_width)
    kept = lax.dynamic_index_in_dim(grad_w_out, core, 1, keepdims=False)
    given = lax.dynamic_index_in_dim(grad_w_out, 1 - core, 1, keepdims=False)
    grad_w_out = in_order(kept.astype(low), swap_core(given.astype(low)), core)
    grad_gain_query, grad_gain_key = gain_grads[0][0], gain_grads[1][0]

    def by_parts(upstream):
        return contract_rows(attn_low, upstream).reshape(2, 2, groups * shard, -1)

    query_normal, key_normal = query_pre * query_factor, key_pre * key_factor
    inner = jnp.stack([query_inner[:, 0], key_inner[:, 0]])
    inner = sum_experts(inner)
    inner, grad_w_out = together(inner, grad_w_out)
    out_parts = scatter_first(grad_w_out)
    inner = inner / model_width
    grad_query_low = (query_factor * (query_scaled - query_normal * inner[0][:, None])).astype(low)
    grad_key_low = (key_factor * (key_scaled - key_normal * inner[1][:, None])).astype(low)
    grad_qkv = jnp.concatenate([grad_query_low, grad_key_low, grad_value_low], axis=1)
    qkv_w_grad = by_parts(grad_qkv)
    grad_qkv, qkv_w_grad = together(grad_qkv, qkv_w_grad)
    qkv_parts = scatter_first(qkv_w_grad)
    grad_in_part = times_transpose(grad_qkv, qkv_w)
    count = len(qkv_parts)
    held = together(grad_in_part.astype(low), mixed, *qkv_parts, *out_parts)
    grad_in_low, mixed, qkv_parts, out_parts = held[0], held[1], held[2 : 2 + count], held[2 + count :]
    grad_attn_in = lax.psum_scatter(grad_in_low, "expert", scatter_dimension=0, tiled=True)
    grad_attn_in = grad_attn_in.astype(wide)
    grad_gain_attn = jnp.sum(grad_in_part * attn_normal, axis=0)
    _, own_normal, own_factor = rms_parts(tok.astype(wide), attn_gain)
    grad_attn_x, _ = rms_back(grad_attn_in, own_normal, own_factor, attn_gain)
    grad_tokens = (grad_hidden + grad_attn_x).astype(low)

    small = jnp.concatenate(
        [
            grad_router,
            grad_gain_attn[None],
            spread_heads(grad_gain_query)[None],
            spread_heads(grad_gain_key)[None],
            grad_gain_mlp[None],
        ],
        axis=0,
    )
    small = small.reshape(pack_rows, devices, shard).transpose(1, 0, 2).reshape(devices, -1, 128)
    held = tied((*scatter_ready(*qkv_parts), *scatter_ready(*out_parts), small), 5)
    send(5)
    qkv_parts, out_parts, small = held[:5], held[5:10], held[10]
    small = lax.all_to_all(small, everyone, split_axis=0, concat_axis=0)
    small = jnp.sum(small, axis=0).reshape(pack_rows, shard)
    grad_w_qkv = scatter_last(*qkv_parts).astype(low)
    grad_w_out = scatter_last(*out_parts)
    small, grad_w_qkv, grad_w_out, grad_gate, grad_up = together(
        small, grad_w_qkv, grad_w_out, grad_gate, grad_up
    )
    pieces = [piece for chunk in chunks for piece in chunk]
    part = 2 * local_count
    grad_gate = add_pieces(grad_gate, pieces[:part], 1)
    grad_up = add_pieces(grad_up, pieces[part : 2 * part], 1)
    grad_w_qkv = grad_w_qkv.reshape(groups, shard, 3 * own_width)
    grad_w_qkv = lax.all_to_all(grad_w_qkv, "expert", split_axis=0, concat_axis=0)
    grad_w_qkv, grad_gate, grad_up, grad_tokens = together(
        grad_w_qkv, grad_gate, grad_up, grad_tokens
    )
    grad_w_qkv = grad_w_qkv.reshape(chips, 2, shard, 3, 2, HEAD_DIM).astype(wide)
    grad_w_qkv = grad_w_qkv.transpose(3, 2, 1, 4, 0, 5).reshape(3, shard, model_width)
    grad_down, grad_w_qkv, grad_tokens = together(grad_down, grad_w_qkv, grad_tokens)
    grad_down = add_pieces(grad_down, pieces[2 * part :], 0)

    output = (hidden + mixed.astype(wide)).astype(low)
    return (
        output[None],
        grad_tokens[None],
        grad_w_qkv[0],
        grad_w_qkv[1],
        grad_w_qkv[2],
        grad_w_out,
        small[:experts].T,
        small[experts],
        small[experts + 1],
        small[experts + 2],
        small[experts + 3],
        grad_gate,
        grad_up,
        grad_down,
    )


def specs(dp):
    both = (dp, "expert") if isinstance(dp, str) else dp + ("expert",)
    rows, weight, vector = P(dp, "expert", None), P(both, None), P(both)
    columns, depth = P("expert", None, dp), P("expert", dp, None)
    taken = (rows, rows, P(dp), rows) + (weight,) * 5 + (vector,) * 4 + (columns, columns, depth)
    given = (rows, rows) + (weight,) * 5 + (vector,) * 4 + (columns, columns, depth)
    return (taken, given)


def solution(mesh):
    parts, groups = mesh.shape["dp"], mesh.shape["expert"]

    def whole(*args):
        model_width = args[0].shape[2]
        by_heads = (
            parts == 4
            and groups % 2 == 0
            and model_width == 2 * HEAD_DIM * groups
            and 2 * model_width == parts * groups * HEAD_DIM
        )
        if by_heads:
            used = jax.sharding.Mesh(
                mesh.devices.reshape(2, 2, groups), ("dy", "dx", "expert")
            )
            taken, given = specs(("dy", "dx"))
            body = per_device_by_heads
        else:
            used = mesh
            taken, given = specs("dp")
            body = per_device
        return jax.shard_map(
            body, mesh=used, in_specs=taken, out_specs=given, check_vma=False
        )(*args)

    return whole
```

```python
import functools

import jax
import jax.numpy as jnp
from jax import lax
from jax.experimental import pallas as pl
from jax.experimental.layout import Layout, with_layout_constraint
from jax.experimental.pallas import tpu as pltpu
from jax.sharding import PartitionSpec as P

HEAD_DIM = 128
TOP = 8


PRECISE = lax.Precision.HIGHEST
EPSILON = 1e-05
ROPE_BASE = 10000.0
MASKED = -1e30


def rms_parts(values, gain):
    factor = lax.rsqrt(jnp.mean(values * values, axis=-1, keepdims=True) + EPSILON)
    normal = values * factor
    return (normal * gain, normal, factor)


def rms_back(upstream, normal, factor, gain):
    scaled = upstream * gain
    inner_mean = jnp.mean(scaled * normal, axis=-1, keepdims=True)
    return (factor * (scaled - normal * inner_mean), jnp.sum(upstream * normal, axis=0))


def rope_tables(positions):
    half_dim = HEAD_DIM // 2
    frequency = ROPE_BASE ** (-2.0 * jnp.arange(half_dim).astype(jnp.float32) / HEAD_DIM)
    angles = positions.astype(jnp.float32)[:, None] * frequency[None, :]
    return (jnp.cos(angles)[:, None, :], jnp.sin(angles)[:, None, :])


def rotate(values, cosine, sine_part, direction):
    half_dim = values.shape[-1] // 2
    front_half = values[..., :half_dim]
    behind = values[..., half_dim:]
    return jnp.concatenate(
        [
            front_half * cosine - direction * behind * sine_part,
            behind * cosine + direction * front_half * sine_part,
        ],
        axis=-1,
    )


def contract_rows(left_side, right_side):
    return lax.dot_general(
        left_side, right_side, (((0,), (0,)), ((), ())), preferred_element_type=jnp.float32
    )


def times_transpose(left_side, right_side):
    return lax.dot_general(
        left_side, right_side, (((1,), (1,)), ((), ())), preferred_element_type=jnp.float32
    )


def score_grads(
    query_heads,
    key_heads,
    value_heads,
    grad_heads,
    log_total,
    row_delta,
    query_place,
    key_place,
    length,
):
    factor = HEAD_DIM ** (-0.5)
    scores = (
        jnp.einsum("qhd,khd->hqk", query_heads, key_heads, preferred_element_type=jnp.float32)
        * factor
    )
    allowed = (key_place[None, :] <= query_place[:, None]) & (key_place[None, :] < length)
    weights_full = jnp.where(allowed[None], jnp.exp(scores - log_total[:, :, None]), 0.0)
    grad_weights = jnp.einsum(
        "qhd,khd->hqk", grad_heads, value_heads, preferred_element_type=jnp.float32
    )
    grad_scores = (weights_full * (grad_weights - row_delta[:, :, None])).astype(jnp.bfloat16)
    return (weights_full.astype(jnp.bfloat16), grad_scores)


def per_device(
    tokens,
    cotangent,
    lengths,
    routes,
    w_query,
    w_key,
    w_value,
    w_output,
    router,
    gain_attn,
    gain_query,
    gain_key,
    gain_mlp,
    w_gate,
    w_up,
    w_down,
):
    tok_rows = tokens.shape[1]
    model_width = tokens.shape[2]
    head_count = model_width // HEAD_DIM
    groups = lax.axis_size("expert")
    seq_len = tok_rows * groups
    length = lengths[0]
    factor = HEAD_DIM ** (-0.5)
    gathered = (
        lax.all_gather(w_query.astype(jnp.bfloat16), ("dp", "expert"), axis=0, tiled=True),
        lax.all_gather(w_key.astype(jnp.bfloat16), ("dp", "expert"), axis=0, tiled=True),
        lax.all_gather(w_value.astype(jnp.bfloat16), ("dp", "expert"), axis=0, tiled=True),
        lax.all_gather(w_output.astype(jnp.bfloat16), ("dp", "expert"), axis=0, tiled=True),
        lax.all_gather(router.astype(jnp.bfloat16), ("dp", "expert"), axis=0, tiled=True),
        lax.all_gather(gain_attn.astype(jnp.bfloat16), ("dp", "expert"), axis=0, tiled=True),
        lax.all_gather(gain_query.astype(jnp.bfloat16), ("dp", "expert"), axis=0, tiled=True),
        lax.all_gather(gain_key.astype(jnp.bfloat16), ("dp", "expert"), axis=0, tiled=True),
        lax.all_gather(gain_mlp.astype(jnp.bfloat16), ("dp", "expert"), axis=0, tiled=True),
    )
    query_weight, key_weight, value_weight, output_weight, router_weight = (
        gathered[0],
        gathered[1],
        gathered[2],
        gathered[3],
        gathered[4],
    )
    attn_gain = gathered[5].astype(jnp.float32)
    query_gain = gathered[6].astype(jnp.float32)
    key_gain = gathered[7].astype(jnp.float32)
    mlp_gain = gathered[8].astype(jnp.float32)
    gate_weight, up_weight, down_weight = (
        lax.all_gather(w_gate.astype(jnp.bfloat16), "dp", axis=2, tiled=True),
        lax.all_gather(w_up.astype(jnp.bfloat16), "dp", axis=2, tiled=True),
        lax.all_gather(w_down.astype(jnp.bfloat16), "dp", axis=1, tiled=True),
    )
    token_rows = tokens[0].astype(jnp.float32)
    attn_in, attn_normal, attn_factor = rms_parts(token_rows, attn_gain)
    attn_low = attn_in.astype(jnp.bfloat16)
    query_pre = jnp.dot(attn_low, query_weight, preferred_element_type=jnp.float32)
    key_pre = jnp.dot(attn_low, key_weight, preferred_element_type=jnp.float32)
    value_low = jnp.dot(attn_low, value_weight, preferred_element_type=jnp.float32).astype(
        jnp.bfloat16
    )
    query_norm, query_normal, query_factor = rms_parts(query_pre, query_gain)
    key_norm, key_normal, key_factor = rms_parts(key_pre, key_gain)
    positions = lax.axis_index("expert") * tok_rows + jnp.arange(tok_rows)
    cosine, sine_part = rope_tables(positions)
    query_low = rotate(
        query_norm.reshape(tok_rows, head_count, HEAD_DIM), cosine, sine_part, 1.0
    ).astype(jnp.bfloat16)
    key_low = (
        rotate(key_norm.reshape(tok_rows, head_count, HEAD_DIM), cosine, sine_part, 1.0)
        .astype(jnp.bfloat16)
        .reshape(tok_rows, model_width)
    )
    whole_keys, whole_values = (
        lax.all_gather(key_low, "expert", axis=0, tiled=True),
        lax.all_gather(value_low, "expert", axis=0, tiled=True),
    )
    all_keys = whole_keys.reshape(seq_len, head_count, HEAD_DIM)
    all_values = whole_values.reshape(seq_len, head_count, HEAD_DIM)
    key_place = jnp.arange(seq_len)
    allowed = (key_place[None, :] <= positions[:, None]) & (key_place[None, :] < length)
    scores = (
        jnp.einsum("qhd,khd->hqk", query_low, all_keys, preferred_element_type=jnp.float32) * factor
    )
    scores = jnp.where(allowed[None], scores, MASKED)
    log_total = jax.nn.logsumexp(scores, axis=-1)
    weights_low = jnp.where(allowed[None], jnp.exp(scores - log_total[:, :, None]), 0.0).astype(
        jnp.bfloat16
    )
    attended = jnp.einsum(
        "hqk,khd->qhd", weights_low, all_values, preferred_element_type=jnp.float32
    ).reshape(tok_rows, model_width)
    attended_low = attended.astype(jnp.bfloat16)
    hidden = token_rows + jnp.dot(attended_low, output_weight, preferred_element_type=jnp.float32)
    mlp_in, mlp_normal, mlp_factor = rms_parts(hidden, mlp_gain)
    mlp_low = mlp_in.astype(jnp.bfloat16)
    logits = jnp.dot(mlp_low, router_weight, preferred_element_type=jnp.float32)
    route_ids = routes[0]
    gate_probs = jax.nn.softmax(jnp.take_along_axis(logits, route_ids, axis=1), axis=-1)
    experts = router_weight.shape[1]
    slot_cap = 2 * tok_rows * TOP // experts
    local_count = experts // groups
    pair_count = tok_rows * TOP
    flat_routes = route_ids.reshape(-1)
    expert_ids = jnp.arange(experts)
    hit_table = (flat_routes[:, None] == expert_ids[None, :]).astype(jnp.int32)
    slot_rank = jnp.sum((jnp.cumsum(hit_table, axis=0) - hit_table) * hit_table, axis=1)
    counts = jnp.sum(hit_table, axis=0)
    slot_ids = flat_routes * slot_cap + slot_rank
    slot_pair = (
        jnp.zeros((experts * slot_cap,), jnp.int32)
        .at[slot_ids]
        .set(jnp.arange(pair_count, dtype=jnp.int32))
    )
    send_rows = mlp_low[slot_pair // TOP].reshape(groups, local_count, slot_cap, model_width)
    send_counts = counts.reshape(groups, local_count).astype(jnp.bfloat16)
    arrived_rows, arrived_counts = (
        lax.all_to_all(send_rows, "expert", split_axis=0, concat_axis=0, tiled=True),
        lax.all_to_all(send_counts, "expert", split_axis=0, concat_axis=0, tiled=True),
    )
    living = (jnp.arange(slot_cap)[None, None, :] < arrived_counts.astype(jnp.int32)[:, :, None])[
        ..., None
    ]
    gate_pre = jnp.einsum(
        "nemd,edf->nemf", arrived_rows, gate_weight, preferred_element_type=jnp.float32
    )
    up_pre = jnp.einsum(
        "nemd,edf->nemf", arrived_rows, up_weight, preferred_element_type=jnp.float32
    )
    gate_sigmoid = jax.nn.sigmoid(gate_pre)
    activity = (gate_pre * gate_sigmoid * up_pre).astype(jnp.bfloat16)
    expert_out = jnp.einsum(
        "nemf,efd->nemd", activity, down_weight, preferred_element_type=jnp.float32
    ).astype(jnp.bfloat16)
    returned = lax.all_to_all(expert_out, "expert", split_axis=0, concat_axis=0, tiled=True)
    pair_out = (
        returned.reshape(experts * slot_cap, model_width)[slot_ids]
        .reshape(tok_rows, TOP, model_width)
        .astype(jnp.float32)
    )
    output = hidden + jnp.sum(gate_probs[:, :, None] * pair_out, axis=1)
    grad_out = cotangent[0].astype(jnp.float32)
    grad_gates = jnp.sum(grad_out[:, None, :] * pair_out, axis=-1)
    pair_grad = (
        (gate_probs[:, :, None] * grad_out[:, None, :])
        .astype(jnp.bfloat16)
        .reshape(pair_count, model_width)
    )
    send_grad = pair_grad[slot_pair].reshape(groups, local_count, slot_cap, model_width)
    arrived_grad = lax.all_to_all(send_grad, "expert", split_axis=0, concat_axis=0, tiled=True)
    arrived_grad = jnp.where(living, arrived_grad, jnp.zeros((), jnp.bfloat16))
    grad_activity = jnp.einsum(
        "nemd,efd->nemf", arrived_grad, down_weight, preferred_element_type=jnp.float32
    )
    grad_gate_pre = (
        grad_activity * up_pre * gate_sigmoid * (1.0 + gate_pre * (1.0 - gate_sigmoid))
    ).astype(jnp.bfloat16)
    grad_up_pre = (grad_activity * gate_pre * gate_sigmoid).astype(jnp.bfloat16)
    grad_down = jnp.einsum(
        "nemf,nemd->efd", activity, arrived_grad, preferred_element_type=jnp.float32
    )
    grad_gate = jnp.einsum(
        "nemd,nemf->edf", arrived_rows, grad_gate_pre, preferred_element_type=jnp.float32
    )
    grad_up = jnp.einsum(
        "nemd,nemf->edf", arrived_rows, grad_up_pre, preferred_element_type=jnp.float32
    )
    input_grad = (
        jnp.einsum("nemf,edf->nemd", grad_gate_pre, gate_weight, preferred_element_type=jnp.float32)
        + jnp.einsum("nemf,edf->nemd", grad_up_pre, up_weight, preferred_element_type=jnp.float32)
    ).astype(jnp.bfloat16)
    sent_back = lax.all_to_all(input_grad, "expert", split_axis=0, concat_axis=0, tiled=True)
    grad_mlp_in = jnp.sum(
        sent_back.reshape(experts * slot_cap, model_width)[slot_ids]
        .reshape(tok_rows, TOP, model_width)
        .astype(jnp.float32),
        axis=1,
    )
    grad_chosen = gate_probs * (
        grad_gates - jnp.sum(gate_probs * grad_gates, axis=-1, keepdims=True)
    )
    route_table = (route_ids[:, :, None] == expert_ids[None, None, :]).astype(jnp.float32)
    grad_logits = jnp.sum(grad_chosen[:, :, None] * route_table, axis=1)
    grad_router = jnp.einsum(
        "td,te->de", mlp_low.astype(jnp.float32), grad_logits, precision=PRECISE
    )
    grad_mlp_in = grad_mlp_in + jnp.einsum(
        "te,de->td", grad_logits, router_weight.astype(jnp.float32), precision=PRECISE
    )
    grad_hidden_norm, grad_gain_mlp = rms_back(grad_mlp_in, mlp_normal, mlp_factor, mlp_gain)
    grad_hidden = grad_out + grad_hidden_norm
    grad_attn_low = grad_hidden.astype(jnp.bfloat16)
    grad_w_out = contract_rows(attended_low, grad_attn_low)
    grad_attended = times_transpose(grad_attn_low, output_weight).astype(jnp.bfloat16)
    row_delta = jnp.sum(
        (grad_attended.astype(jnp.float32) * attended).reshape(tok_rows, head_count, HEAD_DIM),
        axis=-1,
    ).T
    grad_heads = grad_attended.reshape(tok_rows, head_count, HEAD_DIM)
    block_rows = min(512, seq_len)
    block_total = seq_len // block_rows

    def key_part(number):
        offset = number * block_rows
        block_keys = lax.dynamic_slice_in_dim(all_keys, offset, block_rows, 0)
        block_values = lax.dynamic_slice_in_dim(all_values, offset, block_rows, 0)
        weights_part, grad_scores = score_grads(
            query_low,
            block_keys,
            block_values,
            grad_heads,
            log_total,
            row_delta,
            positions,
            offset + jnp.arange(block_rows),
            length,
        )
        grad_query_part = (
            jnp.einsum("hqk,khd->qhd", grad_scores, block_keys, preferred_element_type=jnp.float32)
            * factor
        )
        grad_key_part = (
            jnp.einsum("hqk,qhd->khd", grad_scores, query_low, preferred_element_type=jnp.float32)
            * factor
        )
        grad_value_part = jnp.einsum(
            "hqk,qhd->khd", weights_part, grad_heads, preferred_element_type=jnp.float32
        )
        return (
            grad_query_part,
            grad_key_part.reshape(block_rows, model_width),
            grad_value_part.reshape(block_rows, model_width),
        )

    query_parts, key_parts, value_parts = lax.map(
        lambda number: key_part(number), jnp.arange(block_total)
    )
    grad_query = jnp.sum(query_parts, axis=0).reshape(tok_rows, model_width)
    grad_key, grad_value = (
        lax.psum_scatter(
            key_parts.reshape(seq_len, model_width).astype(jnp.bfloat16),
            "expert",
            scatter_dimension=0,
            tiled=True,
        ).astype(jnp.float32),
        lax.psum_scatter(
            value_parts.reshape(seq_len, model_width).astype(jnp.bfloat16),
            "expert",
            scatter_dimension=0,
            tiled=True,
        ).astype(jnp.float32),
    )
    grad_value_low = grad_value.astype(jnp.bfloat16)
    grad_query_rot = (
        grad_query.astype(jnp.bfloat16).astype(jnp.float32).reshape(tok_rows, head_count, HEAD_DIM)
    )
    grad_key_rot = (
        grad_key.astype(jnp.bfloat16).astype(jnp.float32).reshape(tok_rows, head_count, HEAD_DIM)
    )
    grad_query_norm = rotate(grad_query_rot, cosine, sine_part, -1.0).reshape(tok_rows, model_width)
    grad_key_norm = rotate(grad_key_rot, cosine, sine_part, -1.0).reshape(tok_rows, model_width)
    grad_query_pre, grad_gain_query = rms_back(
        grad_query_norm, query_normal, query_factor, query_gain
    )
    grad_key_pre, grad_gain_key = rms_back(grad_key_norm, key_normal, key_factor, key_gain)
    grad_query_low = grad_query_pre.astype(jnp.bfloat16)
    grad_key_low = grad_key_pre.astype(jnp.bfloat16)
    grad_wq = contract_rows(attn_low, grad_query_low)
    grad_wk = contract_rows(attn_low, grad_key_low)
    grad_wv = contract_rows(attn_low, grad_value_low)
    grad_attn_in = (
        times_transpose(grad_query_low, query_weight)
        + times_transpose(grad_key_low, key_weight)
        + times_transpose(grad_value_low, value_weight)
    )
    grad_attn_x, grad_gain_attn = rms_back(grad_attn_in, attn_normal, attn_factor, attn_gain)
    grad_tokens = (grad_hidden + grad_attn_x).astype(jnp.bfloat16)
    summed_grads = (
        lax.psum_scatter(grad_wq, ("dp", "expert"), scatter_dimension=0, tiled=True),
        lax.psum_scatter(grad_wk, ("dp", "expert"), scatter_dimension=0, tiled=True),
        lax.psum_scatter(grad_wv, ("dp", "expert"), scatter_dimension=0, tiled=True),
        lax.psum_scatter(grad_w_out, ("dp", "expert"), scatter_dimension=0, tiled=True),
        lax.psum_scatter(grad_router, ("dp", "expert"), scatter_dimension=0, tiled=True),
        lax.psum_scatter(grad_gain_attn, ("dp", "expert"), scatter_dimension=0, tiled=True),
        lax.psum_scatter(grad_gain_query, ("dp", "expert"), scatter_dimension=0, tiled=True),
        lax.psum_scatter(grad_gain_key, ("dp", "expert"), scatter_dimension=0, tiled=True),
        lax.psum_scatter(grad_gain_mlp, ("dp", "expert"), scatter_dimension=0, tiled=True),
    )
    expert_grads = (
        lax.psum_scatter(
            grad_gate.astype(jnp.bfloat16), "dp", scatter_dimension=2, tiled=True
        ).astype(jnp.float32),
        lax.psum_scatter(
            grad_up.astype(jnp.bfloat16), "dp", scatter_dimension=2, tiled=True
        ).astype(jnp.float32),
        lax.psum_scatter(
            grad_down.astype(jnp.bfloat16), "dp", scatter_dimension=1, tiled=True
        ).astype(jnp.float32),
    )
    return (
        output.astype(jnp.bfloat16)[None],
        grad_tokens[None],
        summed_grads[0],
        summed_grads[1],
        summed_grads[2],
        summed_grads[3],
        summed_grads[4],
        summed_grads[5],
        summed_grads[6],
        summed_grads[7],
        summed_grads[8],
        expert_grads[0],
        expert_grads[1],
        expert_grads[2],
    )


FLIP = [(0, 1), (1, 0)]


def in_order(own, other, index):
    first = jnp.where(index == 0, own, other)
    second = jnp.where(index == 0, other, own)
    return jnp.stack([first, second])


def swap_x(block):
    return lax.ppermute(block, "dx", FLIP)


def swap_y(block):
    return lax.ppermute(block, "dy", FLIP)


def swap_core(block):
    groups = lax.axis_size("expert")
    return lax.ppermute(block, "expert", [(i, i ^ 1) for i in range(groups)])


def row_major(value):
    return with_layout_constraint(value, Layout(major_to_minor=tuple(range(value.ndim))))


def together(*values):
    return lax.optimization_barrier(values)


def gather_first(block):
    return (block, swap_x(block), swap_y(block))


def gather_second(block, beside, below):
    half = block.shape[0] // 2
    return (block, beside, below, swap_x(below[:half]), swap_y(beside[half:]))


def gather_last(block, beside, below, upper, under):
    column, row = lax.axis_index("dx"), lax.axis_index("dy")
    across = jnp.concatenate([upper, under], axis=0)
    return in_order(in_order(block, beside, column), in_order(below, across, column), row)


def scatter_first(blocks):
    column, row = lax.axis_index("dx"), lax.axis_index("dy")
    low = jnp.bfloat16

    def pick(at_row, at_column):
        line = lax.dynamic_index_in_dim(blocks, at_row, 0, keepdims=False)
        return lax.dynamic_index_in_dim(line, at_column, 0, keepdims=False)

    half = blocks.shape[2] // 2
    across = pick(1 - row, 1 - column).astype(low)
    beside, below = pick(row, 1 - column), pick(1 - row, column)
    return (
        pick(row, column),
        beside[:half],
        below[half:],
        beside[half:].astype(low),
        below[:half].astype(low),
        swap_y(across[:half]),
        swap_x(across[half:]),
    )


def scatter_ready(kept, beside, below, beside_rest, below_rest, far_below, far_beside):
    low, wide = jnp.bfloat16, jnp.float32
    beside = (beside + far_below.astype(wide)).astype(low)
    below = (below + far_beside.astype(wide)).astype(low)
    return (kept, beside, below, beside_rest, below_rest)


def scatter_last(kept, beside, below, beside_rest, below_rest):
    wide = jnp.float32
    added = jnp.concatenate(
        [
            swap_x(beside).astype(wide) + swap_y(below_rest).astype(wide),
            swap_x(beside_rest).astype(wide) + swap_y(below).astype(wide),
        ]
    )
    return kept + added


def sum_experts(values):
    groups = lax.axis_size("expert")
    flat = values.reshape(-1, 128)
    spread = jnp.broadcast_to(flat[None], (groups,) + flat.shape)
    arrived = lax.all_to_all(spread, "expert", split_axis=0, concat_axis=0)
    return jnp.sum(arrived, axis=0).reshape(values.shape)


def dense_gates(logits, route_ids):
    columns = jnp.arange(logits.shape[-1])
    chosen = jnp.any(route_ids[:, :, None] == columns[None, None, :], axis=1)
    highest = jnp.max(jnp.where(chosen, logits, -jnp.inf), axis=-1, keepdims=True)
    weights = jnp.where(chosen, jnp.exp(logits - highest), 0.0)
    return weights / jnp.sum(weights, axis=-1, keepdims=True)


def mul_nn(left_side, right_side):
    return jnp.dot(left_side, right_side, preferred_element_type=jnp.float32)


VMEM_BYTES = 56 * 1024 * 1024
ROWS = 256


def whole_blocks(count):
    return [pl.BlockSpec(memory_space=pltpu.VMEM)] * count


def turn(values, cosine, signed_sine):
    return values * cosine + pltpu.roll(values, HEAD_DIM // 2, 1) * signed_sine


def allowed_block(first_row, rows, columns, length):
    at_row = first_row + lax.broadcasted_iota(jnp.int32, (rows, columns), 0)
    at_column = lax.broadcasted_iota(jnp.int32, (rows, columns), 1)
    return (at_column <= at_row) & (at_column < length)


def attend_kernel(
    length_ref,
    qkv_ref,
    query_factor_ref,
    key_factor_ref,
    query_gain_ref,
    key_gain_ref,
    cosine_ref,
    sine_ref,
    out_w_ref,
    query_ref,
    key_ref,
    value_ref,
    attended_ref,
    total_ref,
    part_ref,
):
    low = jnp.bfloat16
    seq_len, heads = qkv_ref.shape[0], 2
    length = length_ref[0]
    width = heads * HEAD_DIM
    factor = HEAD_DIM ** (-0.5)

    @pl.loop(0, seq_len // ROWS)
    def _(number):
        rows = pl.ds(pl.multiple_of(number * ROWS, ROWS), ROWS)
        cosine, sine_part = cosine_ref[rows, :], sine_ref[rows, :]
        for head in range(heads):
            part = slice(head * HEAD_DIM, (head + 1) * HEAD_DIM)
            later = slice(width + head * HEAD_DIM, width + (head + 1) * HEAD_DIM)
            query = qkv_ref[rows, part] * query_factor_ref[rows, :] * query_gain_ref[:, part]
            key = qkv_ref[rows, later] * key_factor_ref[rows, :] * key_gain_ref[:, part]
            query_ref[rows, part] = turn(query, cosine, sine_part).astype(low)
            key_ref[rows, part] = turn(key, cosine, sine_part).astype(low)
        value_ref[rows, :] = qkv_ref[rows, 2 * width :].astype(low)

    for number in range(seq_len // ROWS):
        first, end = number * ROWS, (number + 1) * ROWS
        allowed = allowed_block(first, ROWS, end, length)
        done = []
        for head in range(heads):
            part = slice(head * HEAD_DIM, (head + 1) * HEAD_DIM)
            scores = times_transpose(query_ref[first:end, part], key_ref[:end, part]) * factor
            scores = jnp.where(allowed, scores, MASKED)
            highest = jnp.max(scores, axis=1, keepdims=True)
            weights = jnp.exp(scores - highest)
            total = jnp.sum(weights, axis=1, keepdims=True)
            weights = (weights * (1.0 / total)).astype(low)
            total_ref[head, first:end, :] = highest + jnp.log(total)
            attended = mul_nn(weights, value_ref[:end, part])
            attended_ref[first:end, part] = attended
            done.append(attended.astype(low))
        part_ref[first:end, :] = mul_nn(jnp.concatenate(done, axis=1), out_w_ref[...]).astype(low)


def attend(length, qkv, query_factor, key_factor, query_gain, key_gain, cosine, sine_part, out_w):
    seq_len, width, model_width = qkv.shape[0], qkv.shape[1] // 3, out_w.shape[1]
    low, wide = jnp.bfloat16, jnp.float32
    rows = jax.ShapeDtypeStruct((seq_len, width), low)
    return pl.pallas_call(
        attend_kernel,
        in_specs=[pl.BlockSpec(memory_space=pltpu.SMEM)] + whole_blocks(8),
        out_specs=whole_blocks(6),
        out_shape=[
            rows,
            rows,
            rows,
            jax.ShapeDtypeStruct((seq_len, width), wide),
            jax.ShapeDtypeStruct((2, seq_len, 1), wide),
            jax.ShapeDtypeStruct((seq_len, model_width), low),
        ],
        compiler_params=pltpu.CompilerParams(vmem_limit_bytes=VMEM_BYTES),
        cost_estimate=pl.CostEstimate(
            flops=2 * seq_len * width * (seq_len + model_width),
            bytes_accessed=14 * seq_len * width + 2 * seq_len * model_width,
            transcendentals=seq_len * seq_len,
        ),
    )(length, qkv, query_factor, key_factor, query_gain, key_gain, cosine, sine_part, out_w)


def attend_back_kernel(
    length_ref,
    upstream_ref,
    out_w_ref,
    attended_ref,
    total_ref,
    query_ref,
    key_ref,
    value_ref,
    qkv_ref,
    query_factor_ref,
    key_factor_ref,
    query_gain_ref,
    key_gain_ref,
    cosine_ref,
    sine_ref,
    grad_value_ref,
    query_scaled_ref,
    key_scaled_ref,
    query_inner_ref,
    key_inner_ref,
    query_gain_grad_ref,
    key_gain_grad_ref,
    key_sum_ref,
    value_sum_ref,
):
    low, wide = jnp.bfloat16, jnp.float32
    seq_len, heads = qkv_ref.shape[0], 2
    length = length_ref[0]
    width = heads * HEAD_DIM
    factor = HEAD_DIM ** (-0.5)
    blocks = seq_len // ROWS

    def norm_back(sums, rows, head, offset, factor_ref, gain_ref, scaled_ref, inner_ref, grad_ref, fresh):
        part = slice(head * HEAD_DIM, (head + 1) * HEAD_DIM)
        place = slice(offset + head * HEAD_DIM, offset + (head + 1) * HEAD_DIM)
        upstream = turn(sums.astype(low).astype(wide), cosine_ref[rows, :], -sine_ref[rows, :])
        normal = qkv_ref[rows, place] * factor_ref[rows, :]
        gain_part = jnp.sum(upstream * normal, axis=0, keepdims=True)
        scaled = upstream * gain_ref[:, part]
        scaled_ref[rows, part] = scaled
        inner = jnp.sum(scaled * normal, axis=1, keepdims=True)
        if head == 0:
            inner_ref[rows, :] = inner
        else:
            inner_ref[rows, :] += inner
        if fresh:
            grad_ref[:, part] = gain_part
        else:
            grad_ref[:, part] += gain_part

    for number in reversed(range(blocks)):
        first, end = number * ROWS, (number + 1) * ROWS
        allowed = allowed_block(first, ROWS, end, length)
        rows = slice(first, end)
        grads = times_transpose(upstream_ref[rows, :], out_w_ref[...]).astype(low)
        for head in range(heads):
            part = slice(head * HEAD_DIM, (head + 1) * HEAD_DIM)
            query, keys = query_ref[rows, part], key_ref[:end, part]
            grad = grads[:, part]
            delta = jnp.sum(grad.astype(wide) * attended_ref[rows, part], axis=1, keepdims=True)
            scores = times_transpose(query, keys) * factor
            weights = jnp.where(allowed, jnp.exp(scores - total_ref[head, rows, :]), 0.0)
            grad_weights = times_transpose(grad, value_ref[:end, part])
            grad_scores = (weights * (grad_weights - delta)).astype(low)
            query_sum = mul_nn(grad_scores, keys) * factor
            key_sum = contract_rows(grad_scores, query)
            value_sum = contract_rows(weights.astype(low), grad)
            if number == blocks - 1:
                key_sum_ref[:, part] = key_sum
                value_sum_ref[:, part] = value_sum
            else:
                key_sum_ref[:end, part] += key_sum
                value_sum_ref[:end, part] += value_sum
            norm_back(
                query_sum,
                rows,
                head,
                0,
                query_factor_ref,
                query_gain_ref,
                query_scaled_ref,
                query_inner_ref,
                query_gain_grad_ref,
                number == blocks - 1,
            )
    for number in range(blocks):
        rows = slice(number * ROWS, (number + 1) * ROWS)
        grad_value_ref[rows, :] = value_sum_ref[rows, :].astype(low)
        for head in range(heads):
            part = slice(head * HEAD_DIM, (head + 1) * HEAD_DIM)
            norm_back(
                key_sum_ref[rows, part] * factor,
                rows,
                head,
                width,
                key_factor_ref,
                key_gain_ref,
                key_scaled_ref,
                key_inner_ref,
                key_gain_grad_ref,
                number == 0,
            )


def attend_back(length, upstream, out_w, attended, total, query, key, value, qkv, *rest):
    seq_len, width = attended.shape
    low, wide = jnp.bfloat16, jnp.float32
    shape = jax.ShapeDtypeStruct
    return pl.pallas_call(
        attend_back_kernel,
        in_specs=[pl.BlockSpec(memory_space=pltpu.SMEM)] + whole_blocks(14),
        out_specs=whole_blocks(7),
        out_shape=[
            shape((seq_len, width), low),
            shape((seq_len, width), wide),
            shape((seq_len, width), wide),
            shape((seq_len, 1), wide),
            shape((seq_len, 1), wide),
            shape((1, width), wide),
            shape((1, width), wide),
        ],
        scratch_shapes=[pltpu.VMEM((seq_len, width), wide), pltpu.VMEM((seq_len, width), wide)],
        compiler_params=pltpu.CompilerParams(vmem_limit_bytes=VMEM_BYTES),
        cost_estimate=pl.CostEstimate(
            flops=2 * seq_len * width * (3 * seq_len + upstream.shape[1]),
            bytes_accessed=30 * seq_len * width + 2 * upstream.size,
            transcendentals=seq_len * seq_len,
        ),
    )(length, upstream, out_w, attended, total, query, key, value, qkv, *rest)


def put_halves(outs, place, expert, axis, value):
    if len(outs[0].shape) == 3:
        outs[expert[0]][expert[1]] = value
        return
    length = value.shape[axis] // 2
    for half in range(2):
        span = slice(half * length, (half + 1) * length)
        at = (span, slice(None)) if axis == 0 else (slice(None), span)
        outs[2 * place + half][...] = value[at].astype(jnp.bfloat16)


def tall_kernel(count, *refs):
    outs = refs[2 + 4 * count :]
    first, second = refs[0][...].T, refs[1][...].T
    for kind in range(2):
        for expert in range(count):
            place = count * kind + expert
            one, two = refs[2 + 2 * place], refs[3 + 2 * place]
            value = mul_nn(first, one[...]) + mul_nn(second, two[...])
            put_halves(outs, place, (kind, expert), 1, value)


def flat_kernel(count, *refs):
    outs = refs[2 + 2 * count : -1]
    turned_ref = refs[-1]
    length, block = refs[2].shape

    @pl.when(pl.program_id(0) == 0)
    def _():
        for expert in range(count):
            for half in range(2):
                turned_ref[
                    expert * block : (expert + 1) * block, half * length : (half + 1) * length
                ] = refs[2 + 2 * expert + half][...].T

    for expert in range(count):
        span = slice(expert * block, (expert + 1) * block)
        value = mul_nn(turned_ref[span, :length], refs[0][...]) + mul_nn(
            turned_ref[span, length:], refs[1][...]
        )
        put_halves(outs, expert, (0, expert), 0, value)


def weight_grads(rows, sources, which, tall):
    length, model_width = rows[0].shape
    count, _, doubled = sources[0][0].shape
    block = doubled // 2
    tile = min(256, model_width)
    columns = pl.BlockSpec((length, tile), lambda i: (0, i))
    operands, in_specs = list(rows), [columns] * 2
    for pair in sources:
        for expert in range(count):
            operands += list(pair)
            in_specs += [
                pl.BlockSpec(
                    (None, length, block),
                    lambda i, expert=expert: (expert, 0, which),
                    pipeline_mode=pl.Buffered(1),
                )
            ] * 2
    kinds = len(sources)
    if which == 0:
        number, dtype = kinds, jnp.float32
        if tall:
            spec, shape = pl.BlockSpec((count, tile, block), lambda i: (0, i, 0)), (model_width, block)
        else:
            spec, shape = pl.BlockSpec((count, block, tile), lambda i: (0, 0, i)), (block, model_width)
        shape = (count,) + shape
    else:
        number, dtype = 2 * count * kinds, jnp.bfloat16
        if tall:
            spec, shape = pl.BlockSpec((tile, block // 2), lambda i: (i, 0)), (model_width, block // 2)
        else:
            spec, shape = pl.BlockSpec((block // 2, tile), lambda i: (0, i)), (block // 2, model_width)
    scratch = [] if tall else [pltpu.VMEM((count * block, 2 * length), jnp.bfloat16)]
    return pl.pallas_call(
        functools.partial(tall_kernel if tall else flat_kernel, count),
        grid=(model_width // tile,),
        in_specs=in_specs,
        out_specs=[spec] * number,
        out_shape=[jax.ShapeDtypeStruct(shape, dtype)] * number,
        scratch_shapes=scratch,
        compiler_params=pltpu.CompilerParams(vmem_limit_bytes=VMEM_BYTES),
        cost_estimate=pl.CostEstimate(
            flops=4 * length * model_width * count * block * kinds,
            bytes_accessed=4 * length * model_width + 6 * count * model_width * block * kinds,
            transcendentals=0,
        ),
    )(*operands)


def add_kernel(axis, own_ref, *refs):
    out_ref = refs[-1]
    for expert in range(out_ref.shape[0]):
        pair = [ref[...].astype(jnp.float32) for ref in refs[2 * expert : 2 * expert + 2]]
        out_ref[expert] = own_ref[expert] + jnp.concatenate(pair, axis=axis)


def add_pieces(own, pieces, axis):
    count, rows, columns = own.shape
    tile = min(512, rows if axis else columns)
    if axis:
        full = pl.BlockSpec((count, tile, columns), lambda i: (0, i, 0))
        piece = pl.BlockSpec((tile, columns // 2), lambda i: (i, 0))
    else:
        full = pl.BlockSpec((count, rows, tile), lambda i: (0, 0, i))
        piece = pl.BlockSpec((rows // 2, tile), lambda i: (0, i))
    return pl.pallas_call(
        functools.partial(add_kernel, axis),
        grid=((rows if axis else columns) // tile,),
        in_specs=[full] + [piece] * len(pieces),
        out_specs=full,
        out_shape=jax.ShapeDtypeStruct(own.shape, own.dtype),
        input_output_aliases={0: 0},
        compiler_params=pltpu.CompilerParams(vmem_limit_bytes=VMEM_BYTES),
        cost_estimate=pl.CostEstimate(
            flops=own.size, bytes_accessed=10 * own.size, transcendentals=0
        ),
    )(own, *pieces)


def expert_block(gate_pre, up_pre, grad_rows, gates, gate_w, up_w, down_w):
    wide = jnp.float32
    back = jnp.einsum("td,efd->etf", grad_rows, down_w, preferred_element_type=wide)
    sigmoid = jax.nn.sigmoid(gate_pre)
    silu = gate_pre * sigmoid
    activity = silu * up_pre
    gate_grads = jnp.sum(activity * back, axis=-1)
    weight = gates
    scaled = (activity * weight).astype(jnp.bfloat16)
    back = back * weight
    grad_gate_pre = (back * up_pre * sigmoid * (1.0 + gate_pre * (1.0 - sigmoid))).astype(
        jnp.bfloat16
    )
    grad_up_pre = (back * silu).astype(jnp.bfloat16)
    grad_in = (
        jnp.einsum("etf,edf->td", grad_gate_pre, gate_w, preferred_element_type=wide)
        + jnp.einsum("etf,edf->td", grad_up_pre, up_w, preferred_element_type=wide)
    ).astype(jnp.bfloat16)
    return (grad_in, gate_grads, scaled, grad_gate_pre, grad_up_pre)


def per_device_by_heads(
    tokens,
    cotangent,
    lengths,
    routes,
    w_query,
    w_key,
    w_value,
    w_output,
    router,
    gain_attn,
    gain_query,
    gain_key,
    gain_mlp,
    w_gate,
    w_up,
    w_down,
):
    low, wide = jnp.bfloat16, jnp.float32
    everyone = ("dy", "dx", "expert")
    tok_rows, model_width = tokens.shape[1], tokens.shape[2]
    groups = lax.axis_size("expert")
    devices = 4 * groups
    chips = groups // 2
    seq_len = tok_rows * groups
    shard = w_query.shape[0]
    experts = router.shape[1]
    local_count = experts // groups
    group = lax.axis_index("expert")
    chip, core = group // 2, group % 2
    column, row = lax.axis_index("dx"), lax.axis_index("dy")
    length = lengths[0]
    factor = HEAD_DIM ** (-0.5)
    own_width = 2 * HEAD_DIM
    tok, cot = tokens[0], cotangent[0]

    def own_heads(vector):
        blocks = vector.reshape(2, 2, chips, HEAD_DIM)
        blocks = lax.dynamic_index_in_dim(blocks, core, 0, keepdims=False)
        return lax.dynamic_index_in_dim(blocks, chip, 1, keepdims=False).reshape(own_width)

    def spread_heads(vector):
        at_core = (jnp.arange(2) == core)[:, None, None, None]
        at_chip = (jnp.arange(chips) == chip)[None, None, :, None]
        return jnp.where(
            at_core & at_chip, vector.reshape(1, 2, 1, HEAD_DIM), 0.0
        ).reshape(model_width)

    def by_heads(weight):
        blocks = weight.astype(low).reshape(shard, 2, 2, chips, HEAD_DIM)
        return blocks.transpose(3, 1, 0, 2, 4).reshape(groups, shard, own_width)

    sent = jnp.concatenate([by_heads(w_query), by_heads(w_key), by_heads(w_value)], axis=2)
    packed = jnp.concatenate(
        [router.T, gain_attn[None], gain_query[None], gain_key[None], gain_mlp[None]], axis=0
    ).astype(low)
    pack_rows = experts + 4
    packed = packed.reshape(-1, 128)
    numbers = range(local_count)

    def experts_low(weight):
        pieces = [weight[0]]
        for i in numbers[1:]:
            pieces += jnp.split(weight[i], 2)
        return [row_major(piece.astype(low)) for piece in pieces]

    def joined(pieces):
        return [pieces[0]] + [
            jnp.concatenate(pieces[i : i + 2]) for i in range(1, len(pieces), 2)
        ]

    many = 2 * local_count - 1

    cosine, sine_part = rope_tables(jnp.arange(seq_len))
    cosine = jnp.concatenate([cosine[:, 0], cosine[:, 0]], axis=1)
    sine_part = jnp.concatenate([-sine_part[:, 0], sine_part[:, 0]], axis=1)
    sent, packed, out_rows, *gate_own = together(
        sent, packed, w_output.astype(low), *experts_low(w_gate)
    )
    up_own, down_own = experts_low(w_up), experts_low(w_down)
    out_rows, *held = together(out_rows, *up_own, *down_own)
    up_own, down_own = held[:many], held[many:]
    arrived = lax.all_to_all(sent, "expert", split_axis=0, concat_axis=0)
    gate_far = [swap_x(piece) for piece in gate_own[:-1]]
    held = together(
        arrived,
        packed,
        cot,
        cosine,
        sine_part,
        *gather_first(out_rows),
        *gate_far,
        gate_own[-1],
        *up_own,
        *down_own,
    )
    arrived, packed, cot, cosine, sine_part = held[:5]
    out_parts, held = held[5:8], held[8:]
    gate_far, gate_last, held = list(held[: many - 1]), held[many - 1], held[many:]
    up_own, down_own = held[:many], held[many:]
    packed = lax.all_to_all(
        jnp.broadcast_to(packed[None], (devices,) + packed.shape),
        everyone,
        split_axis=0,
        concat_axis=0,
    )
    qkv_parts = gather_first(arrived.reshape(groups * shard, 3 * own_width))
    held = together(packed, *qkv_parts, *gather_second(*out_parts))
    packed, qkv_parts, out_parts = held[0], held[1:4], held[4:]
    packed = (
        packed.reshape(devices, pack_rows, shard).transpose(1, 0, 2).reshape(pack_rows, model_width)
    )
    router_t = packed[:experts]
    attn_gain, query_gain, key_gain, mlp_gain = (
        packed[experts + i].astype(wide) for i in range(4)
    )
    tok_all = lax.all_gather(tok, "expert", axis=0, tiled=True)
    attn_in, attn_normal, _ = rms_parts(tok_all.astype(wide), attn_gain)
    held = together(attn_in.astype(low), *gather_second(*qkv_parts))
    attn_low, qkv_parts = held[0], held[1:]
    qkv_w = gather_last(*qkv_parts).reshape(model_width, 3 * own_width)

    cot_all = lax.all_gather(cot, "expert", axis=0, tiled=True)
    cot_half = lax.dynamic_slice_in_dim(cot_all, core * (seq_len // 2), seq_len // 2, 0)
    cot_half = swap_y(cot_half)

    qkv = jnp.dot(attn_low, qkv_w, preferred_element_type=wide)
    qkv, gate_last, *out_parts = together(qkv, gate_last, *out_parts)
    gate_far.append(swap_x(gate_last))
    out_quad = gather_last(*out_parts)
    out_first = lax.dynamic_index_in_dim(out_quad, core, 0, keepdims=False)
    out_other = swap_core(lax.dynamic_index_in_dim(out_quad, 1 - core, 0, keepdims=False))
    out_w = jnp.moveaxis(in_order(out_first, out_other, core), 0, 1)
    out_w = out_w.reshape(own_width, model_width)
    query_pre, key_pre = qkv[:, :own_width], qkv[:, own_width : 2 * own_width]
    squares = jnp.stack([jnp.sum(query_pre * query_pre, axis=1), jnp.sum(key_pre * key_pre, axis=1)])
    squares = sum_experts(squares)
    factors = lax.rsqrt(squares / model_width + EPSILON)
    query_factor, key_factor = factors[0][:, None], factors[1][:, None]
    query_gain_own, key_gain_own = own_heads(query_gain), own_heads(key_gain)
    norm_args = (
        query_factor,
        key_factor,
        query_gain_own[None],
        key_gain_own[None],
        cosine,
        sine_part,
    )
    query_low, key_low, value_low, attended, log_total, attn_part = attend(
        lengths, qkv, *norm_args, out_w
    )
    attended_low = attended.astype(low)
    held = together(attn_part, cot_all, *gate_far, *up_own, *down_own)
    attn_part, cot_all, gate_far, held = held[0], held[1], held[2 : 2 + many], held[2 + many :]
    up_own, down_own = held[:many], held[many:]
    attn_out = lax.psum_scatter(attn_part, "expert", scatter_dimension=0, tiled=True)
    up_far = [swap_x(piece) for piece in up_own]
    held = together(attn_out, cot_half, *up_far, *down_own)
    attn_out, cot_half, up_far, down_own = held[0], held[1], held[2 : 2 + many], held[2 + many :]
    down_far = [swap_x(piece) for piece in down_own[:-1]]
    cot_near = in_order(cot_half, swap_core(cot_half), core).reshape(seq_len, model_width)
    hidden = tok.astype(wide) + attn_out.astype(wide)
    mlp_in, mlp_normal, mlp_factor = rms_parts(hidden, mlp_gain)
    mlp_low = mlp_in.astype(low)
    gates_own = dense_gates(times_transpose(mlp_low, router_t), routes[0])

    rows_own = lax.all_gather(mlp_low, "expert", axis=0, tiled=True)
    mlp_near = swap_y(mlp_low)

    def doubled(own, far, axis):
        return jnp.stack(
            [jnp.concatenate(pair, axis=axis) for pair in zip(joined(own), joined(far))]
        )

    gates_sent = jnp.stack([gates_own, swap_y(gates_own)])
    gates_sent = gates_sent.reshape(2, tok_rows, groups, local_count).transpose(2, 0, 3, 1)
    gates_sent = lax.all_to_all(gates_sent, "expert", split_axis=0, concat_axis=0)
    gate_w = doubled(gate_own, gate_far, 1)
    cot_near, *up_far = together(cot_near, *up_far)
    up_w = doubled(up_own, up_far, 1)
    held = together(
        rows_own, mlp_near, cot_near, gate_w, up_w, gates_sent, *down_far, down_own[-1]
    )
    rows_own, mlp_near, cot_near, gate_w, up_w, gates_sent = held[:6]
    down_far, down_own = list(held[6:-1]), [*down_own[:-1], held[-1]]
    gates_all = gates_sent.transpose(1, 2, 0, 3).reshape(2, local_count, seq_len, 1)
    down_far.append(swap_x(down_own[-1]))
    rows_near = lax.all_gather(mlp_near, "expert", axis=0, tiled=True)

    def into(rows_in, weight):
        return jnp.einsum("td,edf->etf", rows_in, weight, preferred_element_type=wide)

    own_up_pre = into(rows_own, up_w)
    own_up_pre, *down_far = together(own_up_pre, *down_far)
    down_w = doubled(down_own, down_far, 0)
    part_own = expert_block(
        into(rows_own, gate_w), own_up_pre, cot_all, gates_all[0], gate_w, up_w, down_w
    )
    rows_near, *part_own = together(rows_near, *part_own)
    part_near = expert_block(
        into(rows_near, gate_w),
        into(rows_near, up_w),
        cot_near,
        gates_all[1],
        gate_w,
        up_w,
        down_w,
    )

    grad_in_own = lax.psum_scatter(part_own[0], "expert", scatter_dimension=0, tiled=True)

    def mix(scaled):
        return jnp.einsum("etf,efd->td", scaled, down_w, preferred_element_type=wide).astype(low)

    tall_sources = [(part_own[i], part_near[i]) for i in (3, 4)]
    rows_pair = (rows_own, rows_near)
    far = list(weight_grads(rows_pair, tall_sources, 1, True))
    far[0] = swap_x(far[0])
    held = together(
        part_near[0],
        grad_in_own,
        part_own[1],
        part_near[1],
        part_own[2],
        part_near[2],
        cot_near,
        *far,
    )
    near_in, grad_in_own, part_gates, scaled_pair = held[0], held[1], held[2:4], held[4:6]
    cot_pair, far = (cot_all, held[6]), held[7:]
    flat_sources = [tuple(scaled_pair)]
    grad_in_near = lax.psum_scatter(near_in, "expert", scatter_dimension=0, tiled=True)
    chunks = []
    for size in (1, 2, 1, 4):
        chunks.append(list(far[: size * local_count // 2]))
        far = far[size * local_count // 2 :]

    def send(number):
        chunks[number] = [swap_x(piece) for piece in chunks[number]]

    def tied(values, *numbers):
        held = together(*values, *[piece for i in numbers for piece in chunks[i]])
        place = len(values)
        for i in numbers:
            chunks[i] = list(held[place : place + len(chunks[i])])
            place += len(chunks[i])
        return held[: len(values)]

    send(1)
    far = weight_grads(cot_pair, flat_sources, 1, False)
    for size in (1, 3):
        chunks.append(list(far[: size * local_count // 2]))
        far = far[size * local_count // 2 :]
    own_mixed, near_mixed = mix(scaled_pair[0]), mix(scaled_pair[1])
    gate_grads = jnp.stack(part_gates)
    gate_grads = gate_grads.reshape(2, local_count, groups, tok_rows).transpose(2, 0, 1, 3)
    gate_grads = lax.all_to_all(gate_grads, "expert", split_axis=0, concat_axis=0)
    half_rows = seq_len // 2
    mixed_kept = lax.dynamic_slice_in_dim(near_mixed, core * half_rows, half_rows, 0)
    mixed_sent = lax.dynamic_slice_in_dim(near_mixed, (1 - core) * half_rows, half_rows, 0)
    mixed_half = (mixed_kept.astype(wide) + swap_core(mixed_sent).astype(wide)).astype(low)
    mixed_half, own_mixed, gate_grads = tied((mixed_half, own_mixed, gate_grads), 1, 4, 5)

    gate_grads = gate_grads.transpose(1, 3, 0, 2).reshape(2, tok_rows, experts)
    gate_grads = gate_grads[0] + swap_y(gate_grads[1])
    grad_in_near, gate_grads = tied((grad_in_near, gate_grads), 2)
    send(2)
    grad_mlp_in = grad_in_own.astype(wide) + swap_y(grad_in_near).astype(wide)
    grad_logits = gates_own * (gate_grads - jnp.sum(gates_own * gate_grads, axis=-1, keepdims=True))
    grad_router = jnp.einsum("te,td->ed", grad_logits, mlp_low.astype(wide), precision=PRECISE)
    grad_mlp_in = grad_mlp_in + jnp.einsum(
        "te,ed->td", grad_logits, router_t.astype(wide), precision=PRECISE
    )
    grad_out = cot.astype(wide)
    grad_hidden_norm, grad_gain_mlp = rms_back(grad_mlp_in, mlp_normal, mlp_factor, mlp_gain)
    grad_hidden = grad_out + grad_hidden_norm
    grad_attn_low, mixed_half = tied((grad_hidden.astype(low), mixed_half), 2, 3)
    grad_attn_all = lax.all_gather(grad_attn_low, "expert", axis=0, tiled=True)
    mixed_half = swap_y(mixed_half)
    send(3)

    grad_gate, grad_up = weight_grads(rows_pair, tall_sources, 0, True)
    (grad_down,) = weight_grads(cot_pair, flat_sources, 0, False)
    held = tied((grad_attn_all, mixed_half, grad_gate, grad_up, grad_down), 3, 4)
    grad_attn_all, mixed_half, grad_gate, grad_up, grad_down = held
    send(4)
    mixed = own_mixed.astype(wide)
    half_own = lax.dynamic_slice_in_dim(mixed, core * half_rows, half_rows, 0)
    mixed = lax.dynamic_update_slice_in_dim(
        own_mixed, (half_own + mixed_half.astype(wide)).astype(low), core * half_rows, 0
    )
    mixed = lax.psum_scatter(mixed, "expert", scatter_dimension=0, tiled=True)
    grad_value_low, query_scaled, key_scaled, query_inner, key_inner, *gain_grads = attend_back(
        lengths,
        grad_attn_all,
        out_w,
        attended,
        log_total,
        query_low,
        key_low,
        value_low,
        qkv,
        *norm_args,
    )
    held = tied(
        (grad_value_low, query_scaled, key_scaled, query_inner, key_inner, grad_attn_all), 4
    )
    grad_value_low, query_scaled, key_scaled, query_inner, key_inner, grad_attn_all = held
    grad_w_out = contract_rows(attended_low, grad_attn_all).reshape(2, 2, shard, model_width)
    kept = lax.dynamic_index_in_dim(grad_w_out, core, 1, keepdims=False)
    given = lax.dynamic_index_in_dim(grad_w_out, 1 - core, 1, keepdims=False)
    grad_w_out = in_order(kept.astype(low), swap_core(given.astype(low)), core)
    grad_gain_query, grad_gain_key = gain_grads[0][0], gain_grads[1][0]

    def by_parts(upstream):
        return contract_rows(attn_low, upstream).reshape(2, 2, groups * shard, -1)

    query_normal, key_normal = query_pre * query_factor, key_pre * key_factor
    inner = jnp.stack([query_inner[:, 0], key_inner[:, 0]])
    inner = sum_experts(inner)
    inner, grad_w_out = together(inner, grad_w_out)
    out_parts = scatter_first(grad_w_out)
    inner = inner / model_width
    grad_query_low = (query_factor * (query_scaled - query_normal * inner[0][:, None])).astype(low)
    grad_key_low = (key_factor * (key_scaled - key_normal * inner[1][:, None])).astype(low)
    grad_qkv = jnp.concatenate([grad_query_low, grad_key_low, grad_value_low], axis=1)
    qkv_w_grad = by_parts(grad_qkv)
    grad_qkv, qkv_w_grad = together(grad_qkv, qkv_w_grad)
    qkv_parts = scatter_first(qkv_w_grad)
    grad_in_part = times_transpose(grad_qkv, qkv_w)
    count = len(qkv_parts)
    held = together(grad_in_part.astype(low), mixed, *qkv_parts, *out_parts)
    grad_in_low, mixed, qkv_parts, out_parts = held[0], held[1], held[2 : 2 + count], held[2 + count :]
    grad_attn_in = lax.psum_scatter(grad_in_low, "expert", scatter_dimension=0, tiled=True)
    grad_attn_in = grad_attn_in.astype(wide)
    grad_gain_attn = jnp.sum(grad_in_part * attn_normal, axis=0)
    _, own_normal, own_factor = rms_parts(tok.astype(wide), attn_gain)
    grad_attn_x, _ = rms_back(grad_attn_in, own_normal, own_factor, attn_gain)
    grad_tokens = (grad_hidden + grad_attn_x).astype(low)

    small = jnp.concatenate(
        [
            grad_router,
            grad_gain_attn[None],
            spread_heads(grad_gain_query)[None],
            spread_heads(grad_gain_key)[None],
            grad_gain_mlp[None],
        ],
        axis=0,
    )
    small = small.reshape(pack_rows, devices, shard).transpose(1, 0, 2).reshape(devices, -1, 128)
    held = tied((*scatter_ready(*qkv_parts), *scatter_ready(*out_parts), small), 5)
    send(5)
    qkv_parts, out_parts, small = held[:5], held[5:10], held[10]
    small = lax.all_to_all(small, everyone, split_axis=0, concat_axis=0)
    small = jnp.sum(small, axis=0).reshape(pack_rows, shard)
    grad_w_qkv = scatter_last(*qkv_parts).astype(low)
    grad_w_out = scatter_last(*out_parts)
    small, grad_w_qkv, grad_w_out, grad_gate, grad_up = together(
        small, grad_w_qkv, grad_w_out, grad_gate, grad_up
    )
    pieces = [piece for chunk in chunks for piece in chunk]
    part = 2 * local_count
    grad_gate = add_pieces(grad_gate, pieces[:part], 1)
    grad_up = add_pieces(grad_up, pieces[part : 2 * part], 1)
    grad_w_qkv = grad_w_qkv.reshape(groups, shard, 3 * own_width)
    grad_w_qkv = lax.all_to_all(grad_w_qkv, "expert", split_axis=0, concat_axis=0)
    grad_w_qkv, grad_gate, grad_up, grad_tokens = together(
        grad_w_qkv, grad_gate, grad_up, grad_tokens
    )
    grad_w_qkv = grad_w_qkv.reshape(chips, 2, shard, 3, 2, HEAD_DIM).astype(wide)
    grad_w_qkv = grad_w_qkv.transpose(3, 2, 1, 4, 0, 5).reshape(3, shard, model_width)
    grad_down, grad_w_qkv, grad_tokens = together(grad_down, grad_w_qkv, grad_tokens)
    grad_down = add_pieces(grad_down, pieces[2 * part :], 0)

    output = (hidden + mixed.astype(wide)).astype(low)
    return (
        output[None],
        grad_tokens[None],
        grad_w_qkv[0],
        grad_w_qkv[1],
        grad_w_qkv[2],
        grad_w_out,
        small[:experts].T,
        small[experts],
        small[experts + 1],
        small[experts + 2],
        small[experts + 3],
        grad_gate,
        grad_up,
        grad_down,
    )


def specs(dp):
    both = (dp, "expert") if isinstance(dp, str) else dp + ("expert",)
    rows, weight, vector = P(dp, "expert", None), P(both, None), P(both)
    columns, depth = P("expert", None, dp), P("expert", dp, None)
    taken = (rows, rows, P(dp), rows) + (weight,) * 5 + (vector,) * 4 + (columns, columns, depth)
    given = (rows, rows) + (weight,) * 5 + (vector,) * 4 + (columns, columns, depth)
    return (taken, given)


def solution(mesh):
    parts, groups = mesh.shape["dp"], mesh.shape["expert"]

    def whole(*args):
        model_width = args[0].shape[2]
        by_heads = (
            parts == 4
            and groups % 2 == 0
            and model_width == 2 * HEAD_DIM * groups
            and 2 * model_width == parts * groups * HEAD_DIM
        )
        if by_heads:
            used = jax.sharding.Mesh(
                mesh.devices.reshape(2, 2, groups), ("dy", "dx", "expert")
            )
            taken, given = specs(("dy", "dx"))
            body = per_device_by_heads
        else:
            used = mesh
            taken, given = specs("dp")
            body = per_device
        return jax.shard_map(
            body, mesh=used, in_specs=taken, out_specs=given, check_vma=False
        )(*args)

    return whole
```
